32 devices in a mesh: rollout: 2 (over y), frame: 2 (over core), seq: 8 (over z, x).
Axes of the slice: x: 2, y: 2, z: 4, core: 2. Of those that a mesh axis runs over, the one named last changes fastest.
Arguments:
- queries: bfloat16 [4, 4, 64, 2048], P(('rollout', 'frame'), None, 'seq'), parts along dimension 0, may hold values from -13 to 13
- keys: bfloat16 [4, 4, 64, 2048], P(('rollout', 'frame'), None, 'seq'), parts along dimension 0, may hold values from -13 to 13
- values: bfloat16 [4, 4, 64, 2048], P(('rollout', 'frame'), None, 'seq'), parts along dimension 0, may hold values from -6 to 6
- slot_of: int32 [4, 4], P('rollout'), parts along dimension 0, may hold values from 0 to 7, as said below
- level_of: int32 [4, 4], P('rollout'), parts along dimension 0, may hold values from 0 to 7
- gate_table: float32 [8, 2048], replicated, may hold values from 0.25 to 2
Outputs:
- attended: bfloat16 [4, 4, 64, 2048], P(('rollout', 'frame'), None, 'seq'), parts along dimension 0
The draws below stay inside these ranges and needn't reach their ends.
There are 2 independent parts, one for each index of `rollout`. The reference program is written for one: setup_inputs(seed, part) draws one part's arguments, and reference() takes and returns one part's arrays. A program takes and returns all parts, laid end to end along the dimension named above; an argument that names none is the same for every part. Nothing has to cross between parts.
Inputs may be any that keep to these rules, and one draw needn't show every extreme that they name: `slot_of`: each number 0 to 7 is the slot of exactly one frame.
All inputs are finite; a program needn't handle non-finite values.
Results may differ from the reference program's by a relative error of at most 0.0055.
Values may be sent and summed in bfloat16 or wider, within the bound.
No kernel may reach another device: no remote copies, remote signals or barrier semaphores. Data moves between devices by JAX's collectives and lax.ppermute only.
A program may use at most 64 MiB of HBM per device.

```python
import math
import jax
import jax.numpy as jnp
from jax import lax

H = 16
HEAD = 128
HD = 2048
F = 8
F_LOC = 4
N_TOK = 64
LEVELS = 8
N_FRAME = 2


def draw_queries(key, part):
    drawn = jnp.clip(3.0 * jax.random.normal(jax.random.fold_in(key, 1), (F, N_TOK, HD), jnp.float32), -12.0, 12.0)
    return drawn.reshape(F // F_LOC, F_LOC, N_TOK, HD).astype(jnp.bfloat16)


def draw_keys(key, part):
    drawn = jnp.clip(jax.random.normal(jax.random.fold_in(key, 2), (F, N_TOK, HD), jnp.float32), -4.0, 4.0)
    return drawn.reshape(F // F_LOC, F_LOC, N_TOK, HD).astype(jnp.bfloat16)


def draw_slot_of(key, part):
    order = jax.random.permutation(jax.random.fold_in(key, 3), F)
    return order.astype(jnp.int32).reshape(F // F_LOC, F_LOC)


def with_ends(drawn, stream_key, smallest, largest):
    index_at = [jax.random.randint(jax.random.fold_in(stream_key, axis), (), 0, length) for axis, length in enumerate(drawn.shape)]
    widest = drawn.shape.index(max(drawn.shape))
    neighbour = index_at[:widest] + [(index_at[widest] + 1) % drawn.shape[widest]] + index_at[widest + 1:]
    return drawn.at[tuple(index_at)].set(smallest).at[tuple(neighbour)].set(largest)


def block_scale(own_key, shape, split, smallest, high):
    loudness, own = 1.0, jax.random.fold_in(own_key, 6)
    for position, blocks in split:
        heights = jnp.exp(jax.random.uniform(jax.random.fold_in(own, position), (blocks,), jnp.float32, smallest / len(split), high / len(split)))
        loudness = loudness * jnp.repeat(heights, shape[position] // blocks).reshape([-1 if axis == position else 1 for axis in range(len(shape))])
    return loudness


def bell_draw(key, dims, spread, bound, shards=(), kind=jnp.bfloat16):
    drawn = jax.random.normal(key, dims, jnp.float32) * spread
    if len(shards) > 0:
        drawn = block_scale(key, dims, shards, -0.22, 0.18) * drawn
    return jnp.clip(drawn, min=-bound, max=bound).astype(kind)


def setup_inputs(seed: int = 0, part: int = 0) -> dict:
    seeds = jax.random.split(jax.random.key(seed), 7)
    part_keys = jax.random.split(jax.random.fold_in(seeds[6], part), 7)
    queries = draw_queries(jax.random.fold_in(jax.random.fold_in(seeds[6], part), 71), part)
    keys = draw_keys(jax.random.fold_in(jax.random.fold_in(seeds[6], part), 71), part)
    values = bell_draw(part_keys[2], (N_FRAME, F_LOC, N_TOK, HD), 1.0, 6.0, ((0, 2), (2, 8)))
    slot_of = draw_slot_of(jax.random.fold_in(jax.random.fold_in(seeds[6], part), 71), part)
    level_of = with_ends(jax.random.randint(part_keys[4], (N_FRAME, F_LOC), 0, LEVELS), jax.random.fold_in(part_keys[4], 1), 0, LEVELS - 1).astype(jnp.int32)
    gate_table = jnp.clip(jax.random.uniform(seeds[5], (LEVELS, HD), jnp.float32, 0.25, 2.0), 0.25, 2.0)
    return dict(queries=queries, keys=keys, values=values, slot_of=slot_of, level_of=level_of, gate_table=gate_table)


def reference(queries, keys, values, slot_of, level_of, gate_table):
    frames = queries.shape[0] * queries.shape[1]
    tokens = queries.shape[2]
    query_heads = queries.reshape(frames, tokens, H, HEAD)
    key_heads = keys.reshape(frames * tokens, H, HEAD)
    value_heads = values.reshape(frames * tokens, H, HEAD)
    slot_flat = slot_of.reshape(frames)
    key_slot = jnp.repeat(slot_flat, tokens)
    score_scale = 1.0 / math.sqrt(HEAD)

    def one_head(head):
        key_rows = key_heads[:, head, :]
        value_rows = value_heads[:, head, :]

        def one_frame(frame):
            query_rows = query_heads[frame, :, head, :]
            scores = jnp.dot(query_rows, key_rows.T, preferred_element_type=jnp.float32) * score_scale
            visible = key_slot <= slot_flat[frame]
            scores = jnp.where(visible[None, :], scores, -jnp.inf)
            weights = jnp.exp(scores - lax.optimization_barrier(jnp.max(scores, axis=1, keepdims=True))).astype(jnp.bfloat16)
            total = lax.optimization_barrier(jnp.sum(weights.astype(jnp.float32), axis=1))
            mixed = jnp.dot(weights, value_rows, preferred_element_type=jnp.float32)
            return mixed / total[:, None]
        return lax.map(one_frame, jnp.arange(frames, dtype=jnp.int32))
    mixed = lax.map(one_head, jnp.arange(H, dtype=jnp.int32))
    mixed = jnp.transpose(mixed, (1, 2, 0, 3)).reshape(frames, tokens, H * HEAD)
    gates = gate_table[level_of.reshape(frames)]
    attended = (mixed * gates[:, None, :]).astype(jnp.bfloat16)
    return attended.reshape(queries.shape)
```

```python
import functools
import math

import jax
import jax.numpy as jnp
from jax import lax
from jax.experimental import pallas as pl
from jax.experimental.pallas import tpu as pltpu
from jax.sharding import PartitionSpec as P

H = 16
HEAD = 128
AXES = ("frame", "seq")
SMEM = pl.BlockSpec(memory_space=pltpu.SMEM)
VMEM = pl.BlockSpec(memory_space=pltpu.VMEM)
PARAMS = pltpu.CompilerParams(vmem_limit_bytes=32 * 1024 * 1024)


def pack(*refs):
    out_ref = refs[-1]
    width = out_ref.shape[-1]
    for place, ref in enumerate(refs[:-1]):
        for device in range(out_ref.shape[0]):
            out_ref[device, place] = ref[:, device * width : (device + 1) * width]


def unpack(held_ref, out_ref):
    width = held_ref.shape[-1]
    for device in range(held_ref.shape[0]):
        out_ref[:, device * width : (device + 1) * width] = held_ref[device]


def attend(slot_ref, level_ref, packed_ref, gate_ref, out_ref, *, group_devices, tokens):
    devices, _, rows, width = packed_ref.shape
    local_frames = rows // tokens
    group_count = devices // group_devices
    key_count = devices * rows
    index = lax.broadcasted_iota(jnp.int32, (1, key_count), 1)
    frame = index // (group_devices * rows) * local_frames + index // tokens % local_frames
    key_slots = jnp.zeros((1, key_count), jnp.int32)
    for one in range(group_count * local_frames):
        slot = slot_ref[one // local_frames, one % local_frames]
        key_slots = jnp.where(frame == one, slot, key_slots)
    scale = math.log2(math.e) / math.sqrt(HEAD)
    step = max(1, min(group_devices, 128 // rows))
    for column in range(0, width, HEAD):
        part = pl.ds(column, HEAD)
        keys = packed_ref[:, 1, :, part].reshape(key_count, HEAD)
        values = packed_ref[:, 2, :, part].reshape(key_count, HEAD)
        for group in range(group_count):
            shown = []
            gates = []
            for local in range(local_frames):
                visible = key_slots <= slot_ref[group, local]
                shown.append(jnp.where(visible, 0.0, -jnp.inf).reshape(1, 1, 1, key_count))
                level = level_ref[group, local]
                gates.append(gate_ref[pl.ds(level, 1), part].reshape(1, 1, 1, HEAD))
            shown = jnp.concatenate(shown, axis=1)
            gates = jnp.concatenate(gates, axis=1)
            for start in range(group * group_devices, (group + 1) * group_devices, step):
                queries = packed_ref[start : start + step, 0, :, part].reshape(step * rows, HEAD)
                scores = lax.dot_general(
                    queries, keys, (((1,), (1,)), ((), ())), preferred_element_type=jnp.float32
                )
                scores = scores.reshape(step, local_frames, tokens, key_count) * scale + shown
                scores = scores.reshape(step * rows, key_count)
                weights = jnp.exp2(scores - jnp.max(scores, axis=1, keepdims=True))
                weights = weights.astype(jnp.bfloat16)
                total = jnp.sum(weights.astype(jnp.float32), axis=1, keepdims=True)
                mixed = jnp.dot(weights, values, preferred_element_type=jnp.float32) / total
                mixed = mixed.reshape(step, local_frames, tokens, HEAD) * gates
                out_ref[start : start + step, :, part] = mixed.reshape(step, rows, HEAD).astype(
                    out_ref.dtype
                )


def one_head_each(queries, keys, values, slot_of, level_of, gate_table):
    seq_count = lax.axis_size("seq")
    devices = lax.axis_size("frame") * seq_count
    _, local_frames, tokens, all_width = queries.shape
    rows, width = local_frames * tokens, all_width // devices
    exchange = functools.partial(
        lax.all_to_all, axis_name=AXES, split_axis=0, concat_axis=0, tiled=True
    )
    packed = pl.pallas_call(
        pack,
        out_shape=jax.ShapeDtypeStruct((devices, 3, rows, width), queries.dtype),
        in_specs=[VMEM] * 3,
        out_specs=VMEM,
        compiler_params=PARAMS,
    )(*(taken.reshape(rows, all_width) for taken in (queries, keys, values)))
    packed = exchange(packed)
    device_index = lax.axis_index("frame") * seq_count + lax.axis_index("seq")
    gates = lax.dynamic_slice_in_dim(gate_table, device_index * width, width, 1)
    answer = pl.pallas_call(
        functools.partial(attend, group_devices=seq_count, tokens=tokens),
        out_shape=jax.ShapeDtypeStruct((devices, rows, width), queries.dtype),
        in_specs=[SMEM, SMEM, VMEM, VMEM],
        out_specs=VMEM,
        compiler_params=PARAMS,
    )(slot_of, level_of, packed, gates)
    answer = exchange(answer)
    answer = pl.pallas_call(
        unpack,
        out_shape=jax.ShapeDtypeStruct((rows, all_width), queries.dtype),
        in_specs=[VMEM],
        out_specs=VMEM,
        compiler_params=PARAMS,
    )(answer)
    return answer.reshape(queries.shape)


def shared_heads(queries, keys, values, slot_of, level_of, gate_table):
    devices = lax.axis_size("frame") * lax.axis_size("seq")
    _, local_frames, tokens, _ = queries.shape
    rows, blocks = local_frames * tokens, devices // H
    block_rows = rows // blocks
    exchange = functools.partial(
        lax.all_to_all, axis_name=AXES, split_axis=0, concat_axis=0, tiled=True
    )

    def by_head(taken):
        return taken.reshape(rows, H, HEAD).transpose(1, 0, 2)

    def key_pieces(taken):
        pieces = jnp.broadcast_to(by_head(taken)[:, None], (H, blocks, rows, HEAD))
        return exchange(pieces.reshape(devices, rows, HEAD)).reshape(devices * rows, HEAD)

    key_rows, value_rows = key_pieces(keys), key_pieces(values)
    query_rows = exchange(by_head(queries).reshape(devices, block_rows, HEAD))
    query_rows = query_rows.reshape(devices * block_rows, HEAD)
    device_index = lax.axis_index("frame") * lax.axis_size("seq") + lax.axis_index("seq")
    head, block = device_index // blocks, device_index % blocks

    def per_row(table):
        table = jnp.repeat(table, tokens, axis=1)[:, None]
        return jnp.broadcast_to(table, (table.shape[0], lax.axis_size("seq"), rows))

    row_slots, row_levels = per_row(slot_of), per_row(level_of)
    query_slots = lax.dynamic_slice_in_dim(row_slots, block * block_rows, block_rows, 2)
    levels = lax.dynamic_slice_in_dim(row_levels, block * block_rows, block_rows, 2).reshape(-1)
    scores = lax.dot_general(
        query_rows, key_rows, (((1,), (1,)), ((), ())), preferred_element_type=jnp.float32
    )
    visible = row_slots.reshape(1, -1) <= query_slots.reshape(-1, 1)
    scores = jnp.where(visible, scores * (1.0 / math.sqrt(HEAD)), -jnp.inf)
    weights = jnp.exp(scores - jnp.max(scores, axis=1, keepdims=True)).astype(jnp.bfloat16)
    total = jnp.sum(weights.astype(jnp.float32), axis=1, keepdims=True)
    mixed = jnp.dot(weights, value_rows, preferred_element_type=jnp.float32) / total
    gates = lax.dynamic_slice_in_dim(gate_table, head * HEAD, HEAD, 1)[levels]
    answer = exchange((mixed * gates).astype(queries.dtype).reshape(devices, block_rows, HEAD))
    return answer.reshape(H, rows, HEAD).transpose(1, 0, 2).reshape(queries.shape)


def body(queries, *others):
    devices = lax.axis_size("frame") * lax.axis_size("seq")
    if devices > H:
        return shared_heads(queries, *others)
    return one_head_each(queries, *others)


def solution(mesh):
    return jax.shard_map(
        body,
        mesh=mesh,
        in_specs=(
            P(("rollout", "frame"), None, "seq", None),
            P(("rollout", "frame"), None, "seq", None),
            P(("rollout", "frame"), None, "seq", None),
            P("rollout", None),
            P("rollout", None),
            P(),
        ),
        out_specs=P(("rollout", "frame"), None, "seq", None),
        check_vma=False,
    )
```

```python
import functools
import math

import jax
import jax.numpy as jnp
from jax import lax
from jax.experimental import pallas as pl
from jax.experimental.pallas import tpu as pltpu
from jax.sharding import PartitionSpec as P

H = 16
HEAD = 128
AXES = ("frame", "seq")
SMEM = pl.BlockSpec(memory_space=pltpu.SMEM)
VMEM = pl.BlockSpec(memory_space=pltpu.VMEM)
PARAMS = pltpu.CompilerParams(vmem_limit_bytes=32 * 1024 * 1024)


def pack(index_ref, *refs):
    operands, outs, held_ref, sems = refs[:3], refs[3:-2], refs[-2], refs[-1]
    copies = [
        pltpu.make_async_copy(ref, held_ref.at[place], sems.at[place])
        for place, ref in enumerate(operands)
    ]
    for copy in copies:
        copy.start()
    width = outs[0].shape[-1]
    for place, copy in enumerate(copies):
        copy.wait()
        for offset, out_ref in enumerate(outs):
            column = pl.multiple_of((index_ref[0] ^ offset) * width, width)
            out_ref[place] = held_ref[place, :, pl.ds(column, width)]


def unpack(index_ref, *refs):
    out_ref = refs[-1]
    width = refs[0].shape[-1]
    for offset, ref in enumerate(refs[:-1]):
        column = pl.multiple_of((index_ref[0] ^ offset) * width, width)
        out_ref[:, pl.ds(column, width)] = ref[...]


def attend(index_ref, slot_ref, level_ref, gate_ref, *refs, group_devices, tokens):
    devices = len(refs) // 2
    packed, outs = refs[:devices], refs[devices:]
    _, rows, width = packed[0].shape
    local_frames = rows // tokens
    key_count = devices * rows
    device_index = index_ref[0]
    index = lax.broadcasted_iota(jnp.int32, (1, key_count), 1)
    frame = (device_index ^ (index // rows)) // group_devices * local_frames
    frame = frame + index // tokens % local_frames
    key_slots = jnp.zeros((1, key_count), jnp.int32)
    for one in range(devices // group_devices * local_frames):
        slot = slot_ref[one // local_frames, one % local_frames]
        key_slots = jnp.where(frame == one, slot, key_slots)
    scale = math.log2(math.e) / math.sqrt(HEAD)
    step = max(1, min(group_devices, 128 // rows))
    for column in range(0, width, HEAD):
        part = pl.ds(column, HEAD)
        keys = jnp.concatenate([ref[1, :, part] for ref in packed], axis=0)
        values = jnp.concatenate([ref[2, :, part] for ref in packed], axis=0)
        gate_column = pl.ds(pl.multiple_of(device_index * width + column, HEAD), HEAD)
        gate_block = gate_ref[:, gate_column]
        level_rows = lax.broadcasted_iota(jnp.int32, gate_block.shape, 0)
        for first in range(0, devices, group_devices):
            group = (device_index ^ first) // group_devices
            shown = []
            gates = []
            for local in range(local_frames):
                visible = key_slots <= slot_ref[group, local]
                shown.append(jnp.where(visible, 0.0, -jnp.inf).reshape(1, 1, 1, key_count))
                gate = jnp.where(level_rows == level_ref[group, local], gate_block, 0.0)
                gates.append(jnp.sum(gate, axis=0).reshape(1, 1, 1, HEAD))
            shown = jnp.concatenate(shown, axis=1)
            gates = jnp.concatenate(gates, axis=1)
            for start in range(first, first + group_devices, step):
                taken = range(start, start + step)
                queries = jnp.concatenate([packed[one][0, :, part] for one in taken], axis=0)
                scores = lax.dot_general(
                    queries, keys, (((1,), (1,)), ((), ())), preferred_element_type=jnp.float32
                )
                scores = scores.reshape(step, local_frames, tokens, key_count) * scale + shown
                scores = scores.reshape(step * rows, key_count)
                weights = jnp.exp2(scores - jnp.max(scores, axis=1, keepdims=True))
                weights = weights.astype(jnp.bfloat16)
                total = jnp.sum(weights.astype(jnp.float32), axis=1, keepdims=True)
                mixed = jnp.dot(weights, values, preferred_element_type=jnp.float32) / total
                mixed = mixed.reshape(step, local_frames, tokens, HEAD) * gates
                mixed = mixed.reshape(step, rows, HEAD).astype(jnp.bfloat16)
                for place, one in enumerate(taken):
                    outs[one][:, part] = mixed[place]


def exchange(pieces):
    devices = len(pieces)
    return [
        lax.ppermute(piece, AXES, [(one, one ^ offset) for one in range(devices)])
        if offset
        else piece
        for offset, piece in enumerate(pieces)
    ]


def one_head_each(queries, keys, values, slot_of, level_of, gate_table):
    seq_count = lax.axis_size("seq")
    devices = lax.axis_size("frame") * seq_count
    _, local_frames, tokens, all_width = queries.shape
    rows, width = local_frames * tokens, all_width // devices
    device_index = lax.axis_index("frame") * seq_count + lax.axis_index("seq")
    device_index = device_index.reshape(1)
    packed = pl.pallas_call(
        pack,
        out_shape=[jax.ShapeDtypeStruct((3, rows, width), queries.dtype)] * devices,
        in_specs=[SMEM] + [pl.BlockSpec(memory_space=pltpu.HBM)] * 3,
        out_specs=[VMEM] * devices,
        scratch_shapes=[
            pltpu.VMEM((3, rows, all_width), queries.dtype),
            pltpu.SemaphoreType.DMA((3,)),
        ],
        compiler_params=PARAMS,
    )(device_index, *(taken.reshape(rows, all_width) for taken in (queries, keys, values)))
    packed = exchange(packed)
    answer = pl.pallas_call(
        functools.partial(attend, group_devices=seq_count, tokens=tokens),
        out_shape=[jax.ShapeDtypeStruct((rows, width), queries.dtype)] * devices,
        in_specs=[SMEM] * 3 + [VMEM] * (devices + 1),
        out_specs=[VMEM] * devices,
        compiler_params=PARAMS,
    )(device_index, slot_of, level_of, gate_table, *packed)
    answer = exchange(answer)
    answer = pl.pallas_call(
        unpack,
        out_shape=jax.ShapeDtypeStruct((rows, all_width), queries.dtype),
        in_specs=[SMEM] + [VMEM] * devices,
        out_specs=VMEM,
        compiler_params=PARAMS,
    )(device_index, *answer)
    return answer.reshape(queries.shape)


def shared_heads(queries, keys, values, slot_of, level_of, gate_table):
    devices = lax.axis_size("frame") * lax.axis_size("seq")
    _, local_frames, tokens, _ = queries.shape
    rows, blocks = local_frames * tokens, devices // H
    block_rows = rows // blocks
    exchange = functools.partial(
        lax.all_to_all, axis_name=AXES, split_axis=0, concat_axis=0, tiled=True
    )

    def by_head(taken):
        return taken.reshape(rows, H, HEAD).transpose(1, 0, 2)

    def key_pieces(taken):
        pieces = jnp.broadcast_to(by_head(taken)[:, None], (H, blocks, rows, HEAD))
        return exchange(pieces.reshape(devices, rows, HEAD)).reshape(devices * rows, HEAD)

    key_rows, value_rows = key_pieces(keys), key_pieces(values)
    query_rows = exchange(by_head(queries).reshape(devices, block_rows, HEAD))
    query_rows = query_rows.reshape(devices * block_rows, HEAD)
    device_index = lax.axis_index("frame") * lax.axis_size("seq") + lax.axis_index("seq")
    head, block = device_index // blocks, device_index % blocks

    def per_row(table):
        table = jnp.repeat(table, tokens, axis=1)[:, None]
        return jnp.broadcast_to(table, (table.shape[0], lax.axis_size("seq"), rows))

    row_slots, row_levels = per_row(slot_of), per_row(level_of)
    query_slots = lax.dynamic_slice_in_dim(row_slots, block * block_rows, block_rows, 2)
    levels = lax.dynamic_slice_in_dim(row_levels, block * block_rows, block_rows, 2).reshape(-1)
    scores = lax.dot_general(
        query_rows, key_rows, (((1,), (1,)), ((), ())), preferred_element_type=jnp.float32
    )
    visible = row_slots.reshape(1, -1) <= query_slots.reshape(-1, 1)
    scores = jnp.where(visible, scores * (1.0 / math.sqrt(HEAD)), -jnp.inf)
    weights = jnp.exp(scores - jnp.max(scores, axis=1, keepdims=True)).astype(jnp.bfloat16)
    total = jnp.sum(weights.astype(jnp.float32), axis=1, keepdims=True)
    mixed = jnp.dot(weights, value_rows, preferred_element_type=jnp.float32) / total
    gates = lax.dynamic_slice_in_dim(gate_table, head * HEAD, HEAD, 1)[levels]
    answer = exchange((mixed * gates).astype(queries.dtype).reshape(devices, block_rows, HEAD))
    return answer.reshape(H, rows, HEAD).transpose(1, 0, 2).reshape(queries.shape)


def body(queries, *others):
    devices = lax.axis_size("frame") * lax.axis_size("seq")
    if devices > H:
        return shared_heads(queries, *others)
    return one_head_each(queries, *others)


def solution(mesh):
    return jax.shard_map(
        body,
        mesh=mesh,
        in_specs=(
            P(("rollout", "frame"), None, "seq", None),
            P(("rollout", "frame"), None, "seq", None),
            P(("rollout", "frame"), None, "seq", None),
            P("rollout", None),
            P("rollout", None),
            P(),
        ),
        out_specs=P(("rollout", "frame"), None, "seq", None),
        check_vma=False,
    )
```

```python
import functools
import math

import jax
import jax.numpy as jnp
from jax import lax
from jax.experimental import pallas as pl
from jax.experimental.pallas import tpu as pltpu
from jax.sharding import PartitionSpec as P

H = 16
HEAD = 128
AXES = ("frame", "seq")
SMEM = pl.BlockSpec(memory_space=pltpu.SMEM)
VMEM = pl.BlockSpec(memory_space=pltpu.VMEM)
PARAMS = pltpu.CompilerParams(vmem_limit_bytes=32 * 1024 * 1024)


def pack(query_ref, key_ref, value_ref, pair_ref, own_ref, held_ref, sems):
    copies = [
        pltpu.make_async_copy(ref, held_ref.at[place], sems.at[place])
        for place, ref in enumerate((key_ref, value_ref, query_ref))
    ]
    for copy in copies:
        copy.start()
    width = own_ref.shape[-1]
    for place, copy in enumerate(copies):
        copy.wait()
        for device in range(own_ref.shape[0]):
            taken = held_ref[place, :, device * width : (device + 1) * width]
            if place < 2:
                pair_ref[device, place] = taken
            else:
                own_ref[device] = taken


def unpack(held_ref, out_ref):
    width = held_ref.shape[-1]
    for device in range(held_ref.shape[0]):
        out_ref[:, device * width : (device + 1) * width] = held_ref[device]


def attend(index_ref, slot_ref, level_ref, gate_ref, query_ref, *refs, tokens):
    pair_refs, out_ref = refs[:-1], refs[-1]
    group_count = len(pair_refs)
    devices, _, rows, width = pair_refs[0].shape
    local_frames = rows // tokens
    key_count = group_count * devices * rows
    group = index_ref[0]
    index = lax.broadcasted_iota(jnp.int32, (1, key_count), 1)
    frame = (index // (devices * rows) + group) % group_count * local_frames
    frame = frame + index // tokens % local_frames
    key_slots = jnp.zeros((1, key_count), jnp.int32)
    for one in range(group_count * local_frames):
        slot = slot_ref[one // local_frames, one % local_frames]
        key_slots = jnp.where(frame == one, slot, key_slots)
    shown = []
    for local in range(local_frames):
        visible = key_slots <= slot_ref[group, local]
        shown.append(jnp.where(visible, 0.0, -jnp.inf).reshape(1, 1, 1, key_count))
    shown = jnp.concatenate(shown, axis=1)
    scale = math.log2(math.e) / math.sqrt(HEAD)
    step = max(1, min(devices, 128 // rows))
    for column in range(0, width, HEAD):
        part = pl.ds(column, HEAD)
        gate_column = pl.ds(pl.multiple_of(index_ref[1] * width + column, HEAD), HEAD)
        gate_block = gate_ref[:, gate_column]
        level_rows = lax.broadcasted_iota(jnp.int32, gate_block.shape, 0)
        gates = []
        for local in range(local_frames):
            gate = jnp.where(level_rows == level_ref[group, local], gate_block, 0.0)
            gates.append(jnp.sum(gate, axis=0).reshape(1, 1, 1, HEAD))
        gates = jnp.concatenate(gates, axis=1)
        keys, values = (
            jnp.concatenate(
                [ref[:, place, :, part].reshape(devices * rows, HEAD) for ref in pair_refs]
            )
            for place in range(2)
        )
        for start in range(0, devices, step):
            queries = query_ref[start : start + step, :, part].reshape(step * rows, HEAD)
            scores = lax.dot_general(
                queries, keys, (((1,), (1,)), ((), ())), preferred_element_type=jnp.float32
            )
            scores = scores.reshape(step, local_frames, tokens, key_count) * scale + shown
            scores = scores.reshape(step * rows, key_count)
            weights = jnp.exp2(scores - jnp.max(scores, axis=1, keepdims=True))
            weights = weights.astype(jnp.bfloat16)
            total = jnp.sum(weights.astype(jnp.float32), axis=1, keepdims=True)
            mixed = jnp.dot(weights, values, preferred_element_type=jnp.float32) / total
            mixed = mixed.reshape(step, local_frames, tokens, HEAD) * gates
            out_ref[start : start + step, :, part] = mixed.reshape(step, rows, HEAD).astype(
                out_ref.dtype
            )


def whole_heads(queries, keys, values, slot_of, level_of, gate_table):
    devices = lax.axis_size("seq")
    _, local_frames, tokens, all_width = queries.shape
    rows, width = local_frames * tokens, all_width // devices
    exchange = functools.partial(
        lax.all_to_all, axis_name="seq", split_axis=0, concat_axis=0, tiled=True
    )
    index = jnp.stack([lax.axis_index("frame"), lax.axis_index("seq")])
    pair, own = pl.pallas_call(
        pack,
        out_shape=[
            jax.ShapeDtypeStruct((devices, 2, rows, width), queries.dtype),
            jax.ShapeDtypeStruct((devices, rows, width), queries.dtype),
        ],
        in_specs=[pl.BlockSpec(memory_space=pltpu.HBM)] * 3,
        out_specs=[VMEM] * 2,
        scratch_shapes=[
            pltpu.VMEM((3, rows, all_width), queries.dtype),
            pltpu.SemaphoreType.DMA((3,)),
        ],
        compiler_params=PARAMS,
    )(
        *(
            pltpu.with_memory_space_constraint(taken.reshape(rows, all_width), pltpu.HBM)
            for taken in (queries, keys, values)
        )
    )
    pair = exchange(pair)
    own = exchange(own)
    groups = lax.axis_size("frame")
    pairs = [pair] + [
        lax.ppermute(pair, "frame", [(one, (one - away) % groups) for one in range(groups)])
        for away in range(1, groups)
    ]
    answer = pl.pallas_call(
        functools.partial(attend, tokens=tokens),
        out_shape=jax.ShapeDtypeStruct((devices, rows, width), queries.dtype),
        in_specs=[SMEM] * 3 + [VMEM] * (2 + groups),
        out_specs=VMEM,
        compiler_params=PARAMS,
    )(index, slot_of, level_of, gate_table, own, *pairs)
    answer = exchange(answer)
    answer = pl.pallas_call(
        unpack,
        out_shape=jax.ShapeDtypeStruct((rows, all_width), queries.dtype),
        in_specs=[VMEM],
        out_specs=VMEM,
        compiler_params=PARAMS,
    )(answer)
    return answer.reshape(queries.shape)


def shared_heads(queries, keys, values, slot_of, level_of, gate_table):
    devices = lax.axis_size("frame") * lax.axis_size("seq")
    _, local_frames, tokens, _ = queries.shape
    rows, blocks = local_frames * tokens, devices // H
    block_rows = rows // blocks
    exchange = functools.partial(
        lax.all_to_all, axis_name=AXES, split_axis=0, concat_axis=0, tiled=True
    )

    def by_head(taken):
        return taken.reshape(rows, H, HEAD).transpose(1, 0, 2)

    def key_pieces(taken):
        pieces = jnp.broadcast_to(by_head(taken)[:, None], (H, blocks, rows, HEAD))
        return exchange(pieces.reshape(devices, rows, HEAD)).reshape(devices * rows, HEAD)

    key_rows, value_rows = key_pieces(keys), key_pieces(values)
    query_rows = exchange(by_head(queries).reshape(devices, block_rows, HEAD))
    query_rows = query_rows.reshape(devices * block_rows, HEAD)
    device_index = lax.axis_index("frame") * lax.axis_size("seq") + lax.axis_index("seq")
    head, block = device_index // blocks, device_index % blocks

    def per_row(table):
        table = jnp.repeat(table, tokens, axis=1)[:, None]
        return jnp.broadcast_to(table, (table.shape[0], lax.axis_size("seq"), rows))

    row_slots, row_levels = per_row(slot_of), per_row(level_of)
    query_slots = lax.dynamic_slice_in_dim(row_slots, block * block_rows, block_rows, 2)
    levels = lax.dynamic_slice_in_dim(row_levels, block * block_rows, block_rows, 2).reshape(-1)
    scores = lax.dot_general(
        query_rows, key_rows, (((1,), (1,)), ((), ())), preferred_element_type=jnp.float32
    )
    visible = row_slots.reshape(1, -1) <= query_slots.reshape(-1, 1)
    scores = jnp.where(visible, scores * (1.0 / math.sqrt(HEAD)), -jnp.inf)
    weights = jnp.exp(scores - jnp.max(scores, axis=1, keepdims=True)).astype(jnp.bfloat16)
    total = jnp.sum(weights.astype(jnp.float32), axis=1, keepdims=True)
    mixed = jnp.dot(weights, value_rows, preferred_element_type=jnp.float32) / total
    gates = lax.dynamic_slice_in_dim(gate_table, head * HEAD, HEAD, 1)[levels]
    answer = exchange((mixed * gates).astype(queries.dtype).reshape(devices, block_rows, HEAD))
    return answer.reshape(H, rows, HEAD).transpose(1, 0, 2).reshape(queries.shape)


def body(queries, *others):
    if lax.axis_size("seq") > H:
        return shared_heads(queries, *others)
    return whole_heads(queries, *others)


def solution(mesh):
    return jax.shard_map(
        body,
        mesh=mesh,
        in_specs=(
            P(("rollout", "frame"), None, "seq", None),
            P(("rollout", "frame"), None, "seq", None),
            P(("rollout", "frame"), None, "seq", None),
            P("rollout", None),
            P("rollout", None),
            P(),
        ),
        out_specs=P(("rollout", "frame"), None, "seq", None),
        check_vma=False,
    )
```

```python
import functools
import math

import jax
import jax.numpy as jnp
from jax import lax
from jax.experimental import pallas as pl
from jax.experimental.pallas import tpu as pltpu
from jax.sharding import PartitionSpec as P

H = 16
HEAD = 128
AXES = ("frame", "seq")
SMEM = pl.BlockSpec(memory_space=pltpu.SMEM)
HBM = pl.BlockSpec(memory_space=pltpu.HBM)
VMEM = pl.BlockSpec(memory_space=pltpu.VMEM)
PARAMS = pltpu.CompilerParams(vmem_limit_bytes=32 * 1024 * 1024)


def pack(*refs):
    out_ref, sems = refs[-2:]
    width = out_ref.shape[-1]
    copies = [
        pltpu.make_async_copy(
            ref.at[:, pl.ds(device * width, width)],
            out_ref.at[device, place],
            sems.at[device, place],
        )
        for place, ref in enumerate(refs[:-2])
        for device in range(out_ref.shape[0])
    ]
    for copy in copies:
        copy.start()
    for copy in copies:
        copy.wait()


def unpack(held_ref, out_ref, sems):
    width = held_ref.shape[-1]
    copies = [
        pltpu.make_async_copy(
            held_ref.at[device], out_ref.at[:, pl.ds(device * width, width)], sems.at[device]
        )
        for device in range(held_ref.shape[0])
    ]
    for copy in copies:
        copy.start()
    for copy in copies:
        copy.wait()


def attend(index_ref, slot_ref, level_ref, gate_ref, *refs, tokens):
    packed_refs, out_ref = refs[:-1], refs[-1]
    group_count = len(packed_refs)
    devices, _, rows, width = packed_refs[0].shape
    local_frames = rows // tokens
    key_count = group_count * devices * rows
    group = index_ref[0]
    index = lax.broadcasted_iota(jnp.int32, (1, key_count), 1)
    frame = (index // (devices * rows) + group) % group_count * local_frames
    frame = frame + index // tokens % local_frames
    key_slots = jnp.zeros((1, key_count), jnp.int32)
    for one in range(group_count * local_frames):
        slot = slot_ref[one // local_frames, one % local_frames]
        key_slots = jnp.where(frame == one, slot, key_slots)
    shown = []
    for local in range(local_frames):
        visible = key_slots <= slot_ref[group, local]
        shown.append(jnp.where(visible, 0.0, -jnp.inf).reshape(1, 1, 1, key_count))
    shown = jnp.concatenate(shown, axis=1)
    ones = jnp.ones((key_count, HEAD), jnp.bfloat16)
    scale = math.log2(math.e) / math.sqrt(HEAD)
    step = max(1, min(devices, 128 // rows))
    for column in range(0, width, HEAD):
        part = pl.ds(column, HEAD)
        gate_column = pl.ds(pl.multiple_of(index_ref[1] * width + column, HEAD), HEAD)
        gate_block = gate_ref[:, gate_column]
        level_rows = lax.broadcasted_iota(jnp.int32, gate_block.shape, 0)
        gates = []
        for local in range(local_frames):
            gate = jnp.where(level_rows == level_ref[group, local], gate_block, 0.0)
            gates.append(jnp.sum(gate, axis=0).reshape(1, 1, 1, HEAD))
        gates = jnp.concatenate(gates, axis=1)
        keys, values = (
            jnp.concatenate(
                [ref[:, place, :, part].reshape(devices * rows, HEAD) for ref in packed_refs]
            )
            for place in (1, 2)
        )
        values = jnp.concatenate([values, ones], axis=1)
        for start in range(0, devices, step):
            queries = packed_refs[0][start : start + step, 0, :, part].reshape(step * rows, HEAD)
            scores = lax.dot_general(
                queries, keys, (((1,), (1,)), ((), ())), preferred_element_type=jnp.float32
            )
            scores = scores.reshape(step, local_frames, tokens, key_count) * scale + shown
            scores = scores.reshape(step * rows, key_count)
            weights = jnp.exp2(scores - jnp.max(scores, axis=1, keepdims=True))
            mixed = jnp.dot(
                weights.astype(jnp.bfloat16), values, preferred_element_type=jnp.float32
            )
            mixed = mixed[:, :HEAD] / mixed[:, HEAD:]
            mixed = mixed.reshape(step, local_frames, tokens, HEAD) * gates
            out_ref[start : start + step, :, part] = mixed.reshape(step, rows, HEAD).astype(
                out_ref.dtype
            )


def whole_heads(queries, keys, values, slot_of, level_of, gate_table):
    devices, groups = lax.axis_size("seq"), lax.axis_size("frame")
    _, local_frames, tokens, all_width = queries.shape
    rows, width = local_frames * tokens, all_width // devices
    exchange = functools.partial(
        lax.all_to_all, axis_name="seq", split_axis=0, concat_axis=0, tiled=True
    )
    index = jnp.stack([lax.axis_index("frame"), lax.axis_index("seq")])
    packed = pl.pallas_call(
        pack,
        out_shape=jax.ShapeDtypeStruct((devices, 3, rows, width), queries.dtype),
        in_specs=[HBM] * 3,
        out_specs=VMEM,
        scratch_shapes=[pltpu.SemaphoreType.DMA((devices, 3))],
        compiler_params=PARAMS,
    )(
        *(
            pltpu.with_memory_space_constraint(taken.reshape(rows, all_width), pltpu.HBM)
            for taken in (queries, keys, values)
        )
    )
    packed = exchange(packed)
    packs = [packed] + [
        lax.ppermute(packed, "frame", [(one, (one - away) % groups) for one in range(groups)])
        for away in range(1, groups)
    ]
    answer = pl.pallas_call(
        functools.partial(attend, tokens=tokens),
        out_shape=jax.ShapeDtypeStruct((devices, rows, width), queries.dtype),
        in_specs=[SMEM] * 3 + [VMEM] * (1 + groups),
        out_specs=VMEM,
        compiler_params=PARAMS,
    )(index, slot_of, level_of, gate_table, *packs)
    answer = exchange(answer)
    answer = pl.pallas_call(
        unpack,
        out_shape=jax.ShapeDtypeStruct((rows, all_width), queries.dtype),
        in_specs=[VMEM],
        out_specs=HBM,
        scratch_shapes=[pltpu.SemaphoreType.DMA((devices,))],
        compiler_params=PARAMS,
    )(answer)
    return answer.reshape(queries.shape)


def shared_heads(queries, keys, values, slot_of, level_of, gate_table):
    devices = lax.axis_size("frame") * lax.axis_size("seq")
    _, local_frames, tokens, _ = queries.shape
    rows, blocks = local_frames * tokens, devices // H
    block_rows = rows // blocks
    exchange = functools.partial(
        lax.all_to_all, axis_name=AXES, split_axis=0, concat_axis=0, tiled=True
    )

    def by_head(taken):
        return taken.reshape(rows, H, HEAD).transpose(1, 0, 2)

    def key_pieces(taken):
        pieces = jnp.broadcast_to(by_head(taken)[:, None], (H, blocks, rows, HEAD))
        return exchange(pieces.reshape(devices, rows, HEAD)).reshape(devices * rows, HEAD)

    key_rows, value_rows = key_pieces(keys), key_pieces(values)
    query_rows = exchange(by_head(queries).reshape(devices, block_rows, HEAD))
    query_rows = query_rows.reshape(devices * block_rows, HEAD)
    device_index = lax.axis_index("frame") * lax.axis_size("seq") + lax.axis_index("seq")
    head, block = device_index // blocks, device_index % blocks

    def per_row(table):
        table = jnp.repeat(table, tokens, axis=1)[:, None]
        return jnp.broadcast_to(table, (table.shape[0], lax.axis_size("seq"), rows))

    row_slots, row_levels = per_row(slot_of), per_row(level_of)
    query_slots = lax.dynamic_slice_in_dim(row_slots, block * block_rows, block_rows, 2)
    levels = lax.dynamic_slice_in_dim(row_levels, block * block_rows, block_rows, 2).reshape(-1)
    scores = lax.dot_general(
        query_rows, key_rows, (((1,), (1,)), ((), ())), preferred_element_type=jnp.float32
    )
    visible = row_slots.reshape(1, -1) <= query_slots.reshape(-1, 1)
    scores = jnp.where(visible, scores * (1.0 / math.sqrt(HEAD)), -jnp.inf)
    weights = jnp.exp(scores - jnp.max(scores, axis=1, keepdims=True)).astype(jnp.bfloat16)
    total = jnp.sum(weights.astype(jnp.float32), axis=1, keepdims=True)
    mixed = jnp.dot(weights, value_rows, preferred_element_type=jnp.float32) / total
    gates = lax.dynamic_slice_in_dim(gate_table, head * HEAD, HEAD, 1)[levels]
    answer = exchange((mixed * gates).astype(queries.dtype).reshape(devices, block_rows, HEAD))
    return answer.reshape(H, rows, HEAD).transpose(1, 0, 2).reshape(queries.shape)


def body(queries, *others):
    if lax.axis_size("seq") > H:
        return shared_heads(queries, *others)
    return whole_heads(queries, *others)


def solution(mesh):
    return jax.shard_map(
        body,
        mesh=mesh,
        in_specs=(
            P(("rollout", "frame"), None, "seq", None),
            P(("rollout", "frame"), None, "seq", None),
            P(("rollout", "frame"), None, "seq", None),
            P("rollout", None),
            P("rollout", None),
            P(),
        ),
        out_specs=P(("rollout", "frame"), None, "seq", None),
        check_vma=False,
    )
```

```python
import functools
import math

import jax
import jax.numpy as jnp
from jax import lax
from jax.experimental import pallas as pl
from jax.experimental.pallas import tpu as pltpu
from jax.sharding import PartitionSpec as P

H = 16
HEAD = 128
AXES = ("frame", "seq")
SMEM = pl.BlockSpec(memory_space=pltpu.SMEM)
HBM = pl.BlockSpec(memory_space=pltpu.HBM)
VMEM = pl.BlockSpec(memory_space=pltpu.VMEM)
PARAMS = pltpu.CompilerParams(vmem_limit_bytes=32 * 1024 * 1024)


def far_first(devices):
    return sorted(range(devices), key=lambda away: (away > 0, -(2 * away // devices), away % 2, -away))


def pack(index_ref, *refs):
    operands, outs, sems = refs[:3], refs[3:-1], refs[-1]
    width = outs[0].shape[-1]
    copies = []
    for away, out_ref in zip(far_first(len(outs)), outs):
        column = pl.ds(pl.multiple_of((index_ref[1] ^ away) * width, width), width)
        copies += [
            pltpu.make_async_copy(ref.at[:, column], out_ref.at[place], sems.at[away, place])
            for place, ref in enumerate(operands)
        ]
    for copy in copies:
        copy.start()
    for copy in copies:
        copy.wait()


def stack(*refs):
    pieces, out_ref, sems = refs[:-2], refs[-2], refs[-1]
    copies = [
        pltpu.make_async_copy(ref.at[pl.ds(1, 2)], out_ref.at[away], sems.at[away])
        for away, ref in enumerate(pieces)
    ]
    for copy in copies:
        copy.start()
    for copy in copies:
        copy.wait()


def unpack(held_ref, out_ref, sems):
    width = held_ref.shape[-1]
    copies = [
        pltpu.make_async_copy(
            held_ref.at[device], out_ref.at[:, pl.ds(device * width, width)], sems.at[device]
        )
        for device in range(held_ref.shape[0])
    ]
    for copy in copies:
        copy.start()
    for copy in copies:
        copy.wait()


def attend(index_ref, slot_ref, level_ref, gate_ref, *refs, tokens):
    out_ref = refs[-1]
    devices, rows, width = out_ref.shape
    own_refs, pair_refs = refs[:devices], refs[devices:-1]
    group_count = 1 + len(pair_refs)
    local_frames = rows // tokens
    key_count = group_count * devices * rows
    group = index_ref[0]
    index = lax.broadcasted_iota(jnp.int32, (1, key_count), 1)
    frame = (index // (devices * rows) + group) % group_count * local_frames
    frame = frame + index // tokens % local_frames
    key_slots = jnp.zeros((1, key_count), jnp.int32)
    for one in range(group_count * local_frames):
        slot = slot_ref[one // local_frames, one % local_frames]
        key_slots = jnp.where(frame == one, slot, key_slots)
    shown = []
    for local in range(local_frames):
        visible = key_slots <= slot_ref[group, local]
        shown.append(jnp.where(visible, 0.0, -jnp.inf).reshape(1, 1, 1, key_count))
    shown = jnp.concatenate(shown, axis=1)
    ones = jnp.ones((key_count, HEAD), jnp.bfloat16)
    scale = math.log2(math.e) / math.sqrt(HEAD)
    step = max(1, min(devices, 128 // rows))
    for column in range(0, width, HEAD):
        part = pl.ds(column, HEAD)
        gate_column = pl.ds(pl.multiple_of(index_ref[1] * width + column, HEAD), HEAD)
        gate_block = gate_ref[:, gate_column]
        level_rows = lax.broadcasted_iota(jnp.int32, gate_block.shape, 0)
        gates = []
        for local in range(local_frames):
            gate = jnp.where(level_rows == level_ref[group, local], gate_block, 0.0)
            gates.append(jnp.sum(gate, axis=0).reshape(1, 1, 1, HEAD))
        gates = jnp.concatenate(gates, axis=1)
        keys, values = (
            jnp.concatenate(
                [ref[1 + place, :, part] for ref in own_refs]
                + [ref[:, place, :, part].reshape(devices * rows, HEAD) for ref in pair_refs]
            )
            for place in range(2)
        )
        values = jnp.concatenate([values, ones], axis=1)
        for start in range(0, devices, step):
            queries = jnp.concatenate([ref[0, :, part] for ref in own_refs[start : start + step]])
            scores = lax.dot_general(
                queries, keys, (((1,), (1,)), ((), ())), preferred_element_type=jnp.float32
            )
            scores = scores.reshape(step, local_frames, tokens, key_count) * scale + shown
            scores = scores.reshape(step * rows, key_count)
            weights = jnp.exp2(scores - jnp.max(scores, axis=1, keepdims=True))
            mixed = jnp.dot(
                weights.astype(jnp.bfloat16), values, preferred_element_type=jnp.float32
            )
            mixed = mixed[:, :HEAD] / mixed[:, HEAD:]
            mixed = mixed.reshape(step, local_frames, tokens, HEAD) * gates
            mixed = mixed.reshape(step, rows, HEAD).astype(out_ref.dtype)
            for place, away in enumerate(far_first(devices)[start : start + step]):
                out_ref[index_ref[1] ^ away, :, part] = mixed[place]


def whole_heads(queries, keys, values, slot_of, level_of, gate_table):
    devices, groups = lax.axis_size("seq"), lax.axis_size("frame")
    _, local_frames, tokens, all_width = queries.shape
    rows, width = local_frames * tokens, all_width // devices
    index = jnp.stack([lax.axis_index("frame"), lax.axis_index("seq")])
    pieces = pl.pallas_call(
        pack,
        out_shape=[jax.ShapeDtypeStruct((3, rows, width), queries.dtype)] * devices,
        in_specs=[SMEM] + [HBM] * 3,
        out_specs=[VMEM] * devices,
        scratch_shapes=[pltpu.SemaphoreType.DMA((devices, 3))],
        compiler_params=PARAMS,
    )(
        index,
        *(
            pltpu.with_memory_space_constraint(taken.reshape(rows, all_width), pltpu.HBM)
            for taken in (queries, keys, values)
        ),
    )
    pieces = [
        lax.ppermute(piece, "seq", [(one, one ^ away) for one in range(devices)])
        if away
        else piece
        for away, piece in zip(far_first(devices), pieces)
    ]
    pair = pl.pallas_call(
        stack,
        out_shape=jax.ShapeDtypeStruct((devices, 2, rows, width), queries.dtype),
        in_specs=[VMEM] * devices,
        out_specs=VMEM,
        scratch_shapes=[pltpu.SemaphoreType.DMA((devices,))],
        compiler_params=PARAMS,
    )(*pieces)
    pairs = [
        lax.ppermute(pair, "frame", [(one, (one - away) % groups) for one in range(groups)])
        for away in range(1, groups)
    ]
    answer = pl.pallas_call(
        functools.partial(attend, tokens=tokens),
        out_shape=jax.ShapeDtypeStruct((devices, rows, width), queries.dtype),
        in_specs=[SMEM] * 3 + [VMEM] * (devices + groups),
        out_specs=VMEM,
        compiler_params=PARAMS,
    )(index, slot_of, level_of, gate_table, *pieces, *pairs)
    answer = lax.all_to_all(answer, "seq", split_axis=0, concat_axis=0, tiled=True)
    answer = pl.pallas_call(
        unpack,
        out_shape=jax.ShapeDtypeStruct((rows, all_width), queries.dtype),
        in_specs=[VMEM],
        out_specs=HBM,
        scratch_shapes=[pltpu.SemaphoreType.DMA((devices,))],
        compiler_params=PARAMS,
    )(answer)
    return answer.reshape(queries.shape)


def shared_heads(queries, keys, values, slot_of, level_of, gate_table):
    devices = lax.axis_size("frame") * lax.axis_size("seq")
    _, local_frames, tokens, _ = queries.shape
    rows, blocks = local_frames * tokens, devices // H
    block_rows = rows // blocks
    exchange = functools.partial(
        lax.all_to_all, axis_name=AXES, split_axis=0, concat_axis=0, tiled=True
    )

    def by_head(taken):
        return taken.reshape(rows, H, HEAD).transpose(1, 0, 2)

    def key_pieces(taken):
        pieces = jnp.broadcast_to(by_head(taken)[:, None], (H, blocks, rows, HEAD))
        return exchange(pieces.reshape(devices, rows, HEAD)).reshape(devices * rows, HEAD)

    key_rows, value_rows = key_pieces(keys), key_pieces(values)
    query_rows = exchange(by_head(queries).reshape(devices, block_rows, HEAD))
    query_rows = query_rows.reshape(devices * block_rows, HEAD)
    device_index = lax.axis_index("frame") * lax.axis_size("seq") + lax.axis_index("seq")
    head, block = device_index // blocks, device_index % blocks

    def per_row(table):
        table = jnp.repeat(table, tokens, axis=1)[:, None]
        return jnp.broadcast_to(table, (table.shape[0], lax.axis_size("seq"), rows))

    row_slots, row_levels = per_row(slot_of), per_row(level_of)
    query_slots = lax.dynamic_slice_in_dim(row_slots, block * block_rows, block_rows, 2)
    levels = lax.dynamic_slice_in_dim(row_levels, block * block_rows, block_rows, 2).reshape(-1)
    scores = lax.dot_general(
        query_rows, key_rows, (((1,), (1,)), ((), ())), preferred_element_type=jnp.float32
    )
    visible = row_slots.reshape(1, -1) <= query_slots.reshape(-1, 1)
    scores = jnp.where(visible, scores * (1.0 / math.sqrt(HEAD)), -jnp.inf)
    weights = jnp.exp(scores - jnp.max(scores, axis=1, keepdims=True)).astype(jnp.bfloat16)
    total = jnp.sum(weights.astype(jnp.float32), axis=1, keepdims=True)
    mixed = jnp.dot(weights, value_rows, preferred_element_type=jnp.float32) / total
    gates = lax.dynamic_slice_in_dim(gate_table, head * HEAD, HEAD, 1)[levels]
    answer = exchange((mixed * gates).astype(queries.dtype).reshape(devices, block_rows, HEAD))
    return answer.reshape(H, rows, HEAD).transpose(1, 0, 2).reshape(queries.shape)


def body(queries, *others):
    devices = lax.axis_size("seq")
    if devices > H or devices & (devices - 1):
        return shared_heads(queries, *others)
    return whole_heads(queries, *others)


def solution(mesh):
    return jax.shard_map(
        body,
        mesh=mesh,
        in_specs=(
            P(("rollout", "frame"), None, "seq", None),
            P(("rollout", "frame"), None, "seq", None),
            P(("rollout", "frame"), None, "seq", None),
            P("rollout", None),
            P("rollout", None),
            P(),
        ),
        out_specs=P(("rollout", "frame"), None, "seq", None),
        check_vma=False,
    )
```

```python
import functools
import math

import jax
import jax.numpy as jnp
from jax import lax
from jax.experimental import pallas as pl
from jax.experimental.pallas import tpu as pltpu
from jax.sharding import PartitionSpec as P

H = 16
HEAD = 128
AXES = ("frame", "seq")
SMEM = pl.BlockSpec(memory_space=pltpu.SMEM)
HBM = pl.BlockSpec(memory_space=pltpu.HBM)
VMEM = pl.BlockSpec(memory_space=pltpu.VMEM)
PARAMS = pltpu.CompilerParams(vmem_limit_bytes=32 * 1024 * 1024)


def far_first(count):
    return sorted(range(count), key=lambda away: (away > 0, -(2 * away // count), away % 2, -away))


def columns_of(place, width):
    return pl.ds(pl.multiple_of(place * width, width), width)


def run(copies):
    for copy in copies:
        copy.start()
    for copy in copies:
        copy.wait()


def pack(*refs, near):
    operands, outs, sems = refs[:3], refs[3:-1], refs[-1]
    place = lax.axis_index("seq") // near
    copies = []
    for number, (away, out_ref) in enumerate(zip(far_first(len(outs)), outs)):
        columns = columns_of(place ^ away, out_ref.shape[-1])
        copies += [
            pltpu.make_async_copy(ref.at[:, columns], out_ref.at[kind], sems.at[number, kind])
            for kind, ref in enumerate(operands)
        ]
    run(copies)


def stack(*refs):
    pieces, out_ref, sems = refs[:-2], refs[-2], refs[-1]
    run(
        [
            pltpu.make_async_copy(ref.at[pl.ds(1, 2)], out_ref.at[number], sems.at[number])
            for number, ref in enumerate(pieces)
        ]
    )


def unpack(*refs, near):
    answers, out_ref, sems = refs[:-2], refs[-2], refs[-1]
    place = lax.axis_index("seq") // near
    run(
        [
            pltpu.make_async_copy(
                ref, out_ref.at[:, columns_of(place ^ away, ref.shape[-1])], sems.at[number]
            )
            for number, (away, ref) in enumerate(zip(far_first(len(answers)), answers))
        ]
    )


def attend(slot_ref, level_ref, gate_ref, *refs, pieces, near, tokens):
    held_refs, pair_refs, outs = refs[: near * pieces], refs[near * pieces : -pieces], refs[-pieces:]
    rows, width = outs[0].shape
    group_count = 1 + len(pair_refs)
    local_frames = rows // tokens
    group_keys = near * pieces * rows
    key_count = group_count * group_keys
    group = lax.axis_index("frame")
    index = lax.broadcasted_iota(jnp.int32, (1, key_count), 1)
    frame = (index // group_keys + group) % group_count * local_frames
    frame = frame + index // tokens % local_frames
    key_slots = jnp.zeros((1, key_count), jnp.int32)
    for one in range(group_count * local_frames):
        slot = slot_ref[one // local_frames, one % local_frames]
        key_slots = jnp.where(frame == one, slot, key_slots)
    shown = []
    for local in range(local_frames):
        visible = key_slots <= slot_ref[group, local]
        shown.append(jnp.where(visible, 0.0, -jnp.inf).reshape(1, 1, 1, key_count))
    shown = jnp.concatenate(shown, axis=1)
    ones = jnp.ones((key_count, HEAD), jnp.bfloat16)
    scale = math.log2(math.e) / math.sqrt(HEAD)
    gate_blocks = gate_ref[:, columns_of(lax.axis_index("seq") // near, width)]
    level_rows = lax.broadcasted_iota(jnp.int32, gate_blocks.shape, 0)
    gate_rows = [
        jnp.sum(
            jnp.where(level_rows == level_ref[group, local], gate_blocks, 0.0),
            axis=0,
            keepdims=True,
        )
        for local in range(local_frames)
    ]
    step = max(1, min(pieces, 128 // rows))
    for column in range(0, width, HEAD):
        part = slice(column, column + HEAD)
        gates = jnp.concatenate([row[:, part].reshape(1, 1, 1, HEAD) for row in gate_rows], axis=1)
        keys, values = (
            jnp.concatenate(
                [ref[1 + kind, :, part] for ref in held_refs]
                + [ref[:, kind, :, part].reshape(group_keys, HEAD) for ref in pair_refs]
            )
            for kind in range(2)
        )
        values = jnp.concatenate([values, ones], axis=1)
        for start in range(0, pieces, step):
            queries = jnp.concatenate([ref[0, :, part] for ref in held_refs[start : start + step]])
            scores = lax.dot_general(
                queries, keys, (((1,), (1,)), ((), ())), preferred_element_type=jnp.float32
            )
            scores = scores.reshape(step, local_frames, tokens, key_count) * scale + shown
            scores = scores.reshape(step * rows, key_count)
            weights = jnp.exp2(scores - jnp.max(scores, axis=1, keepdims=True))
            mixed = jnp.dot(
                weights.astype(jnp.bfloat16), values, preferred_element_type=jnp.float32
            )
            mixed = mixed[:, :HEAD] / mixed[:, HEAD:]
            mixed = mixed.reshape(step, local_frames, tokens, HEAD) * gates
            mixed = mixed.reshape(step, rows, HEAD).astype(jnp.bfloat16)
            for number in range(step):
                outs[start + number][:, part] = mixed[number]


def whole_heads(queries, keys, values, slot_of, level_of, gate_table):
    devices, groups = lax.axis_size("seq"), lax.axis_size("frame")
    near = min(2, devices)
    count = devices // near
    _, local_frames, tokens, all_width = queries.shape
    rows, width = local_frames * tokens, all_width // count

    def swap(taken, away):
        return lax.ppermute(taken, "seq", [(one, one ^ away) for one in range(devices)])

    def swap_far(taken):
        return [
            swap(one, away * near) if away else one for away, one in zip(far_first(count), taken)
        ]

    pieces = pl.pallas_call(
        functools.partial(pack, near=near),
        out_shape=[jax.ShapeDtypeStruct((3, rows, width), queries.dtype)] * count,
        in_specs=[HBM] * 3,
        out_specs=[VMEM] * count,
        scratch_shapes=[pltpu.SemaphoreType.DMA((count, 3))],
        compiler_params=PARAMS,
    )(
        *(
            pltpu.with_memory_space_constraint(taken.reshape(rows, all_width), pltpu.HBM)
            for taken in (queries, keys, values)
        ),
    )
    pieces = swap_far(pieces)
    held = pieces + [swap(piece, away) for away in range(1, near) for piece in pieces]
    pair = pl.pallas_call(
        stack,
        out_shape=jax.ShapeDtypeStruct((len(held), 2, rows, width), queries.dtype),
        in_specs=[VMEM] * len(held),
        out_specs=VMEM,
        scratch_shapes=[pltpu.SemaphoreType.DMA((len(held),))],
        compiler_params=PARAMS,
    )(*held)
    pairs = [
        lax.ppermute(pair, "frame", [(one, (one - away) % groups) for one in range(groups)])
        for away in range(1, groups)
    ]
    answers = pl.pallas_call(
        functools.partial(attend, pieces=count, near=near, tokens=tokens),
        out_shape=[jax.ShapeDtypeStruct((rows, width), queries.dtype)] * count,
        in_specs=[SMEM] * 2 + [VMEM] * (len(held) + groups),
        out_specs=[VMEM] * count,
        compiler_params=PARAMS,
    )(slot_of, level_of, gate_table, *held, *pairs)
    answers = swap_far(answers)
    answer = pl.pallas_call(
        functools.partial(unpack, near=near),
        out_shape=jax.ShapeDtypeStruct((rows, all_width), queries.dtype),
        in_specs=[VMEM] * count,
        out_specs=HBM,
        scratch_shapes=[pltpu.SemaphoreType.DMA((count,))],
        compiler_params=PARAMS,
    )(*answers)
    return answer.reshape(queries.shape)


def shared_heads(queries, keys, values, slot_of, level_of, gate_table):
    devices = lax.axis_size("frame") * lax.axis_size("seq")
    _, local_frames, tokens, _ = queries.shape
    rows, blocks = local_frames * tokens, devices // H
    block_rows = rows // blocks
    exchange = functools.partial(
        lax.all_to_all, axis_name=AXES, split_axis=0, concat_axis=0, tiled=True
    )

    def by_head(taken):
        return taken.reshape(rows, H, HEAD).transpose(1, 0, 2)

    def key_pieces(taken):
        pieces = jnp.broadcast_to(by_head(taken)[:, None], (H, blocks, rows, HEAD))
        return exchange(pieces.reshape(devices, rows, HEAD)).reshape(devices * rows, HEAD)

    key_rows, value_rows = key_pieces(keys), key_pieces(values)
    query_rows = exchange(by_head(queries).reshape(devices, block_rows, HEAD))
    query_rows = query_rows.reshape(devices * block_rows, HEAD)
    device_index = lax.axis_index("frame") * lax.axis_size("seq") + lax.axis_index("seq")
    head, block = device_index // blocks, device_index % blocks

    def per_row(table):
        table = jnp.repeat(table, tokens, axis=1)[:, None]
        return jnp.broadcast_to(table, (table.shape[0], lax.axis_size("seq"), rows))

    row_slots, row_levels = per_row(slot_of), per_row(level_of)
    query_slots = lax.dynamic_slice_in_dim(row_slots, block * block_rows, block_rows, 2)
    levels = lax.dynamic_slice_in_dim(row_levels, block * block_rows, block_rows, 2).reshape(-1)
    scores = lax.dot_general(
        query_rows, key_rows, (((1,), (1,)), ((), ())), preferred_element_type=jnp.float32
    )
    visible = row_slots.reshape(1, -1) <= query_slots.reshape(-1, 1)
    scores = jnp.where(visible, scores * (1.0 / math.sqrt(HEAD)), -jnp.inf)
    weights = jnp.exp(scores - jnp.max(scores, axis=1, keepdims=True)).astype(jnp.bfloat16)
    total = jnp.sum(weights.astype(jnp.float32), axis=1, keepdims=True)
    mixed = jnp.dot(weights, value_rows, preferred_element_type=jnp.float32) / total
    gates = lax.dynamic_slice_in_dim(gate_table, head * HEAD, HEAD, 1)[levels]
    answer = exchange((mixed * gates).astype(queries.dtype).reshape(devices, block_rows, HEAD))
    return answer.reshape(H, rows, HEAD).transpose(1, 0, 2).reshape(queries.shape)


def body(queries, *others):
    devices = lax.axis_size("seq")
    if devices > H or devices & (devices - 1):
        return shared_heads(queries, *others)
    return whole_heads(queries, *others)


def solution(mesh):
    return jax.shard_map(
        body,
        mesh=mesh,
        in_specs=(
            P(("rollout", "frame"), None, "seq", None),
            P(("rollout", "frame"), None, "seq", None),
            P(("rollout", "frame"), None, "seq", None),
            P("rollout", None),
            P("rollout", None),
            P(),
        ),
        out_specs=P(("rollout", "frame"), None, "seq", None),
        check_vma=False,
    )
```

```python
import functools
import math

import jax
import jax.numpy as jnp
from jax import lax
from jax.experimental import pallas as pl
from jax.experimental.pallas import tpu as pltpu
from jax.sharding import PartitionSpec as P

H = 16
HEAD = 128
AXES = ("frame", "seq")
SMEM = pl.BlockSpec(memory_space=pltpu.SMEM)
HBM = pl.BlockSpec(memory_space=pltpu.HBM)
VMEM = pl.BlockSpec(memory_space=pltpu.VMEM)
PARAMS = pltpu.CompilerParams(vmem_limit_bytes=32 * 1024 * 1024)


def far_first(count):
    return sorted(range(count), key=lambda away: (away > 0, -(2 * away // count), away % 2, -away))


def columns_of(place, width):
    return pl.ds(pl.multiple_of(place * width, width), width)


def run(copies):
    for copy in copies:
        copy.start()
    for copy in copies:
        copy.wait()


def pack(*refs, near):
    query_ref, key_ref, value_ref, *outs, sems = refs
    place = lax.axis_index("seq") // near
    count = len(outs) // 2
    copies = []
    for number, away in enumerate(far_first(count)):
        pair_ref, own_ref = outs[number], outs[count + number]
        columns = columns_of(place ^ away, own_ref.shape[-1])
        for kind, (ref, out_ref) in enumerate(
            ((key_ref, pair_ref.at[0]), (value_ref, pair_ref.at[1]), (query_ref, own_ref))
        ):
            copies.append(pltpu.make_async_copy(ref.at[:, columns], out_ref, sems.at[number, kind]))
    run(copies)


def stack(*refs):
    *pieces, out_ref, sems = refs
    run(
        [
            pltpu.make_async_copy(ref, out_ref.at[number], sems.at[number])
            for number, ref in enumerate(pieces)
        ]
    )


def unpack(*refs, near):
    answers, out_ref, sems = refs[:-2], refs[-2], refs[-1]
    place = lax.axis_index("seq") // near
    run(
        [
            pltpu.make_async_copy(
                ref, out_ref.at[:, columns_of(place ^ away, ref.shape[-1])], sems.at[number]
            )
            for number, (away, ref) in enumerate(zip(far_first(len(answers)), answers))
        ]
    )


def attend(slot_ref, level_ref, gate_ref, *refs, pieces, near, tokens):
    query_refs, refs, outs = refs[:pieces], refs[pieces:-pieces], refs[-pieces:]
    held_refs, stack_refs = refs[: near * pieces], refs[near * pieces :]
    rows, width = outs[0].shape
    group_count = 1 + len(stack_refs) // near
    local_frames = rows // tokens
    group_keys = near * pieces * rows
    key_count = group_count * group_keys
    group = lax.axis_index("frame")
    index = lax.broadcasted_iota(jnp.int32, (1, key_count), 1)
    frame = (index // group_keys + group) % group_count * local_frames
    frame = frame + index // tokens % local_frames
    key_slots = jnp.zeros((1, key_count), jnp.int32)
    for one in range(group_count * local_frames):
        slot = slot_ref[one // local_frames, one % local_frames]
        key_slots = jnp.where(frame == one, slot, key_slots)
    shown = []
    for local in range(local_frames):
        visible = key_slots <= slot_ref[group, local]
        shown.append(jnp.where(visible, 0.0, -jnp.inf).reshape(1, 1, 1, key_count))
    shown = jnp.concatenate(shown, axis=1)
    ones = jnp.ones((key_count, HEAD), jnp.bfloat16)
    scale = math.log2(math.e) / math.sqrt(HEAD)
    gate_blocks = gate_ref[:, columns_of(lax.axis_index("seq") // near, width)]
    level_rows = lax.broadcasted_iota(jnp.int32, gate_blocks.shape, 0)
    gate_rows = [
        jnp.sum(
            jnp.where(level_rows == level_ref[group, local], gate_blocks, 0.0),
            axis=0,
            keepdims=True,
        )
        for local in range(local_frames)
    ]
    step = max(1, min(pieces, 128 // rows))
    for column in range(0, width, HEAD):
        part = slice(column, column + HEAD)
        gates = jnp.concatenate([row[:, part].reshape(1, 1, 1, HEAD) for row in gate_rows], axis=1)
        keys, values = (
            jnp.concatenate(
                [ref[kind, :, part] for ref in held_refs]
                + [ref[:, kind, :, part].reshape(pieces * rows, HEAD) for ref in stack_refs]
            )
            for kind in range(2)
        )
        values = jnp.concatenate([values, ones], axis=1)
        for start in range(0, pieces, step):
            queries = jnp.concatenate([ref[:, part] for ref in query_refs[start : start + step]])
            scores = lax.dot_general(
                queries, keys, (((1,), (1,)), ((), ())), preferred_element_type=jnp.float32
            )
            scores = scores.reshape(step, local_frames, tokens, key_count) * scale + shown
            scores = scores.reshape(step * rows, key_count)
            weights = jnp.exp2(scores - jnp.max(scores, axis=1, keepdims=True))
            mixed = jnp.dot(
                weights.astype(jnp.bfloat16), values, preferred_element_type=jnp.float32
            )
            mixed = mixed[:, :HEAD] / mixed[:, HEAD:]
            mixed = mixed.reshape(step, local_frames, tokens, HEAD) * gates
            mixed = mixed.reshape(step, rows, HEAD).astype(jnp.bfloat16)
            for number in range(step):
                outs[start + number][:, part] = mixed[number]


def whole_heads(queries, keys, values, slot_of, level_of, gate_table):
    devices, groups = lax.axis_size("seq"), lax.axis_size("frame")
    near = min(2, devices)
    count = devices // near
    _, local_frames, tokens, all_width = queries.shape
    rows, width = local_frames * tokens, all_width // count

    def swap(taken, away):
        return lax.ppermute(taken, "seq", [(one, one ^ away) for one in range(devices)])

    def swap_far(taken):
        return [
            swap(one, away * near) if away else one for away, one in zip(far_first(count), taken)
        ]

    sent = pl.pallas_call(
        functools.partial(pack, near=near),
        out_shape=[jax.ShapeDtypeStruct((2, rows, width), queries.dtype)] * count
        + [jax.ShapeDtypeStruct((rows, width), queries.dtype)] * count,
        in_specs=[HBM] * 3,
        out_specs=[VMEM] * (2 * count),
        scratch_shapes=[pltpu.SemaphoreType.DMA((count, 3))],
        compiler_params=PARAMS,
    )(
        *(
            pltpu.with_memory_space_constraint(taken.reshape(rows, all_width), pltpu.HBM)
            for taken in (queries, keys, values)
        ),
    )
    pairs = swap_far(sent[:count])
    own = swap_far(sent[count:])
    held = [pairs] + [[swap(piece, away) for piece in pairs] for away in range(1, near)]
    stacks = [
        pl.pallas_call(
            stack,
            out_shape=jax.ShapeDtypeStruct((count, 2, rows, width), queries.dtype),
            in_specs=[VMEM] * count,
            out_specs=VMEM,
            scratch_shapes=[pltpu.SemaphoreType.DMA((count,))],
            compiler_params=PARAMS,
        )(*taken)
        for taken in held
    ]
    stacks = [
        lax.ppermute(taken, "frame", [(one, (one - away) % groups) for one in range(groups)])
        for away in range(1, groups)
        for taken in stacks
    ]
    held = sum(held, [])
    answers = pl.pallas_call(
        functools.partial(attend, pieces=count, near=near, tokens=tokens),
        out_shape=[jax.ShapeDtypeStruct((rows, width), queries.dtype)] * count,
        in_specs=[SMEM] * 2 + [VMEM] * (1 + count + len(held) + len(stacks)),
        out_specs=[VMEM] * count,
        compiler_params=PARAMS,
    )(slot_of, level_of, gate_table, *own, *held, *stacks)
    answers = swap_far(answers)
    answer = pl.pallas_call(
        functools.partial(unpack, near=near),
        out_shape=jax.ShapeDtypeStruct((rows, all_width), queries.dtype),
        in_specs=[VMEM] * count,
        out_specs=HBM,
        scratch_shapes=[pltpu.SemaphoreType.DMA((count,))],
        compiler_params=PARAMS,
    )(*answers)
    return answer.reshape(queries.shape)


def shared_heads(queries, keys, values, slot_of, level_of, gate_table):
    devices = lax.axis_size("frame") * lax.axis_size("seq")
    _, local_frames, tokens, _ = queries.shape
    rows, blocks = local_frames * tokens, devices // H
    block_rows = rows // blocks
    exchange = functools.partial(
        lax.all_to_all, axis_name=AXES, split_axis=0, concat_axis=0, tiled=True
    )

    def by_head(taken):
        return taken.reshape(rows, H, HEAD).transpose(1, 0, 2)

    def key_pieces(taken):
        pieces = jnp.broadcast_to(by_head(taken)[:, None], (H, blocks, rows, HEAD))
        return exchange(pieces.reshape(devices, rows, HEAD)).reshape(devices * rows, HEAD)

    key_rows, value_rows = key_pieces(keys), key_pieces(values)
    query_rows = exchange(by_head(queries).reshape(devices, block_rows, HEAD))
    query_rows = query_rows.reshape(devices * block_rows, HEAD)
    device_index = lax.axis_index("frame") * lax.axis_size("seq") + lax.axis_index("seq")
    head, block = device_index // blocks, device_index % blocks

    def per_row(table):
        table = jnp.repeat(table, tokens, axis=1)[:, None]
        return jnp.broadcast_to(table, (table.shape[0], lax.axis_size("seq"), rows))

    row_slots, row_levels = per_row(slot_of), per_row(level_of)
    query_slots = lax.dynamic_slice_in_dim(row_slots, block * block_rows, block_rows, 2)
    levels = lax.dynamic_slice_in_dim(row_levels, block * block_rows, block_rows, 2).reshape(-1)
    scores = lax.dot_general(
        query_rows, key_rows, (((1,), (1,)), ((), ())), preferred_element_type=jnp.float32
    )
    visible = row_slots.reshape(1, -1) <= query_slots.reshape(-1, 1)
    scores = jnp.where(visible, scores * (1.0 / math.sqrt(HEAD)), -jnp.inf)
    weights = jnp.exp(scores - jnp.max(scores, axis=1, keepdims=True)).astype(jnp.bfloat16)
    total = jnp.sum(weights.astype(jnp.float32), axis=1, keepdims=True)
    mixed = jnp.dot(weights, value_rows, preferred_element_type=jnp.float32) / total
    gates = lax.dynamic_slice_in_dim(gate_table, head * HEAD, HEAD, 1)[levels]
    answer = exchange((mixed * gates).astype(queries.dtype).reshape(devices, block_rows, HEAD))
    return answer.reshape(H, rows, HEAD).transpose(1, 0, 2).reshape(queries.shape)


def body(queries, *others):
    devices = lax.axis_size("seq")
    if devices > H or devices & (devices - 1):
        return shared_heads(queries, *others)
    return whole_heads(queries, *others)


def solution(mesh):
    return jax.shard_map(
        body,
        mesh=mesh,
        in_specs=(
            P(("rollout", "frame"), None, "seq", None),
            P(("rollout", "frame"), None, "seq", None),
            P(("rollout", "frame"), None, "seq", None),
            P("rollout", None),
            P("rollout", None),
            P(),
        ),
        out_specs=P(("rollout", "frame"), None, "seq", None),
        check_vma=False,
    )
```

```python
import functools
import math

import jax
import jax.numpy as jnp
from jax import lax
from jax.experimental import pallas as pl
from jax.experimental.pallas import tpu as pltpu
from jax.sharding import PartitionSpec as P

H = 16
HEAD = 128
AXES = ("frame", "seq")
SMEM = pl.BlockSpec(memory_space=pltpu.SMEM)
HBM = pl.BlockSpec(memory_space=pltpu.HBM)
VMEM = pl.BlockSpec(memory_space=pltpu.VMEM)
PARAMS = pltpu.CompilerParams(vmem_limit_bytes=32 * 1024 * 1024)


def columns_of(place, width):
    return pl.ds(pl.multiple_of(place * width, width), width)


def run(copies):
    for copy in copies:
        copy.start()
    for copy in copies:
        copy.wait()


def pack(*refs, near):
    query_ref, key_ref, value_ref, *outs, sems = refs
    place = lax.axis_index("seq") // near
    count = len(outs) // 2
    copies = []
    for away in range(count):
        pair_ref, own_ref = outs[away], outs[count + away]
        columns = columns_of(place ^ away, own_ref.shape[-1])
        for kind, (ref, out_ref) in enumerate(
            ((key_ref, pair_ref.at[0]), (value_ref, pair_ref.at[1]), (query_ref, own_ref))
        ):
            copies.append(pltpu.make_async_copy(ref.at[:, columns], out_ref, sems.at[away, kind]))
    run(copies)


def stack(*refs, count):
    *refs, sems = refs
    outs = refs[-(len(refs) // (count + 1)) :]
    run(
        [
            pltpu.make_async_copy(ref, outs[number // count].at[number % count], sems.at[number])
            for number, ref in enumerate(refs[: -len(outs)])
        ]
    )


def unpack(*refs, near):
    *answers, out_ref, sems = refs
    place = lax.axis_index("seq") // near
    run(
        [
            pltpu.make_async_copy(
                ref, out_ref.at[:, columns_of(place ^ away, ref.shape[-1])], sems.at[away]
            )
            for away, ref in enumerate(answers)
        ]
    )


def attend(slot_ref, level_ref, gate_ref, query_ref, *refs, near, tokens):
    pieces = query_ref.shape[0]
    refs, outs = refs[:-pieces], refs[-pieces:]
    held_refs, stack_refs = refs[: near * pieces], refs[near * pieces :]
    rows, width = outs[0].shape
    group_count = 1 + len(stack_refs) // near
    local_frames = rows // tokens
    group_keys = near * pieces * rows
    key_count = group_count * group_keys
    group = lax.axis_index("frame")
    index = lax.broadcasted_iota(jnp.int32, (1, key_count), 1)
    frame = (index // group_keys + group) % group_count * local_frames
    frame = frame + index // tokens % local_frames
    key_slots = jnp.zeros((1, key_count), jnp.int32)
    for one in range(group_count * local_frames):
        slot = slot_ref[one // local_frames, one % local_frames]
        key_slots = jnp.where(frame == one, slot, key_slots)
    shown = []
    for local in range(local_frames):
        visible = key_slots <= slot_ref[group, local]
        shown.append(jnp.where(visible, 0.0, -jnp.inf).reshape(1, 1, 1, key_count))
    shown = jnp.concatenate(shown, axis=1)
    ones = jnp.ones((key_count, HEAD), jnp.bfloat16)
    scale = math.log2(math.e) / math.sqrt(HEAD)
    gate_blocks = gate_ref[:, columns_of(lax.axis_index("seq") // near, width)]
    level_rows = lax.broadcasted_iota(jnp.int32, gate_blocks.shape, 0)
    gate_rows = [
        jnp.sum(
            jnp.where(level_rows == level_ref[group, local], gate_blocks, 0.0),
            axis=0,
            keepdims=True,
        )
        for local in range(local_frames)
    ]
    step = max(1, min(pieces, 128 // rows))
    for column in range(0, width, HEAD):
        part = slice(column, column + HEAD)
        gates = jnp.concatenate([row[:, part].reshape(1, 1, 1, HEAD) for row in gate_rows], axis=1)
        keys, values = (
            jnp.concatenate(
                [ref[kind, :, part] for ref in held_refs]
                + [ref[:, kind, :, part].reshape(pieces * rows, HEAD) for ref in stack_refs]
            )
            for kind in range(2)
        )
        values = jnp.concatenate([values, ones], axis=1)
        for start in range(0, pieces, step):
            queries = query_ref[start : start + step, :, part].reshape(step * rows, HEAD)
            scores = lax.dot_general(
                queries, keys, (((1,), (1,)), ((), ())), preferred_element_type=jnp.float32
            )
            scores = scores.reshape(step, local_frames, tokens, key_count) * scale + shown
            scores = scores.reshape(step * rows, key_count)
            weights = jnp.exp2(scores - jnp.max(scores, axis=1, keepdims=True))
            mixed = jnp.dot(
                weights.astype(jnp.bfloat16), values, preferred_element_type=jnp.float32
            )
            mixed = mixed[:, :HEAD] / mixed[:, HEAD:]
            mixed = mixed.reshape(step, local_frames, tokens, HEAD) * gates
            mixed = mixed.reshape(step, rows, HEAD).astype(jnp.bfloat16)
            for number in range(step):
                outs[start + number][:, part] = mixed[number]


def whole_heads(queries, keys, values, slot_of, level_of, gate_table):
    devices, groups = lax.axis_size("seq"), lax.axis_size("frame")
    near = min(2, devices)
    count = devices // near
    _, local_frames, tokens, all_width = queries.shape
    rows, width = local_frames * tokens, all_width // count

    def swap(taken, away):
        return lax.ppermute(taken, "seq", [(one, one ^ away) for one in range(devices)])

    def swap_far(taken):
        return [swap(one, away * near) if away else one for away, one in enumerate(taken)]

    sent = pl.pallas_call(
        functools.partial(pack, near=near),
        out_shape=[jax.ShapeDtypeStruct((2, rows, width), queries.dtype)] * count
        + [jax.ShapeDtypeStruct((rows, width), queries.dtype)] * count,
        in_specs=[HBM] * 3,
        out_specs=[VMEM] * (2 * count),
        scratch_shapes=[pltpu.SemaphoreType.DMA((count, 3))],
        compiler_params=PARAMS,
    )(
        *(
            pltpu.with_memory_space_constraint(taken.reshape(rows, all_width), pltpu.HBM)
            for taken in (queries, keys, values)
        ),
    )
    pairs = swap_far(sent[:count])
    own = swap_far(sent[count:])
    held = [pairs] + [[swap(piece, away) for piece in pairs] for away in range(1, near)]

    def stacked(*kinds):
        return pl.pallas_call(
            functools.partial(stack, count=count),
            out_shape=[
                jax.ShapeDtypeStruct((count,) + taken[0].shape, queries.dtype) for taken in kinds
            ],
            in_specs=[VMEM] * (len(kinds) * count),
            out_specs=[VMEM] * len(kinds),
            scratch_shapes=[pltpu.SemaphoreType.DMA((len(kinds) * count,))],
            compiler_params=PARAMS,
        )(*sum(kinds, []))

    stacks = [stacked(taken)[0] for taken in held[:-1]]
    last, own = stacked(held[-1], own)
    stacks.append(last)
    stacks = [
        lax.ppermute(taken, "frame", [(one, (one - away) % groups) for one in range(groups)])
        for away in range(1, groups)
        for taken in stacks
    ]
    held = sum(held, [])
    answers = pl.pallas_call(
        functools.partial(attend, near=near, tokens=tokens),
        out_shape=[jax.ShapeDtypeStruct((rows, width), queries.dtype)] * count,
        in_specs=[SMEM] * 2 + [VMEM] * (2 + len(held) + len(stacks)),
        out_specs=[VMEM] * count,
        compiler_params=PARAMS,
    )(slot_of, level_of, gate_table, own, *held, *stacks)
    answers = swap_far(answers)
    answer = pl.pallas_call(
        functools.partial(unpack, near=near),
        out_shape=jax.ShapeDtypeStruct((rows, all_width), queries.dtype),
        in_specs=[VMEM] * count,
        out_specs=HBM,
        scratch_shapes=[pltpu.SemaphoreType.DMA((count,))],
        compiler_params=PARAMS,
    )(*answers)
    return answer.reshape(queries.shape)


def shared_heads(queries, keys, values, slot_of, level_of, gate_table):
    devices = lax.axis_size("frame") * lax.axis_size("seq")
    _, local_frames, tokens, _ = queries.shape
    rows, blocks = local_frames * tokens, devices // H
    block_rows = rows // blocks
    exchange = functools.partial(
        lax.all_to_all, axis_name=AXES, split_axis=0, concat_axis=0, tiled=True
    )

    def by_head(taken):
        return taken.reshape(rows, H, HEAD).transpose(1, 0, 2)

    def key_pieces(taken):
        pieces = jnp.broadcast_to(by_head(taken)[:, None], (H, blocks, rows, HEAD))
        return exchange(pieces.reshape(devices, rows, HEAD)).reshape(devices * rows, HEAD)

    key_rows, value_rows = key_pieces(keys), key_pieces(values)
    query_rows = exchange(by_head(queries).reshape(devices, block_rows, HEAD))
    query_rows = query_rows.reshape(devices * block_rows, HEAD)
    device_index = lax.axis_index("frame") * lax.axis_size("seq") + lax.axis_index("seq")
    head, block = device_index // blocks, device_index % blocks

    def per_row(table):
        table = jnp.repeat(table, tokens, axis=1)[:, None]
        return jnp.broadcast_to(table, (table.shape[0], lax.axis_size("seq"), rows))

    row_slots, row_levels = per_row(slot_of), per_row(level_of)
    query_slots = lax.dynamic_slice_in_dim(row_slots, block * block_rows, block_rows, 2)
    levels = lax.dynamic_slice_in_dim(row_levels, block * block_rows, block_rows, 2).reshape(-1)
    scores = lax.dot_general(
        query_rows, key_rows, (((1,), (1,)), ((), ())), preferred_element_type=jnp.float32
    )
    visible = row_slots.reshape(1, -1) <= query_slots.reshape(-1, 1)
    scores = jnp.where(visible, scores * (1.0 / math.sqrt(HEAD)), -jnp.inf)
    weights = jnp.exp(scores - jnp.max(scores, axis=1, keepdims=True)).astype(jnp.bfloat16)
    total = jnp.sum(weights.astype(jnp.float32), axis=1, keepdims=True)
    mixed = jnp.dot(weights, value_rows, preferred_element_type=jnp.float32) / total
    gates = lax.dynamic_slice_in_dim(gate_table, head * HEAD, HEAD, 1)[levels]
    answer = exchange((mixed * gates).astype(queries.dtype).reshape(devices, block_rows, HEAD))
    return answer.reshape(H, rows, HEAD).transpose(1, 0, 2).reshape(queries.shape)


def body(queries, *others):
    devices = lax.axis_size("seq")
    if devices > H or devices & (devices - 1):
        return shared_heads(queries, *others)
    return whole_heads(queries, *others)


def solution(mesh):
    return jax.shard_map(
        body,
        mesh=mesh,
        in_specs=(
            P(("rollout", "frame"), None, "seq", None),
            P(("rollout", "frame"), None, "seq", None),
            P(("rollout", "frame"), None, "seq", None),
            P("rollout", None),
            P("rollout", None),
            P(),
        ),
        out_specs=P(("rollout", "frame"), None, "seq", None),
        check_vma=False,
    )
```

```python
import functools
import math

import jax
import jax.numpy as jnp
from jax import lax
from jax.experimental import pallas as pl
from jax.experimental.pallas import tpu as pltpu
from jax.sharding import PartitionSpec as P

H = 16
HEAD = 128
AXES = ("frame", "seq")
SMEM = pl.BlockSpec(memory_space=pltpu.SMEM)
HBM = pl.BlockSpec(memory_space=pltpu.HBM)
VMEM = pl.BlockSpec(memory_space=pltpu.VMEM)
PARAMS = pltpu.CompilerParams(vmem_limit_bytes=32 * 1024 * 1024)


def attend(slot_ref, level_ref, gate_ref, query_ref, key_ref, value_ref, out_ref, *, tokens):
    rows, width = query_ref.shape
    groups, local_frames = slot_ref.shape
    group = lax.axis_index("frame")
    key_count = key_ref.shape[0]
    index = lax.broadcasted_iota(jnp.int32, (1, key_count), 1)
    frame = index // (key_count // groups) * local_frames + index // tokens % local_frames
    key_slots = jnp.zeros((1, key_count), jnp.int32)
    for one in range(groups * local_frames):
        slot = slot_ref[one // local_frames, one % local_frames]
        key_slots = jnp.where(frame == one, slot, key_slots)
    shown = []
    for local in range(local_frames):
        visible = key_slots <= slot_ref[group, local]
        shown.append(jnp.where(visible, 0.0, -jnp.inf).reshape(1, 1, key_count))
    shown = jnp.concatenate(shown, axis=0)
    gate_blocks = gate_ref[...]
    level_rows = lax.broadcasted_iota(jnp.int32, gate_blocks.shape, 0)
    gate_rows = [
        jnp.sum(
            jnp.where(level_rows == level_ref[group, local], gate_blocks, 0.0),
            axis=0,
            keepdims=True,
        )
        for local in range(local_frames)
    ]
    ones = jnp.ones((key_count, HEAD), jnp.bfloat16)
    scale = math.log2(math.e) / math.sqrt(HEAD)
    for column in range(0, width, HEAD):
        part = slice(column, column + HEAD)
        gates = jnp.concatenate([row[:, part].reshape(1, 1, HEAD) for row in gate_rows], axis=0)
        scores = lax.dot_general(
            query_ref[:, part],
            key_ref[:, part],
            (((1,), (1,)), ((), ())),
            preferred_element_type=jnp.float32,
        )
        scores = scores.reshape(local_frames, tokens, key_count) * scale + shown
        scores = scores.reshape(rows, key_count)
        weights = jnp.exp2(scores - jnp.max(scores, axis=1, keepdims=True))
        values = jnp.concatenate([value_ref[:, part], ones], axis=1)
        mixed = jnp.dot(weights.astype(jnp.bfloat16), values, preferred_element_type=jnp.float32)
        mixed = (mixed[:, :HEAD] / mixed[:, HEAD:]).reshape(local_frames, tokens, HEAD) * gates
        out_ref[:, part] = mixed.reshape(rows, HEAD).astype(out_ref.dtype)


def whole_heads(queries, keys, values, slot_of, level_of, gate_table):
    _, local_frames, tokens, width = queries.shape
    rows = local_frames * tokens
    keys, values = (
        lax.all_gather(taken.reshape(rows, width), AXES, axis=0, tiled=True)
        for taken in (keys, values)
    )
    answer = pl.pallas_call(
        functools.partial(attend, tokens=tokens),
        out_shape=jax.ShapeDtypeStruct((rows, width), queries.dtype),
        in_specs=[SMEM] * 2 + [VMEM] * 4,
        out_specs=VMEM,
        compiler_params=PARAMS,
    )(slot_of, level_of, gate_table, queries.reshape(rows, width), keys, values)
    return answer.reshape(queries.shape)


def shared_heads(queries, keys, values, slot_of, level_of, gate_table):
    devices = lax.axis_size("frame") * lax.axis_size("seq")
    _, local_frames, tokens, _ = queries.shape
    rows, blocks = local_frames * tokens, devices // H
    block_rows = rows // blocks
    exchange = functools.partial(
        lax.all_to_all, axis_name=AXES, split_axis=0, concat_axis=0, tiled=True
    )

    def by_head(taken):
        return taken.reshape(rows, H, HEAD).transpose(1, 0, 2)

    def key_pieces(taken):
        pieces = jnp.broadcast_to(by_head(taken)[:, None], (H, blocks, rows, HEAD))
        return exchange(pieces.reshape(devices, rows, HEAD)).reshape(devices * rows, HEAD)

    key_rows, value_rows = key_pieces(keys), key_pieces(values)
    query_rows = exchange(by_head(queries).reshape(devices, block_rows, HEAD))
    query_rows = query_rows.reshape(devices * block_rows, HEAD)
    device_index = lax.axis_index("frame") * lax.axis_size("seq") + lax.axis_index("seq")
    head, block = device_index // blocks, device_index % blocks

    def per_row(table):
        table = jnp.repeat(table, tokens, axis=1)[:, None]
        return jnp.broadcast_to(table, (table.shape[0], lax.axis_size("seq"), rows))

    row_slots, row_levels = per_row(slot_of), per_row(level_of)
    query_slots = lax.dynamic_slice_in_dim(row_slots, block * block_rows, block_rows, 2)
    levels = lax.dynamic_slice_in_dim(row_levels, block * block_rows, block_rows, 2).reshape(-1)
    scores = lax.dot_general(
        query_rows, key_rows, (((1,), (1,)), ((), ())), preferred_element_type=jnp.float32
    )
    visible = row_slots.reshape(1, -1) <= query_slots.reshape(-1, 1)
    scores = jnp.where(visible, scores * (1.0 / math.sqrt(HEAD)), -jnp.inf)
    weights = jnp.exp(scores - jnp.max(scores, axis=1, keepdims=True)).astype(jnp.bfloat16)
    total = jnp.sum(weights.astype(jnp.float32), axis=1, keepdims=True)
    mixed = jnp.dot(weights, value_rows, preferred_element_type=jnp.float32) / total
    gates = lax.dynamic_slice_in_dim(gate_table, head * HEAD, HEAD, 1)[levels]
    answer = exchange((mixed * gates).astype(queries.dtype).reshape(devices, block_rows, HEAD))
    return answer.reshape(H, rows, HEAD).transpose(1, 0, 2).reshape(queries.shape)


def body(queries, *others):
    if lax.axis_size("seq") > H:
        return shared_heads(queries, *others)
    return whole_heads(queries, *others)


def solution(mesh):
    return jax.shard_map(
        body,
        mesh=mesh,
        in_specs=(
            P(("rollout", "frame"), None, "seq", None),
            P(("rollout", "frame"), None, "seq", None),
            P(("rollout", "frame"), None, "seq", None),
            P("rollout", None),
            P("rollout", None),
            P(),
        ),
        out_specs=P(("rollout", "frame"), None, "seq", None),
        check_vma=False,
    )
```

```python
import functools
import math

import jax
import jax.numpy as jnp
from jax import lax
from jax.experimental import pallas as pl
from jax.experimental.pallas import tpu as pltpu
from jax.sharding import PartitionSpec as P

H = 16
HEAD = 128
AXES = ("frame", "seq")
SMEM = pl.BlockSpec(memory_space=pltpu.SMEM)
HBM = pl.BlockSpec(memory_space=pltpu.HBM)
VMEM = pl.BlockSpec(memory_space=pltpu.VMEM)
PARAMS = pltpu.CompilerParams(vmem_limit_bytes=32 * 1024 * 1024)


def columns_of(place, width):
    return pl.ds(pl.multiple_of(place * width, width), width)


def run(copies):
    for copy in copies:
        copy.start()
    for copy in copies:
        copy.wait()


def pack(*refs):
    *operands, out_ref, sems = refs
    run(
        [
            pltpu.make_async_copy(
                ref.at[:, columns_of(device, out_ref.shape[-1])],
                out_ref.at[device, kind],
                sems.at[device, kind],
            )
            for device in range(out_ref.shape[0])
            for kind, ref in enumerate(operands)
        ]
    )


def unpack(held_ref, out_ref, sems):
    devices, _, width = held_ref.shape
    run(
        [
            pltpu.make_async_copy(
                held_ref.at[device], out_ref.at[:, columns_of(device, width)], sems.at[device]
            )
            for device in range(devices)
        ]
    )


def attend(slot_ref, level_ref, gate_ref, packed_ref, out_ref, *, tokens):
    groups, local_frames = slot_ref.shape
    devices, rows, width = out_ref.shape
    group_devices = devices // groups
    group_rows = group_devices * rows
    key_count = devices * rows
    index = lax.broadcasted_iota(jnp.int32, (1, key_count), 1)
    frame = index // group_rows * local_frames + index // tokens % local_frames
    key_slots = jnp.zeros((1, key_count), jnp.int32)
    for one in range(groups * local_frames):
        slot = slot_ref[one // local_frames, one % local_frames]
        key_slots = jnp.where(frame == one, slot, key_slots)
    gate_blocks = gate_ref[
        :, columns_of(lax.axis_index("frame") * lax.axis_size("seq") + lax.axis_index("seq"), width)
    ]
    level_rows = lax.broadcasted_iota(jnp.int32, gate_blocks.shape, 0)
    ones = jnp.ones((key_count, HEAD), jnp.bfloat16)
    scale = math.log2(math.e) / math.sqrt(HEAD)
    step = max(1, min(group_devices, 128 // rows))
    for group in range(groups):
        shown, gate_rows = [], []
        for local in range(local_frames):
            visible = key_slots <= slot_ref[group, local]
            shown.append(jnp.where(visible, 0.0, -jnp.inf).reshape(1, 1, 1, key_count))
            gate = jnp.where(level_rows == level_ref[group, local], gate_blocks, 0.0)
            gate_rows.append(jnp.sum(gate, axis=0, keepdims=True))
        shown = jnp.concatenate(shown, axis=1)
        for column in range(0, width, HEAD):
            part = slice(column, column + HEAD)
            gates = [row[:, part].reshape(1, 1, 1, HEAD) for row in gate_rows]
            gates = jnp.concatenate(gates, axis=1)
            keys = packed_ref[:, 1, :, part].reshape(key_count, HEAD)
            values = packed_ref[:, 2, :, part].reshape(key_count, HEAD)
            values = jnp.concatenate([values, ones], axis=1)
            for start in range(group * group_devices, (group + 1) * group_devices, step):
                queries = packed_ref[start : start + step, 0, :, part].reshape(step * rows, HEAD)
                scores = lax.dot_general(
                    queries, keys, (((1,), (1,)), ((), ())), preferred_element_type=jnp.float32
                )
                scores = scores.reshape(step, local_frames, tokens, key_count) * scale + shown
                scores = scores.reshape(step * rows, key_count)
                weights = jnp.exp2(scores - jnp.max(scores, axis=1, keepdims=True))
                mixed = jnp.dot(
                    weights.astype(jnp.bfloat16), values, preferred_element_type=jnp.float32
                )
                mixed = mixed[:, :HEAD] / mixed[:, HEAD:]
                mixed = mixed.reshape(step, local_frames, tokens, HEAD) * gates
                out_ref[start : start + step, :, part] = mixed.reshape(step, rows, HEAD).astype(
                    out_ref.dtype
                )


def whole_heads(queries, keys, values, slot_of, level_of, gate_table):
    devices = lax.axis_size("frame") * lax.axis_size("seq")
    _, local_frames, tokens, all_width = queries.shape
    rows, width = local_frames * tokens, all_width // devices
    exchange = functools.partial(
        lax.all_to_all, axis_name=AXES, split_axis=0, concat_axis=0, tiled=True
    )
    packed = pl.pallas_call(
        pack,
        out_shape=jax.ShapeDtypeStruct((devices, 3, rows, width), queries.dtype),
        in_specs=[HBM] * 3,
        out_specs=VMEM,
        scratch_shapes=[pltpu.SemaphoreType.DMA((devices, 3))],
        compiler_params=PARAMS,
    )(
        *(
            pltpu.with_memory_space_constraint(taken.reshape(rows, all_width), pltpu.HBM)
            for taken in (queries, keys, values)
        )
    )
    answer = pl.pallas_call(
        functools.partial(attend, tokens=tokens),
        out_shape=jax.ShapeDtypeStruct((devices, rows, width), queries.dtype),
        in_specs=[SMEM] * 2 + [VMEM] * 2,
        out_specs=VMEM,
        compiler_params=PARAMS,
    )(slot_of, level_of, gate_table, exchange(packed))
    answer = pl.pallas_call(
        unpack,
        out_shape=jax.ShapeDtypeStruct((rows, all_width), queries.dtype),
        in_specs=[VMEM],
        out_specs=HBM,
        scratch_shapes=[pltpu.SemaphoreType.DMA((devices,))],
        compiler_params=PARAMS,
    )(exchange(answer))
    return answer.reshape(queries.shape)


def shared_heads(queries, keys, values, slot_of, level_of, gate_table):
    devices = lax.axis_size("frame") * lax.axis_size("seq")
    _, local_frames, tokens, _ = queries.shape
    rows, blocks = local_frames * tokens, devices // H
    block_rows = rows // blocks
    exchange = functools.partial(
        lax.all_to_all, axis_name=AXES, split_axis=0, concat_axis=0, tiled=True
    )

    def by_head(taken):
        return taken.reshape(rows, H, HEAD).transpose(1, 0, 2)

    def key_pieces(taken):
        pieces = jnp.broadcast_to(by_head(taken)[:, None], (H, blocks, rows, HEAD))
        return exchange(pieces.reshape(devices, rows, HEAD)).reshape(devices * rows, HEAD)

    key_rows, value_rows = key_pieces(keys), key_pieces(values)
    query_rows = exchange(by_head(queries).reshape(devices, block_rows, HEAD))
    query_rows = query_rows.reshape(devices * block_rows, HEAD)
    device_index = lax.axis_index("frame") * lax.axis_size("seq") + lax.axis_index("seq")
    head, block = device_index // blocks, device_index % blocks

    def per_row(table):
        table = jnp.repeat(table, tokens, axis=1)[:, None]
        return jnp.broadcast_to(table, (table.shape[0], lax.axis_size("seq"), rows))

    row_slots, row_levels = per_row(slot_of), per_row(level_of)
    query_slots = lax.dynamic_slice_in_dim(row_slots, block * block_rows, block_rows, 2)
    levels = lax.dynamic_slice_in_dim(row_levels, block * block_rows, block_rows, 2).reshape(-1)
    scores = lax.dot_general(
        query_rows, key_rows, (((1,), (1,)), ((), ())), preferred_element_type=jnp.float32
    )
    visible = row_slots.reshape(1, -1) <= query_slots.reshape(-1, 1)
    scores = jnp.where(visible, scores * (1.0 / math.sqrt(HEAD)), -jnp.inf)
    weights = jnp.exp(scores - jnp.max(scores, axis=1, keepdims=True)).astype(jnp.bfloat16)
    total = jnp.sum(weights.astype(jnp.float32), axis=1, keepdims=True)
    mixed = jnp.dot(weights, value_rows, preferred_element_type=jnp.float32) / total
    gates = lax.dynamic_slice_in_dim(gate_table, head * HEAD, HEAD, 1)[levels]
    answer = exchange((mixed * gates).astype(queries.dtype).reshape(devices, block_rows, HEAD))
    return answer.reshape(H, rows, HEAD).transpose(1, 0, 2).reshape(queries.shape)


def body(queries, *others):
    if lax.axis_size("frame") * lax.axis_size("seq") > H:
        return shared_heads(queries, *others)
    return whole_heads(queries, *others)


def solution(mesh):
    return jax.shard_map(
        body,
        mesh=mesh,
        in_specs=(
            P(("rollout", "frame"), None, "seq", None),
            P(("rollout", "frame"), None, "seq", None),
            P(("rollout", "frame"), None, "seq", None),
            P("rollout", None),
            P("rollout", None),
            P(),
        ),
        out_specs=P(("rollout", "frame"), None, "seq", None),
        check_vma=False,
    )
```

```python
import functools
import math

import jax
import jax.numpy as jnp
from jax import lax
from jax.experimental import pallas as pl
from jax.experimental.pallas import tpu as pltpu
from jax.sharding import PartitionSpec as P

H = 16
HEAD = 128
AXES = ("frame", "seq")
SMEM = pl.BlockSpec(memory_space=pltpu.SMEM)
HBM = pl.BlockSpec(memory_space=pltpu.HBM)
VMEM = pl.BlockSpec(memory_space=pltpu.VMEM)
PARAMS = pltpu.CompilerParams(vmem_limit_bytes=32 * 1024 * 1024)


def columns_of(place, width):
    return pl.ds(pl.multiple_of(place * width, width), width)


def run(copies):
    for copy in copies:
        copy.start()
    for copy in copies:
        copy.wait()


def pack(*refs, near):
    query_ref, key_ref, value_ref, *outs, sems = refs
    place = lax.axis_index("seq") // near
    count = len(outs) // 2
    copies = []
    for away in range(count):
        pair_ref, own_ref = outs[away], outs[count + away]
        columns = columns_of(place ^ away, own_ref.shape[-1])
        for kind, (ref, out_ref) in enumerate(
            ((key_ref, pair_ref.at[0]), (value_ref, pair_ref.at[1]), (query_ref, own_ref))
        ):
            copies.append(pltpu.make_async_copy(ref.at[:, columns], out_ref, sems.at[away, kind]))
    run(copies)


def move(*refs, plan):
    *refs, sems = refs
    outs = refs[len(plan) :]
    run(
        [
            pltpu.make_async_copy(
                ref, outs[number] if at is None else outs[number].at[at], sems.at[one]
            )
            for one, (ref, (number, at)) in enumerate(zip(refs, plan))
        ]
    )


def unpack(*refs, near):
    *answers, out_ref, sems = refs
    place = lax.axis_index("seq") // near
    run(
        [
            pltpu.make_async_copy(
                ref, out_ref.at[:, columns_of(place ^ away, ref.shape[-1])], sems.at[away]
            )
            for away, ref in enumerate(answers)
        ]
    )


def attend(slot_ref, level_ref, gate_ref, query_ref, *refs, near, tokens):
    pieces = query_ref.shape[0]
    refs, outs = refs[:-pieces], refs[-pieces:]
    held_refs, stack_refs = refs[: near * pieces], refs[near * pieces :]
    rows, width = outs[0].shape
    group_count = slot_ref.shape[0]
    local_frames = rows // tokens
    group_keys = near * pieces * rows
    key_count = group_count * group_keys
    group = lax.axis_index("frame")
    index = lax.broadcasted_iota(jnp.int32, (1, key_count), 1)
    frame = (index // group_keys + group) % group_count * local_frames
    frame = frame + index // tokens % local_frames
    key_slots = jnp.zeros((1, key_count), jnp.int32)
    for one in range(group_count * local_frames):
        slot = slot_ref[one // local_frames, one % local_frames]
        key_slots = jnp.where(frame == one, slot, key_slots)
    shown = []
    for local in range(local_frames):
        visible = key_slots <= slot_ref[group, local]
        shown.append(jnp.where(visible, 0.0, -jnp.inf).reshape(1, 1, 1, key_count))
    shown = jnp.concatenate(shown, axis=1)
    ones = jnp.ones((key_count, HEAD), jnp.bfloat16)
    scale = math.log2(math.e) / math.sqrt(HEAD)
    gate_blocks = gate_ref[:, columns_of(lax.axis_index("seq") // near, width)]
    level_rows = lax.broadcasted_iota(jnp.int32, gate_blocks.shape, 0)
    gate_rows = [
        jnp.sum(
            jnp.where(level_rows == level_ref[group, local], gate_blocks, 0.0),
            axis=0,
            keepdims=True,
        )
        for local in range(local_frames)
    ]
    step = max(1, min(pieces, 128 // rows))
    for column in range(0, width, HEAD):
        part = slice(column, column + HEAD)
        gates = jnp.concatenate([row[:, part].reshape(1, 1, 1, HEAD) for row in gate_rows], axis=1)
        keys, values = (
            jnp.concatenate(
                [ref[kind, :, part] for ref in held_refs]
                + [ref[:, kind, :, part].reshape(ref.shape[0] * rows, HEAD) for ref in stack_refs]
            )
            for kind in range(2)
        )
        values = jnp.concatenate([values, ones], axis=1)
        for start in range(0, pieces, step):
            queries = query_ref[start : start + step, :, part].reshape(step * rows, HEAD)
            scores = lax.dot_general(
                queries, keys, (((1,), (1,)), ((), ())), preferred_element_type=jnp.float32
            )
            scores = scores.reshape(step, local_frames, tokens, key_count) * scale + shown
            scores = scores.reshape(step * rows, key_count)
            weights = jnp.exp2(scores - jnp.max(scores, axis=1, keepdims=True))
            mixed = jnp.dot(
                weights.astype(jnp.bfloat16), values, preferred_element_type=jnp.float32
            )
            mixed = mixed[:, :HEAD] / mixed[:, HEAD:]
            mixed = mixed.reshape(step, local_frames, tokens, HEAD) * gates
            mixed = mixed.reshape(step, rows, HEAD).astype(jnp.bfloat16)
            for number in range(step):
                outs[start + number][:, part] = mixed[number]


def whole_heads(queries, keys, values, slot_of, level_of, gate_table):
    devices, groups = lax.axis_size("seq"), lax.axis_size("frame")
    near = min(2, devices)
    count = devices // near
    _, local_frames, tokens, all_width = queries.shape
    rows, width = local_frames * tokens, all_width // count

    def swap(taken, away):
        return lax.ppermute(taken, "seq", [(one, one ^ away) for one in range(devices)])

    def swap_far(taken):
        return [swap(one, away * near) if away else one for away, one in enumerate(taken)]

    sent = pl.pallas_call(
        functools.partial(pack, near=near),
        out_shape=[jax.ShapeDtypeStruct((2, rows, width), queries.dtype)] * count
        + [jax.ShapeDtypeStruct((rows, width), queries.dtype)] * count,
        in_specs=[HBM] * 3,
        out_specs=[VMEM] * (2 * count),
        scratch_shapes=[pltpu.SemaphoreType.DMA((count, 3))],
        compiler_params=PARAMS,
    )(
        *(
            pltpu.with_memory_space_constraint(taken.reshape(rows, all_width), pltpu.HBM)
            for taken in (queries, keys, values)
        ),
    )
    def moved(taken, plan, shapes):
        return pl.pallas_call(
            functools.partial(move, plan=plan),
            out_shape=[jax.ShapeDtypeStruct(shape, queries.dtype) for shape in shapes],
            in_specs=[VMEM] * len(taken),
            out_specs=[VMEM] * len(shapes),
            scratch_shapes=[pltpu.SemaphoreType.DMA((len(taken),))],
            compiler_params=PARAMS,
        )(*taken)

    pair_shape, own_shape = (2, rows, width), (rows, width)
    pairs = swap_far(sent[:count])
    held = [[piece] + [swap(piece, away) for away in range(1, near)] for piece in pairs]
    half = max(1, count // 2)
    early, late = sum(held[:half], []), sum(held[half:], [])
    first, *own = moved(
        [*early, *sent[count:]],
        [(0, at) for at in range(len(early))] + [(1 + at, None) for at in range(count)],
        [(len(early), *pair_shape)] + [own_shape] * count,
    )
    second, own = moved(
        [*late, *swap_far(own)],
        [(0, at) for at in range(len(late))] + [(1, at) for at in range(count)],
        [(len(late), *pair_shape), (count, *own_shape)],
    )
    stacks = [first, second]
    held = [early, late]
    stacks = [
        lax.ppermute(taken, "frame", [(one, (one - away) % groups) for one in range(groups)])
        for away in range(1, groups)
        for taken in stacks
    ]
    held = sum(held, [])
    answers = pl.pallas_call(
        functools.partial(attend, near=near, tokens=tokens),
        out_shape=[jax.ShapeDtypeStruct((rows, width), queries.dtype)] * count,
        in_specs=[SMEM] * 2 + [VMEM] * (2 + len(held) + len(stacks)),
        out_specs=[VMEM] * count,
        compiler_params=PARAMS,
    )(slot_of, level_of, gate_table, own, *held, *stacks)
    answers = swap_far(answers)
    answer = pl.pallas_call(
        functools.partial(unpack, near=near),
        out_shape=jax.ShapeDtypeStruct((rows, all_width), queries.dtype),
        in_specs=[VMEM] * count,
        out_specs=HBM,
        scratch_shapes=[pltpu.SemaphoreType.DMA((count,))],
        compiler_params=PARAMS,
    )(*answers)
    return answer.reshape(queries.shape)


def shared_heads(queries, keys, values, slot_of, level_of, gate_table):
    devices = lax.axis_size("frame") * lax.axis_size("seq")
    _, local_frames, tokens, _ = queries.shape
    rows, blocks = local_frames * tokens, devices // H
    block_rows = rows // blocks
    exchange = functools.partial(
        lax.all_to_all, axis_name=AXES, split_axis=0, concat_axis=0, tiled=True
    )

    def by_head(taken):
        return taken.reshape(rows, H, HEAD).transpose(1, 0, 2)

    def key_pieces(taken):
        pieces = jnp.broadcast_to(by_head(taken)[:, None], (H, blocks, rows, HEAD))
        return exchange(pieces.reshape(devices, rows, HEAD)).reshape(devices * rows, HEAD)

    key_rows, value_rows = key_pieces(keys), key_pieces(values)
    query_rows = exchange(by_head(queries).reshape(devices, block_rows, HEAD))
    query_rows = query_rows.reshape(devices * block_rows, HEAD)
    device_index = lax.axis_index("frame") * lax.axis_size("seq") + lax.axis_index("seq")
    head, block = device_index // blocks, device_index % blocks

    def per_row(table):
        table = jnp.repeat(table, tokens, axis=1)[:, None]
        return jnp.broadcast_to(table, (table.shape[0], lax.axis_size("seq"), rows))

    row_slots, row_levels = per_row(slot_of), per_row(level_of)
    query_slots = lax.dynamic_slice_in_dim(row_slots, block * block_rows, block_rows, 2)
    levels = lax.dynamic_slice_in_dim(row_levels, block * block_rows, block_rows, 2).reshape(-1)
    scores = lax.dot_general(
        query_rows, key_rows, (((1,), (1,)), ((), ())), preferred_element_type=jnp.float32
    )
    visible = row_slots.reshape(1, -1) <= query_slots.reshape(-1, 1)
    scores = jnp.where(visible, scores * (1.0 / math.sqrt(HEAD)), -jnp.inf)
    weights = jnp.exp(scores - jnp.max(scores, axis=1, keepdims=True)).astype(jnp.bfloat16)
    total = jnp.sum(weights.astype(jnp.float32), axis=1, keepdims=True)
    mixed = jnp.dot(weights, value_rows, preferred_element_type=jnp.float32) / total
    gates = lax.dynamic_slice_in_dim(gate_table, head * HEAD, HEAD, 1)[levels]
    answer = exchange((mixed * gates).astype(queries.dtype).reshape(devices, block_rows, HEAD))
    return answer.reshape(H, rows, HEAD).transpose(1, 0, 2).reshape(queries.shape)


def body(queries, *others):
    devices = lax.axis_size("seq")
    if devices > H or devices & (devices - 1):
        return shared_heads(queries, *others)
    return whole_heads(queries, *others)


def solution(mesh):
    return jax.shard_map(
        body,
        mesh=mesh,
        in_specs=(
            P(("rollout", "frame"), None, "seq", None),
            P(("rollout", "frame"), None, "seq", None),
            P(("rollout", "frame"), None, "seq", None),
            P("rollout", None),
            P("rollout", None),
            P(),
        ),
        out_specs=P(("rollout", "frame"), None, "seq", None),
        check_vma=False,
    )
```

```python
import functools
import math

import jax
import jax.numpy as jnp
from jax import lax
from jax.experimental import pallas as pl
from jax.experimental.pallas import tpu as pltpu
from jax.sharding import PartitionSpec as P

H = 16
HEAD = 128
AXES = ("frame", "seq")
HBM = pl.BlockSpec(memory_space=pltpu.HBM)
VMEM = pl.BlockSpec(memory_space=pltpu.VMEM)
PARAMS = pltpu.CompilerParams(vmem_limit_bytes=32 * 1024 * 1024)


def run(copies):
    for copy in copies:
        copy.start()
    for copy in copies:
        copy.wait()


def pack(*refs):
    *operands, out_ref, sems = refs
    run(
        [
            pltpu.make_async_copy(ref.at[frame], out_ref.at[:, kind, frame], sems.at[kind, frame])
            for kind, ref in enumerate(operands)
            for frame in range(ref.shape[0])
        ]
    )


def unpack(held_ref, out_ref, sems):
    run(
        [
            pltpu.make_async_copy(held_ref.at[:, frame], out_ref.at[frame], sems.at[frame])
            for frame in range(out_ref.shape[0])
        ]
    )


def entry(ref, row, column):
    return ref[row : row + 1, column : column + 1]


def attend(slot_ref, level_ref, gate_ref, packed_ref, out_ref, *, tokens):
    groups, local_frames = slot_ref.shape
    devices, rows, width = out_ref.shape
    group_devices = devices // groups
    group_rows = group_devices * rows
    key_count = devices * rows
    index = lax.broadcasted_iota(jnp.int32, (1, key_count), 1)
    frame = index // group_rows * local_frames + index // tokens % local_frames
    key_slots = jnp.zeros((1, key_count), jnp.int32)
    for one in range(groups * local_frames):
        key_slots = jnp.where(
            frame == one, entry(slot_ref, one // local_frames, one % local_frames), key_slots
        )
    place = lax.axis_index("frame") * lax.axis_size("seq") + lax.axis_index("seq")
    gate_blocks = gate_ref[:, pl.ds(pl.multiple_of(place * width, width), width)]
    level_rows = lax.broadcasted_iota(jnp.int32, gate_blocks.shape, 0)
    ones = jnp.ones((key_count, HEAD), jnp.bfloat16)
    scale = math.log2(math.e) / math.sqrt(HEAD)
    step = max(1, min(group_devices, 128 // rows))
    for group in range(groups):
        shown, gate_rows = [], []
        for local in range(local_frames):
            visible = key_slots <= entry(slot_ref, group, local)
            shown.append(jnp.where(visible, 0.0, -jnp.inf).reshape(1, 1, 1, key_count))
            gate = jnp.where(level_rows == entry(level_ref, group, local), gate_blocks, 0.0)
            gate_rows.append(jnp.sum(gate, axis=0, keepdims=True))
        shown = jnp.concatenate(shown, axis=1)
        for column in range(0, width, HEAD):
            part = slice(column, column + HEAD)
            gates = [row[:, part].reshape(1, 1, 1, HEAD) for row in gate_rows]
            gates = jnp.concatenate(gates, axis=1)
            keys = packed_ref[:, 1, :, part].reshape(key_count, HEAD)
            values = packed_ref[:, 2, :, part].reshape(key_count, HEAD)
            values = jnp.concatenate([values, ones], axis=1)
            for start in range(group * group_devices, (group + 1) * group_devices, step):
                queries = packed_ref[start : start + step, 0, :, part].reshape(step * rows, HEAD)
                scores = lax.dot_general(
                    queries, keys, (((1,), (1,)), ((), ())), preferred_element_type=jnp.float32
                )
                scores = scores.reshape(step, local_frames, tokens, key_count) * scale + shown
                scores = scores.reshape(step * rows, key_count)
                weights = jnp.exp2(scores - jnp.max(scores, axis=1, keepdims=True))
                mixed = jnp.dot(
                    weights.astype(jnp.bfloat16), values, preferred_element_type=jnp.float32
                )
                mixed = mixed[:, :HEAD] / mixed[:, HEAD:]
                mixed = mixed.reshape(step, local_frames, tokens, HEAD) * gates
                out_ref[start : start + step, :, part] = mixed.reshape(step, rows, HEAD).astype(
                    out_ref.dtype
                )


def whole_heads(queries, keys, values, slot_of, level_of, gate_table):
    devices = lax.axis_size("frame") * lax.axis_size("seq")
    _, local_frames, tokens, all_width = queries.shape
    rows, width = local_frames * tokens, all_width // devices
    exchange = functools.partial(
        lax.all_to_all, axis_name=AXES, split_axis=0, concat_axis=0, tiled=True
    )
    def by_head(taken):
        return taken.reshape(local_frames, tokens, devices, width).transpose(0, 2, 1, 3)

    packed = pl.pallas_call(
        pack,
        out_shape=jax.ShapeDtypeStruct((devices, 3, local_frames, tokens, width), queries.dtype),
        in_specs=[HBM] * 3,
        out_specs=VMEM,
        scratch_shapes=[pltpu.SemaphoreType.DMA((3, local_frames))],
        compiler_params=PARAMS,
    )(
        *(
            pltpu.with_memory_space_constraint(by_head(taken), pltpu.HBM)
            for taken in (queries, keys, values)
        )
    )
    packed = exchange(packed)
    answer = pl.pallas_call(
        functools.partial(attend, tokens=tokens),
        out_shape=jax.ShapeDtypeStruct((devices, rows, width), queries.dtype),
        in_specs=[VMEM] * 4,
        out_specs=VMEM,
        compiler_params=PARAMS,
    )(slot_of, level_of, gate_table, packed.reshape(devices, 3, rows, width))
    answer = exchange(answer.reshape(devices, local_frames, tokens, width))
    answer = pl.pallas_call(
        unpack,
        out_shape=jax.ShapeDtypeStruct((local_frames, devices, tokens, width), queries.dtype),
        in_specs=[VMEM],
        out_specs=HBM,
        scratch_shapes=[pltpu.SemaphoreType.DMA((local_frames,))],
        compiler_params=PARAMS,
    )(answer)
    return answer.transpose(0, 2, 1, 3).reshape(queries.shape)


def shared_heads(queries, keys, values, slot_of, level_of, gate_table):
    devices = lax.axis_size("frame") * lax.axis_size("seq")
    _, local_frames, tokens, _ = queries.shape
    rows, blocks = local_frames * tokens, devices // H
    block_rows = rows // blocks
    exchange = functools.partial(
        lax.all_to_all, axis_name=AXES, split_axis=0, concat_axis=0, tiled=True
    )

    def by_head(taken):
        return taken.reshape(rows, H, HEAD).transpose(1, 0, 2)

    def key_pieces(taken):
        pieces = jnp.broadcast_to(by_head(taken)[:, None], (H, blocks, rows, HEAD))
        return exchange(pieces.reshape(devices, rows, HEAD)).reshape(devices * rows, HEAD)

    key_rows, value_rows = key_pieces(keys), key_pieces(values)
    query_rows = exchange(by_head(queries).reshape(devices, block_rows, HEAD))
    query_rows = query_rows.reshape(devices * block_rows, HEAD)
    device_index = lax.axis_index("frame") * lax.axis_size("seq") + lax.axis_index("seq")
    head, block = device_index // blocks, device_index % blocks

    def per_row(table):
        table = jnp.repeat(table, tokens, axis=1)[:, None]
        return jnp.broadcast_to(table, (table.shape[0], lax.axis_size("seq"), rows))

    row_slots, row_levels = per_row(slot_of), per_row(level_of)
    query_slots = lax.dynamic_slice_in_dim(row_slots, block * block_rows, block_rows, 2)
    levels = lax.dynamic_slice_in_dim(row_levels, block * block_rows, block_rows, 2).reshape(-1)
    scores = lax.dot_general(
        query_rows, key_rows, (((1,), (1,)), ((), ())), preferred_element_type=jnp.float32
    )
    visible = row_slots.reshape(1, -1) <= query_slots.reshape(-1, 1)
    scores = jnp.where(visible, scores * (1.0 / math.sqrt(HEAD)), -jnp.inf)
    weights = jnp.exp(scores - jnp.max(scores, axis=1, keepdims=True)).astype(jnp.bfloat16)
    total = jnp.sum(weights.astype(jnp.float32), axis=1, keepdims=True)
    mixed = jnp.dot(weights, value_rows, preferred_element_type=jnp.float32) / total
    gates = lax.dynamic_slice_in_dim(gate_table, head * HEAD, HEAD, 1)[levels]
    answer = exchange((mixed * gates).astype(queries.dtype).reshape(devices, block_rows, HEAD))
    return answer.reshape(H, rows, HEAD).transpose(1, 0, 2).reshape(queries.shape)


def body(queries, *others):
    if lax.axis_size("frame") * lax.axis_size("seq") > H:
        return shared_heads(queries, *others)
    return whole_heads(queries, *others)


def solution(mesh):
    return jax.shard_map(
        body,
        mesh=mesh,
        in_specs=(
            P(("rollout", "frame"), None, "seq", None),
            P(("rollout", "frame"), None, "seq", None),
            P(("rollout", "frame"), None, "seq", None),
            P("rollout", None),
            P("rollout", None),
            P(),
        ),
        out_specs=P(("rollout", "frame"), None, "seq", None),
        check_vma=False,
    )
```

```python
import functools
import math

import jax
import jax.numpy as jnp
from jax import lax
from jax.experimental import pallas as pl
from jax.experimental.pallas import tpu as pltpu
from jax.sharding import PartitionSpec as P

H = 16
HEAD = 128
AXES = ("frame", "seq")
SPLIT = ("frame", "far")
HBM = pl.BlockSpec(memory_space=pltpu.HBM)
VMEM = pl.BlockSpec(memory_space=pltpu.VMEM)
PARAMS = pltpu.CompilerParams(vmem_limit_bytes=32 * 1024 * 1024)


def run(copies):
    for copy in copies:
        copy.start()
    for copy in copies:
        copy.wait()


def pack(*refs):
    key_ref, value_ref, query_ref, slot_ref, level_ref, gate_ref = refs[:6]
    pair_ref, own_ref, slot_out, level_out, gate_out, sems, table_sems = refs[6:]
    width = gate_out.shape[-1]
    place = lax.axis_index("frame") * lax.axis_size("far") + lax.axis_index("far")
    columns = pl.ds(pl.multiple_of(place * width, width), width)
    cut = [
        pltpu.make_async_copy(ref.at[frame], out_ref.at[:, frame], sems.at[kind, frame])
        for kind, (ref, out_ref) in enumerate(
            ((key_ref, pair_ref.at[:, 0]), (value_ref, pair_ref.at[:, 1]), (query_ref, own_ref))
        )
        for frame in range(ref.shape[0])
    ]
    tables = [
        pltpu.make_async_copy(ref, out_ref, table_sems.at[kind])
        for kind, (ref, out_ref) in enumerate(
            ((slot_ref, slot_out), (level_ref, level_out), (gate_ref.at[:, columns], gate_out))
        )
    ]
    run(cut + tables)


def unpack(held_ref, out_ref, sems):
    run(
        [
            pltpu.make_async_copy(held_ref.at[:, frame], out_ref.at[frame], sems.at[frame])
            for frame in range(out_ref.shape[0])
        ]
    )


def entry(ref, row, column):
    return ref[row : row + 1, column : column + 1]


def attend(slot_ref, level_ref, gate_ref, query_ref, *refs, tokens):
    *pair_refs, out_ref = refs
    groups, local_frames = slot_ref.shape
    devices, rows, width = out_ref.shape
    group_rows = devices // groups * rows
    pair_keys = devices * rows
    key_count = len(pair_refs) * pair_keys
    index = lax.broadcasted_iota(jnp.int32, (1, key_count), 1)
    frame = index % pair_keys // group_rows * local_frames + index // tokens % local_frames
    key_slots = jnp.zeros((1, key_count), jnp.int32)
    for one in range(groups * local_frames):
        key_slots = jnp.where(
            frame == one, entry(slot_ref, one // local_frames, one % local_frames), key_slots
        )
    gate_blocks = gate_ref[...]
    level_rows = lax.broadcasted_iota(jnp.int32, gate_blocks.shape, 0)
    ones = jnp.ones((key_count, HEAD), jnp.bfloat16)
    scale = math.log2(math.e) / math.sqrt(HEAD)
    group_devices = devices // groups
    step = max(1, min(group_devices, 128 // rows))
    for group in range(groups):
        shown, gate_rows = [], []
        for local in range(local_frames):
            visible = key_slots <= entry(slot_ref, group, local)
            shown.append(jnp.where(visible, 0.0, -jnp.inf).reshape(1, 1, 1, key_count))
            gate = jnp.where(level_rows == entry(level_ref, group, local), gate_blocks, 0.0)
            gate_rows.append(jnp.sum(gate, axis=0, keepdims=True))
        shown = jnp.concatenate(shown, axis=1)
        for column in range(0, width, HEAD):
            part = slice(column, column + HEAD)
            gates = [row[:, part].reshape(1, 1, 1, HEAD) for row in gate_rows]
            gates = jnp.concatenate(gates, axis=1)
            keys, values = (
                jnp.concatenate([ref[:, kind, :, part].reshape(pair_keys, HEAD) for ref in pair_refs])
                for kind in range(2)
            )
            values = jnp.concatenate([values, ones], axis=1)
            for start in range(group * group_devices, (group + 1) * group_devices, step):
                queries = query_ref[start : start + step, :, part].reshape(step * rows, HEAD)
                scores = lax.dot_general(
                    queries, keys, (((1,), (1,)), ((), ())), preferred_element_type=jnp.float32
                )
                scores = scores.reshape(step, local_frames, tokens, key_count) * scale + shown
                scores = scores.reshape(step * rows, key_count)
                weights = jnp.exp2(scores - jnp.max(scores, axis=1, keepdims=True))
                mixed = jnp.dot(
                    weights.astype(jnp.bfloat16), values, preferred_element_type=jnp.float32
                )
                mixed = mixed[:, :HEAD] / mixed[:, HEAD:]
                mixed = mixed.reshape(step, local_frames, tokens, HEAD) * gates
                out_ref[start : start + step, :, part] = mixed.reshape(step, rows, HEAD).astype(
                    out_ref.dtype
                )


def whole_heads(queries, keys, values, slot_of, level_of, gate_table):
    devices, near = lax.axis_size("frame") * lax.axis_size("far"), lax.axis_size("near")
    _, local_frames, tokens, all_width = queries.shape
    rows, width = local_frames * tokens, all_width // devices
    exchange = functools.partial(
        lax.all_to_all, axis_name=SPLIT, split_axis=0, concat_axis=0, tiled=True
    )
    piece = (local_frames, tokens, width)

    def in_hbm(taken):
        return pltpu.with_memory_space_constraint(taken, pltpu.HBM)

    def by_head(taken):
        return taken.reshape(local_frames, tokens, devices, width).transpose(0, 2, 1, 3)

    pair, own, slots, levels, gates = pl.pallas_call(
        pack,
        out_shape=[
            jax.ShapeDtypeStruct((devices, 2, *piece), queries.dtype),
            jax.ShapeDtypeStruct((devices, *piece), queries.dtype),
            jax.ShapeDtypeStruct(slot_of.shape, slot_of.dtype),
            jax.ShapeDtypeStruct(level_of.shape, level_of.dtype),
            jax.ShapeDtypeStruct((gate_table.shape[0], width), gate_table.dtype),
        ],
        in_specs=[HBM] * 6,
        out_specs=[VMEM] * 5,
        scratch_shapes=[pltpu.SemaphoreType.DMA((3, local_frames)), pltpu.SemaphoreType.DMA((3,))],
        compiler_params=PARAMS,
    )(
        *(in_hbm(by_head(taken)) for taken in (keys, values, queries)),
        *(in_hbm(taken) for taken in (slot_of, level_of, gate_table)),
    )
    pair = exchange(pair).reshape(devices, 2, rows, width)
    pairs = [pair] + [
        lax.ppermute(pair, "near", [(one, (one - away) % near) for one in range(near)])
        for away in range(1, near)
    ]
    own = exchange(own).reshape(devices, rows, width)
    answer = pl.pallas_call(
        functools.partial(attend, tokens=tokens),
        out_shape=jax.ShapeDtypeStruct((devices, rows, width), queries.dtype),
        in_specs=[VMEM] * (4 + near),
        out_specs=VMEM,
        compiler_params=PARAMS,
    )(slots, levels, gates, own, *pairs)
    answer = exchange(answer.reshape(devices, *piece))
    answer = pl.pallas_call(
        unpack,
        out_shape=jax.ShapeDtypeStruct((local_frames, devices, tokens, width), queries.dtype),
        in_specs=[VMEM],
        out_specs=HBM,
        scratch_shapes=[pltpu.SemaphoreType.DMA((local_frames,))],
        compiler_params=PARAMS,
    )(answer)
    return answer.transpose(0, 2, 1, 3).reshape(queries.shape)


def shared_heads(queries, keys, values, slot_of, level_of, gate_table):
    devices = lax.axis_size("frame") * lax.axis_size("seq")
    _, local_frames, tokens, _ = queries.shape
    rows, blocks = local_frames * tokens, devices // H
    block_rows = rows // blocks
    exchange = functools.partial(
        lax.all_to_all, axis_name=AXES, split_axis=0, concat_axis=0, tiled=True
    )

    def by_head(taken):
        return taken.reshape(rows, H, HEAD).transpose(1, 0, 2)

    def key_pieces(taken):
        pieces = jnp.broadcast_to(by_head(taken)[:, None], (H, blocks, rows, HEAD))
        return exchange(pieces.reshape(devices, rows, HEAD)).reshape(devices * rows, HEAD)

    key_rows, value_rows = key_pieces(keys), key_pieces(values)
    query_rows = exchange(by_head(queries).reshape(devices, block_rows, HEAD))
    query_rows = query_rows.reshape(devices * block_rows, HEAD)
    device_index = lax.axis_index("frame") * lax.axis_size("seq") + lax.axis_index("seq")
    head, block = device_index // blocks, device_index % blocks

    def per_row(table):
        table = jnp.repeat(table, tokens, axis=1)[:, None]
        return jnp.broadcast_to(table, (table.shape[0], lax.axis_size("seq"), rows))

    row_slots, row_levels = per_row(slot_of), per_row(level_of)
    query_slots = lax.dynamic_slice_in_dim(row_slots, block * block_rows, block_rows, 2)
    levels = lax.dynamic_slice_in_dim(row_levels, block * block_rows, block_rows, 2).reshape(-1)
    scores = lax.dot_general(
        query_rows, key_rows, (((1,), (1,)), ((), ())), preferred_element_type=jnp.float32
    )
    visible = row_slots.reshape(1, -1) <= query_slots.reshape(-1, 1)
    scores = jnp.where(visible, scores * (1.0 / math.sqrt(HEAD)), -jnp.inf)
    weights = jnp.exp(scores - jnp.max(scores, axis=1, keepdims=True)).astype(jnp.bfloat16)
    total = jnp.sum(weights.astype(jnp.float32), axis=1, keepdims=True)
    mixed = jnp.dot(weights, value_rows, preferred_element_type=jnp.float32) / total
    gates = lax.dynamic_slice_in_dim(gate_table, head * HEAD, HEAD, 1)[levels]
    answer = exchange((mixed * gates).astype(queries.dtype).reshape(devices, block_rows, HEAD))
    return answer.reshape(H, rows, HEAD).transpose(1, 0, 2).reshape(queries.shape)


def solution(mesh):
    sizes = dict(mesh.shape)
    body, seq = shared_heads, "seq"
    if sizes["frame"] * sizes["seq"] <= H:
        near = 2 - sizes["seq"] % 2
        shape = (sizes["rollout"], sizes["frame"], sizes["seq"] // near, near)
        mesh = jax.sharding.Mesh(mesh.devices.reshape(shape), ("rollout", "frame", "far", "near"))
        body, seq = whole_heads, ("far", "near")
    tokens = P(("rollout", "frame"), None, seq, None)
    return jax.shard_map(
        body,
        mesh=mesh,
        in_specs=(tokens, tokens, tokens, P("rollout", None), P("rollout", None), P()),
        out_specs=tokens,
        check_vma=False,
    )
```

```python
import functools
import math

import jax
import jax.numpy as jnp
from jax import lax
from jax.experimental import pallas as pl
from jax.experimental.pallas import tpu as pltpu
from jax.sharding import PartitionSpec as P

H = 16
HEAD = 128
AXES = ("frame", "seq")
HBM = pl.BlockSpec(memory_space=pltpu.HBM)
VMEM = pl.BlockSpec(memory_space=pltpu.VMEM)
PARAMS = pltpu.CompilerParams(vmem_limit_bytes=32 * 1024 * 1024)


def run(copies):
    for copy in copies:
        copy.start()
    for copy in copies:
        copy.wait()


def pack(*refs):
    *operands, slot_ref, level_ref, gate_ref = refs[:6]
    packed_ref, slot_out, level_out, gate_out, sems, table_sems = refs[6:]
    width = gate_out.shape[-1]
    place = lax.axis_index("frame") * lax.axis_size("seq") + lax.axis_index("seq")
    columns = pl.ds(pl.multiple_of(place * width, width), width)
    tables = ((slot_ref, slot_out), (level_ref, level_out), (gate_ref.at[:, columns], gate_out))
    run(
        [
            pltpu.make_async_copy(
                ref.at[frame], packed_ref.at[:, kind, frame], sems.at[kind, frame]
            )
            for kind, ref in enumerate(operands)
            for frame in range(ref.shape[0])
        ]
        + [
            pltpu.make_async_copy(ref, out_ref, table_sems.at[kind])
            for kind, (ref, out_ref) in enumerate(tables)
        ]
    )


def unpack(held_ref, out_ref, sems):
    run(
        [
            pltpu.make_async_copy(held_ref.at[:, frame], out_ref.at[frame], sems.at[frame])
            for frame in range(out_ref.shape[0])
        ]
    )


def entry(ref, row, column):
    return ref[row : row + 1, column : column + 1]


def attend(slot_ref, level_ref, gate_ref, packed_ref, out_ref, *, tokens):
    groups, local_frames = slot_ref.shape
    devices, rows, width = out_ref.shape
    group_devices = devices // groups
    group_rows = group_devices * rows
    key_count = devices * rows
    index = lax.broadcasted_iota(jnp.int32, (1, key_count), 1)
    frame = index // group_rows * local_frames + index // tokens % local_frames
    key_slots = jnp.zeros((1, key_count), jnp.int32)
    for one in range(groups * local_frames):
        key_slots = jnp.where(
            frame == one, entry(slot_ref, one // local_frames, one % local_frames), key_slots
        )
    gate_blocks = gate_ref[...]
    level_rows = lax.broadcasted_iota(jnp.int32, gate_blocks.shape, 0)
    ones = jnp.ones((key_count, HEAD), jnp.bfloat16)
    scale = math.log2(math.e) / math.sqrt(HEAD)
    step = max(1, min(group_devices, 128 // rows))
    for group in range(groups):
        shown, gate_rows = [], []
        for local in range(local_frames):
            visible = key_slots <= entry(slot_ref, group, local)
            shown.append(jnp.where(visible, 0.0, -jnp.inf).reshape(1, 1, 1, key_count))
            gate = jnp.where(level_rows == entry(level_ref, group, local), gate_blocks, 0.0)
            gate_rows.append(jnp.sum(gate, axis=0, keepdims=True))
        shown = jnp.concatenate(shown, axis=1)
        for column in range(0, width, HEAD):
            part = slice(column, column + HEAD)
            gates = [row[:, part].reshape(1, 1, 1, HEAD) for row in gate_rows]
            gates = jnp.concatenate(gates, axis=1)
            keys = packed_ref[:, 1, :, part].reshape(key_count, HEAD)
            values = packed_ref[:, 2, :, part].reshape(key_count, HEAD)
            values = jnp.concatenate([values, ones], axis=1)
            for start in range(group * group_devices, (group + 1) * group_devices, step):
                queries = packed_ref[start : start + step, 0, :, part].reshape(step * rows, HEAD)
                scores = lax.dot_general(
                    queries, keys, (((1,), (1,)), ((), ())), preferred_element_type=jnp.float32
                )
                scores = scores.reshape(step, local_frames, tokens, key_count) * scale + shown
                scores = scores.reshape(step * rows, key_count)
                weights = jnp.exp2(scores - jnp.max(scores, axis=1, keepdims=True))
                mixed = jnp.dot(
                    weights.astype(jnp.bfloat16), values, preferred_element_type=jnp.float32
                )
                mixed = mixed[:, :HEAD] / mixed[:, HEAD:]
                mixed = mixed.reshape(step, local_frames, tokens, HEAD) * gates
                out_ref[start : start + step, :, part] = mixed.reshape(step, rows, HEAD).astype(
                    out_ref.dtype
                )


def whole_heads(queries, keys, values, slot_of, level_of, gate_table):
    devices = lax.axis_size("frame") * lax.axis_size("seq")
    _, local_frames, tokens, all_width = queries.shape
    rows, width = local_frames * tokens, all_width // devices
    piece = (local_frames, tokens, width)
    exchange = functools.partial(
        lax.all_to_all, axis_name=AXES, split_axis=0, concat_axis=0, tiled=True
    )

    def in_hbm(taken):
        return pltpu.with_memory_space_constraint(taken, pltpu.HBM)

    def by_head(taken):
        return taken.reshape(local_frames, tokens, devices, width).transpose(0, 2, 1, 3)

    packed, slots, levels, gates = pl.pallas_call(
        pack,
        out_shape=[
            jax.ShapeDtypeStruct((devices, 3, *piece), queries.dtype),
            jax.ShapeDtypeStruct(slot_of.shape, slot_of.dtype),
            jax.ShapeDtypeStruct(level_of.shape, level_of.dtype),
            jax.ShapeDtypeStruct((gate_table.shape[0], width), gate_table.dtype),
        ],
        in_specs=[HBM] * 6,
        out_specs=[VMEM] * 4,
        scratch_shapes=[pltpu.SemaphoreType.DMA((3, local_frames)), pltpu.SemaphoreType.DMA((3,))],
        compiler_params=PARAMS,
    )(
        *(in_hbm(by_head(taken)) for taken in (queries, keys, values)),
        *(in_hbm(taken) for taken in (slot_of, level_of, gate_table)),
    )
    packed = exchange(packed).reshape(devices, 3, rows, width)
    answer = pl.pallas_call(
        functools.partial(attend, tokens=tokens),
        out_shape=jax.ShapeDtypeStruct((devices, rows, width), queries.dtype),
        in_specs=[VMEM] * 4,
        out_specs=VMEM,
        compiler_params=PARAMS,
    )(slots, levels, gates, packed)
    answer = exchange(answer.reshape(devices, *piece))
    answer = pl.pallas_call(
        unpack,
        out_shape=jax.ShapeDtypeStruct((local_frames, devices, tokens, width), queries.dtype),
        in_specs=[VMEM],
        out_specs=HBM,
        scratch_shapes=[pltpu.SemaphoreType.DMA((local_frames,))],
        compiler_params=PARAMS,
    )(answer)
    return answer.transpose(0, 2, 1, 3).reshape(queries.shape)


def shared_heads(queries, keys, values, slot_of, level_of, gate_table):
    devices = lax.axis_size("frame") * lax.axis_size("seq")
    _, local_frames, tokens, _ = queries.shape
    rows, blocks = local_frames * tokens, devices // H
    block_rows = rows // blocks
    exchange = functools.partial(
        lax.all_to_all, axis_name=AXES, split_axis=0, concat_axis=0, tiled=True
    )

    def by_head(taken):
        return taken.reshape(rows, H, HEAD).transpose(1, 0, 2)

    def key_pieces(taken):
        pieces = jnp.broadcast_to(by_head(taken)[:, None], (H, blocks, rows, HEAD))
        return exchange(pieces.reshape(devices, rows, HEAD)).reshape(devices * rows, HEAD)

    key_rows, value_rows = key_pieces(keys), key_pieces(values)
    query_rows = exchange(by_head(queries).reshape(devices, block_rows, HEAD))
    query_rows = query_rows.reshape(devices * block_rows, HEAD)
    device_index = lax.axis_index("frame") * lax.axis_size("seq") + lax.axis_index("seq")
    head, block = device_index // blocks, device_index % blocks

    def per_row(table):
        table = jnp.repeat(table, tokens, axis=1)[:, None]
        return jnp.broadcast_to(table, (table.shape[0], lax.axis_size("seq"), rows))

    row_slots, row_levels = per_row(slot_of), per_row(level_of)
    query_slots = lax.dynamic_slice_in_dim(row_slots, block * block_rows, block_rows, 2)
    levels = lax.dynamic_slice_in_dim(row_levels, block * block_rows, block_rows, 2).reshape(-1)
    scores = lax.dot_general(
        query_rows, key_rows, (((1,), (1,)), ((), ())), preferred_element_type=jnp.float32
    )
    visible = row_slots.reshape(1, -1) <= query_slots.reshape(-1, 1)
    scores = jnp.where(visible, scores * (1.0 / math.sqrt(HEAD)), -jnp.inf)
    weights = jnp.exp(scores - jnp.max(scores, axis=1, keepdims=True)).astype(jnp.bfloat16)
    total = jnp.sum(weights.astype(jnp.float32), axis=1, keepdims=True)
    mixed = jnp.dot(weights, value_rows, preferred_element_type=jnp.float32) / total
    gates = lax.dynamic_slice_in_dim(gate_table, head * HEAD, HEAD, 1)[levels]
    answer = exchange((mixed * gates).astype(queries.dtype).reshape(devices, block_rows, HEAD))
    return answer.reshape(H, rows, HEAD).transpose(1, 0, 2).reshape(queries.shape)


def solution(mesh):
    tokens = P(("rollout", "frame"), None, "seq", None)
    return jax.shard_map(
        whole_heads if mesh.shape["frame"] * mesh.shape["seq"] <= H else shared_heads,
        mesh=mesh,
        in_specs=(tokens, tokens, tokens, P("rollout", None), P("rollout", None), P()),
        out_specs=tokens,
        check_vma=False,
    )
```

```python
import functools
import math

import jax
import jax.numpy as jnp
from jax import lax
from jax.experimental import pallas as pl
from jax.experimental.pallas import tpu as pltpu
from jax.sharding import PartitionSpec as P

H = 16
HEAD = 128
AXES = ("seq", "frame")
HBM = pl.BlockSpec(memory_space=pltpu.HBM)
VMEM = pl.BlockSpec(memory_space=pltpu.VMEM)
PARAMS = pltpu.CompilerParams(vmem_limit_bytes=32 * 1024 * 1024)


def run(copies):
    for copy in copies:
        copy.start()
    for copy in copies:
        copy.wait()


def pack(*refs):
    *operands, slot_ref, level_ref, gate_ref = refs[:6]
    packed_ref, slot_out, level_out, gate_out, sems, table_sems = refs[6:]
    width = gate_out.shape[-1]
    place = lax.axis_index("seq") * lax.axis_size("frame") + lax.axis_index("frame")
    columns = pl.ds(pl.multiple_of(place * width, width), width)
    tables = ((slot_ref, slot_out), (level_ref, level_out), (gate_ref.at[:, columns], gate_out))
    run(
        [
            pltpu.make_async_copy(
                ref.at[frame], packed_ref.at[:, kind, frame], sems.at[kind, frame]
            )
            for kind, ref in enumerate(operands)
            for frame in range(ref.shape[0])
        ]
        + [
            pltpu.make_async_copy(ref, out_ref, table_sems.at[kind])
            for kind, (ref, out_ref) in enumerate(tables)
        ]
    )


def unpack(held_ref, out_ref, sems):
    run(
        [
            pltpu.make_async_copy(held_ref.at[:, frame], out_ref.at[frame], sems.at[frame])
            for frame in range(out_ref.shape[0])
        ]
    )


def entry(ref, row, column):
    return ref[row : row + 1, column : column + 1]


def attend(slot_ref, level_ref, gate_ref, packed_ref, out_ref, *, tokens):
    local_frames = slot_ref.shape[1]
    places, groups, rows, width = out_ref.shape
    key_count = places * groups * rows
    index = lax.broadcasted_iota(jnp.int32, (1, key_count), 1)
    frame = index // tokens % (groups * local_frames)
    key_slots = jnp.zeros((1, key_count), jnp.int32)
    for one in range(groups * local_frames):
        key_slots = jnp.where(
            frame == one, entry(slot_ref, one // local_frames, one % local_frames), key_slots
        )
    gate_blocks = gate_ref[...]
    level_rows = lax.broadcasted_iota(jnp.int32, gate_blocks.shape, 0)
    ones = jnp.ones((key_count, HEAD), jnp.bfloat16)
    scale = math.log2(math.e) / math.sqrt(HEAD)
    step = max(1, min(places, 128 // rows))
    for group in range(groups):
        shown, gate_rows = [], []
        for local in range(local_frames):
            visible = key_slots <= entry(slot_ref, group, local)
            shown.append(jnp.where(visible, 0.0, -jnp.inf).reshape(1, 1, 1, key_count))
            gate = jnp.where(level_rows == entry(level_ref, group, local), gate_blocks, 0.0)
            gate_rows.append(jnp.sum(gate, axis=0, keepdims=True))
        shown = jnp.concatenate(shown, axis=1)
        for column in range(0, width, HEAD):
            part = slice(column, column + HEAD)
            gates = [row[:, part].reshape(1, 1, 1, HEAD) for row in gate_rows]
            gates = jnp.concatenate(gates, axis=1)
            keys = packed_ref[:, :, 1, :, part].reshape(key_count, HEAD)
            values = packed_ref[:, :, 2, :, part].reshape(key_count, HEAD)
            values = jnp.concatenate([values, ones], axis=1)
            for start in range(0, places, step):
                queries = packed_ref[start : start + step, group, 0, :, part]
                queries = queries.reshape(step * rows, HEAD)
                scores = lax.dot_general(
                    queries, keys, (((1,), (1,)), ((), ())), preferred_element_type=jnp.float32
                )
                scores = scores.reshape(step, local_frames, tokens, key_count) * scale + shown
                scores = scores.reshape(step * rows, key_count)
                weights = jnp.exp2(scores - jnp.max(scores, axis=1, keepdims=True))
                mixed = jnp.dot(
                    weights.astype(jnp.bfloat16), values, preferred_element_type=jnp.float32
                )
                mixed = mixed[:, :HEAD] / mixed[:, HEAD:]
                mixed = mixed.reshape(step, local_frames, tokens, HEAD) * gates
                out_ref[start : start + step, group, :, part] = mixed.reshape(
                    step, rows, HEAD
                ).astype(out_ref.dtype)


def whole_heads(queries, keys, values, slot_of, level_of, gate_table):
    devices = lax.axis_size("frame") * lax.axis_size("seq")
    _, local_frames, tokens, all_width = queries.shape
    rows, width = local_frames * tokens, all_width // devices
    piece = (local_frames, tokens, width)
    exchange = functools.partial(
        lax.all_to_all, axis_name=AXES, split_axis=0, concat_axis=0, tiled=True
    )

    def in_hbm(taken):
        return pltpu.with_memory_space_constraint(taken, pltpu.HBM)

    def by_head(taken):
        return taken.reshape(local_frames, tokens, devices, width).transpose(0, 2, 1, 3)

    packed, slots, levels, gates = pl.pallas_call(
        pack,
        out_shape=[
            jax.ShapeDtypeStruct((devices, 3, *piece), queries.dtype),
            jax.ShapeDtypeStruct(slot_of.shape, slot_of.dtype),
            jax.ShapeDtypeStruct(level_of.shape, level_of.dtype),
            jax.ShapeDtypeStruct((gate_table.shape[0], width), gate_table.dtype),
        ],
        in_specs=[HBM] * 6,
        out_specs=[VMEM] * 4,
        scratch_shapes=[pltpu.SemaphoreType.DMA((3, local_frames)), pltpu.SemaphoreType.DMA((3,))],
        compiler_params=PARAMS,
    )(
        *(in_hbm(by_head(taken)) for taken in (queries, keys, values)),
        *(in_hbm(taken) for taken in (slot_of, level_of, gate_table)),
    )
    places = (lax.axis_size("seq"), lax.axis_size("frame"))
    packed = exchange(packed).reshape(*places, 3, rows, width)
    answer = pl.pallas_call(
        functools.partial(attend, tokens=tokens),
        out_shape=jax.ShapeDtypeStruct((*places, rows, width), queries.dtype),
        in_specs=[VMEM] * 4,
        out_specs=VMEM,
        compiler_params=PARAMS,
    )(slots, levels, gates, packed)
    answer = exchange(answer.reshape(devices, *piece))
    answer = pl.pallas_call(
        unpack,
        out_shape=jax.ShapeDtypeStruct((local_frames, devices, tokens, width), queries.dtype),
        in_specs=[VMEM],
        out_specs=HBM,
        scratch_shapes=[pltpu.SemaphoreType.DMA((local_frames,))],
        compiler_params=PARAMS,
    )(answer)
    return answer.transpose(0, 2, 1, 3).reshape(queries.shape)


def shared_heads(queries, keys, values, slot_of, level_of, gate_table):
    devices = lax.axis_size("frame") * lax.axis_size("seq")
    _, local_frames, tokens, _ = queries.shape
    rows, blocks = local_frames * tokens, devices // H
    block_rows = rows // blocks
    exchange = functools.partial(
        lax.all_to_all, axis_name=AXES, split_axis=0, concat_axis=0, tiled=True
    )

    def by_head(taken):
        return taken.reshape(rows, H, HEAD).transpose(1, 0, 2)

    def key_pieces(taken):
        pieces = jnp.broadcast_to(by_head(taken)[:, None], (H, blocks, rows, HEAD))
        return exchange(pieces.reshape(devices, rows, HEAD)).reshape(devices * rows, HEAD)

    key_rows, value_rows = key_pieces(keys), key_pieces(values)
    query_rows = exchange(by_head(queries).reshape(devices, block_rows, HEAD))
    query_rows = query_rows.reshape(devices * block_rows, HEAD)
    device_index = lax.axis_index("frame") * lax.axis_size("seq") + lax.axis_index("seq")
    head, block = device_index // blocks, device_index % blocks

    def per_row(table):
        table = jnp.repeat(table, tokens, axis=1)[:, None]
        return jnp.broadcast_to(table, (table.shape[0], lax.axis_size("seq"), rows))

    row_slots, row_levels = per_row(slot_of), per_row(level_of)
    query_slots = lax.dynamic_slice_in_dim(row_slots, block * block_rows, block_rows, 2)
    levels = lax.dynamic_slice_in_dim(row_levels, block * block_rows, block_rows, 2).reshape(-1)
    scores = lax.dot_general(
        query_rows, key_rows, (((1,), (1,)), ((), ())), preferred_element_type=jnp.float32
    )
    visible = row_slots.reshape(1, -1) <= query_slots.reshape(-1, 1)
    scores = jnp.where(visible, scores * (1.0 / math.sqrt(HEAD)), -jnp.inf)
    weights = jnp.exp(scores - jnp.max(scores, axis=1, keepdims=True)).astype(jnp.bfloat16)
    total = jnp.sum(weights.astype(jnp.float32), axis=1, keepdims=True)
    mixed = jnp.dot(weights, value_rows, preferred_element_type=jnp.float32) / total
    gates = lax.dynamic_slice_in_dim(gate_table, head * HEAD, HEAD, 1)[levels]
    answer = exchange((mixed * gates).astype(queries.dtype).reshape(devices, block_rows, HEAD))
    return answer.reshape(H, rows, HEAD).transpose(1, 0, 2).reshape(queries.shape)


def solution(mesh):
    tokens = P(("rollout", "frame"), None, "seq", None)
    return jax.shard_map(
        whole_heads if mesh.shape["frame"] * mesh.shape["seq"] <= H else shared_heads,
        mesh=mesh,
        in_specs=(tokens, tokens, tokens, P("rollout", None), P("rollout", None), P()),
        out_specs=tokens,
        check_vma=False,
    )
```

```python
import functools
import math

import jax
import jax.numpy as jnp
from jax import lax
from jax.experimental import pallas as pl
from jax.experimental.pallas import tpu as pltpu
from jax.sharding import PartitionSpec as P

H = 16
HEAD = 128
AXES = ("frame", "seq")
HBM = pl.BlockSpec(memory_space=pltpu.HBM)
VMEM = pl.BlockSpec(memory_space=pltpu.VMEM)
PARAMS = pltpu.CompilerParams(vmem_limit_bytes=32 * 1024 * 1024)


def far_first(devices):
    return sorted(range(devices), key=lambda away: (-(2 * away // devices), away % 2, -away))


def run(copies):
    for copy in copies:
        copy.start()
    for copy in copies:
        copy.wait()


def pack(*refs):
    *operands, slot_ref, level_ref, gate_ref = refs[:6]
    *outs, slot_out, level_out, gate_out, sems, table_sems = refs[6:]
    width = gate_out.shape[-1]
    place = lax.axis_index("seq")

    def columns(place):
        return pl.ds(pl.multiple_of(place * width, width), width)

    tables = (
        (slot_ref, slot_out),
        (level_ref, level_out),
        (gate_ref.at[:, columns(place)], gate_out),
    )
    run(
        [
            pltpu.make_async_copy(
                ref.at[:, columns(place ^ away)], out_ref.at[kind], sems.at[away, kind]
            )
            for away, out_ref in zip(far_first(len(outs)), outs)
            for kind, ref in enumerate(operands)
        ]
        + [
            pltpu.make_async_copy(ref, out_ref, table_sems.at[kind])
            for kind, (ref, out_ref) in enumerate(tables)
        ]
    )


def stack(*refs):
    *pieces, out_ref, sems = refs
    run(
        [
            pltpu.make_async_copy(ref.at[pl.ds(1, 2)], out_ref.at[number], sems.at[number])
            for number, ref in enumerate(pieces)
        ]
    )


def unpack(held_ref, out_ref, sems):
    run(
        [
            pltpu.make_async_copy(held_ref.at[:, frame], out_ref.at[frame], sems.at[frame])
            for frame in range(out_ref.shape[0])
        ]
    )


def entry(ref, row, column):
    return ref[row : row + 1, column : column + 1]


def attend(slot_ref, level_ref, gate_ref, *refs, tokens):
    out_ref = refs[-1]
    devices, rows, width = out_ref.shape
    own_refs, pair_refs = refs[:devices], refs[devices:-1]
    groups, local_frames = slot_ref.shape
    group_keys = devices * rows
    key_count = groups * group_keys
    group = lax.axis_index("frame")
    index = lax.broadcasted_iota(jnp.int32, (1, key_count), 1)
    frame = (index // group_keys + group) % groups * local_frames + index // tokens % local_frames
    key_slots = jnp.zeros((1, key_count), jnp.int32)
    for one in range(groups * local_frames):
        key_slots = jnp.where(
            frame == one, entry(slot_ref, one // local_frames, one % local_frames), key_slots
        )
    gate_blocks = gate_ref[...]
    level_rows = lax.broadcasted_iota(jnp.int32, gate_blocks.shape, 0)
    shown, gate_rows = [], []
    for local in range(local_frames):
        slot, level = entry(slot_ref, 0, local), entry(level_ref, 0, local)
        for other in range(1, groups):
            slot = jnp.where(group == other, entry(slot_ref, other, local), slot)
            level = jnp.where(group == other, entry(level_ref, other, local), level)
        shown.append(jnp.where(key_slots <= slot, 0.0, -jnp.inf).reshape(1, 1, 1, key_count))
        gate = jnp.where(level_rows == level, gate_blocks, 0.0)
        gate_rows.append(jnp.sum(gate, axis=0, keepdims=True))
    shown = jnp.concatenate(shown, axis=1)
    ones = jnp.ones((key_count, HEAD), jnp.bfloat16)
    scale = math.log2(math.e) / math.sqrt(HEAD)
    step = max(1, min(devices, 128 // rows))
    for column in range(0, width, HEAD):
        part = slice(column, column + HEAD)
        gates = [row[:, part].reshape(1, 1, 1, HEAD) for row in gate_rows]
        gates = jnp.concatenate(gates, axis=1)
        keys, values = (
            jnp.concatenate(
                [ref[1 + kind, :, part] for ref in own_refs]
                + [ref[:, kind, :, part].reshape(ref.shape[0] * rows, HEAD) for ref in pair_refs]
            )
            for kind in range(2)
        )
        values = jnp.concatenate([values, ones], axis=1)
        for start in range(0, devices, step):
            queries = jnp.concatenate([ref[0, :, part] for ref in own_refs[start : start + step]])
            scores = lax.dot_general(
                queries, keys, (((1,), (1,)), ((), ())), preferred_element_type=jnp.float32
            )
            scores = scores.reshape(step, local_frames, tokens, key_count) * scale + shown
            scores = scores.reshape(step * rows, key_count)
            weights = jnp.exp2(scores - jnp.max(scores, axis=1, keepdims=True))
            mixed = jnp.dot(
                weights.astype(jnp.bfloat16), values, preferred_element_type=jnp.float32
            )
            mixed = mixed[:, :HEAD] / mixed[:, HEAD:]
            mixed = mixed.reshape(step, local_frames, tokens, HEAD) * gates
            mixed = mixed.reshape(step, rows, HEAD).astype(out_ref.dtype)
            for number, away in enumerate(far_first(devices)[start : start + step]):
                out_ref[lax.axis_index("seq") ^ away, :, part] = mixed[number]


def whole_heads(queries, keys, values, slot_of, level_of, gate_table):
    devices, groups = lax.axis_size("seq"), lax.axis_size("frame")
    _, local_frames, tokens, all_width = queries.shape
    rows, width = local_frames * tokens, all_width // devices
    half = max(1, devices // 2)

    def in_hbm(taken):
        return pltpu.with_memory_space_constraint(taken, pltpu.HBM)

    *pieces, slots, levels, gates = pl.pallas_call(
        pack,
        out_shape=[jax.ShapeDtypeStruct((3, rows, width), queries.dtype)] * devices
        + [
            jax.ShapeDtypeStruct(slot_of.shape, slot_of.dtype),
            jax.ShapeDtypeStruct(level_of.shape, level_of.dtype),
            jax.ShapeDtypeStruct((gate_table.shape[0], width), gate_table.dtype),
        ],
        in_specs=[HBM] * 6,
        out_specs=[VMEM] * (devices + 3),
        scratch_shapes=[pltpu.SemaphoreType.DMA((devices, 3)), pltpu.SemaphoreType.DMA((3,))],
        compiler_params=PARAMS,
    )(
        *(in_hbm(taken.reshape(rows, all_width)) for taken in (queries, keys, values)),
        *(in_hbm(taken) for taken in (slot_of, level_of, gate_table)),
    )
    pieces = [
        lax.ppermute(piece, "seq", [(one, one ^ away) for one in range(devices)])
        if away
        else piece
        for away, piece in zip(far_first(devices), pieces)
    ]

    def stacked(taken):
        return pl.pallas_call(
            stack,
            out_shape=jax.ShapeDtypeStruct((len(taken), 2, rows, width), queries.dtype),
            in_specs=[VMEM] * len(taken),
            out_specs=VMEM,
            scratch_shapes=[pltpu.SemaphoreType.DMA((len(taken),))],
            compiler_params=PARAMS,
        )(*taken)

    stacks = [stacked(taken) for taken in (pieces[half:], pieces[:half]) if taken]
    stacks = [
        lax.ppermute(taken, "frame", [(one, (one - away) % groups) for one in range(groups)])
        for away in range(1, groups)
        for taken in stacks
    ]
    answer = pl.pallas_call(
        functools.partial(attend, tokens=tokens),
        out_shape=jax.ShapeDtypeStruct((devices, rows, width), queries.dtype),
        in_specs=[VMEM] * (3 + devices + len(stacks)),
        out_specs=VMEM,
        compiler_params=PARAMS,
    )(slots, levels, gates, *pieces, *stacks)
    answer = answer.reshape(devices, local_frames, tokens, width)
    answer = lax.all_to_all(answer, "seq", split_axis=0, concat_axis=0, tiled=True)
    answer = pl.pallas_call(
        unpack,
        out_shape=jax.ShapeDtypeStruct((local_frames, devices, tokens, width), queries.dtype),
        in_specs=[VMEM],
        out_specs=HBM,
        scratch_shapes=[pltpu.SemaphoreType.DMA((local_frames,))],
        compiler_params=PARAMS,
    )(answer)
    return answer.transpose(0, 2, 1, 3).reshape(queries.shape)


def shared_heads(queries, keys, values, slot_of, level_of, gate_table):
    devices = lax.axis_size("frame") * lax.axis_size("seq")
    _, local_frames, tokens, _ = queries.shape
    rows, blocks = local_frames * tokens, devices // H
    block_rows = rows // blocks
    exchange = functools.partial(
        lax.all_to_all, axis_name=AXES, split_axis=0, concat_axis=0, tiled=True
    )

    def by_head(taken):
        return taken.reshape(rows, H, HEAD).transpose(1, 0, 2)

    def key_pieces(taken):
        pieces = jnp.broadcast_to(by_head(taken)[:, None], (H, blocks, rows, HEAD))
        return exchange(pieces.reshape(devices, rows, HEAD)).reshape(devices * rows, HEAD)

    key_rows, value_rows = key_pieces(keys), key_pieces(values)
    query_rows = exchange(by_head(queries).reshape(devices, block_rows, HEAD))
    query_rows = query_rows.reshape(devices * block_rows, HEAD)
    device_index = lax.axis_index("frame") * lax.axis_size("seq") + lax.axis_index("seq")
    head, block = device_index // blocks, device_index % blocks

    def per_row(table):
        table = jnp.repeat(table, tokens, axis=1)[:, None]
        return jnp.broadcast_to(table, (table.shape[0], lax.axis_size("seq"), rows))

    row_slots, row_levels = per_row(slot_of), per_row(level_of)
    query_slots = lax.dynamic_slice_in_dim(row_slots, block * block_rows, block_rows, 2)
    levels = lax.dynamic_slice_in_dim(row_levels, block * block_rows, block_rows, 2).reshape(-1)
    scores = lax.dot_general(
        query_rows, key_rows, (((1,), (1,)), ((), ())), preferred_element_type=jnp.float32
    )
    visible = row_slots.reshape(1, -1) <= query_slots.reshape(-1, 1)
    scores = jnp.where(visible, scores * (1.0 / math.sqrt(HEAD)), -jnp.inf)
    weights = jnp.exp(scores - jnp.max(scores, axis=1, keepdims=True)).astype(jnp.bfloat16)
    total = jnp.sum(weights.astype(jnp.float32), axis=1, keepdims=True)
    mixed = jnp.dot(weights, value_rows, preferred_element_type=jnp.float32) / total
    gates = lax.dynamic_slice_in_dim(gate_table, head * HEAD, HEAD, 1)[levels]
    answer = exchange((mixed * gates).astype(queries.dtype).reshape(devices, block_rows, HEAD))
    return answer.reshape(H, rows, HEAD).transpose(1, 0, 2).reshape(queries.shape)


def solution(mesh):
    seq = mesh.shape["seq"]
    tokens = P(("rollout", "frame"), None, "seq", None)
    return jax.shard_map(
        whole_heads if seq <= H and seq & (seq - 1) == 0 else shared_heads,
        mesh=mesh,
        in_specs=(tokens, tokens, tokens, P("rollout", None), P("rollout", None), P()),
        out_specs=tokens,
        check_vma=False,
    )
```

```python
import functools
import math

import jax
import jax.numpy as jnp
from jax import lax
from jax.experimental import pallas as pl
from jax.experimental.pallas import tpu as pltpu
from jax.sharding import PartitionSpec as P

H = 16
HEAD = 128
AXES = ("frame", "seq")
HBM = pl.BlockSpec(memory_space=pltpu.HBM)
VMEM = pl.BlockSpec(memory_space=pltpu.VMEM)
PARAMS = pltpu.CompilerParams(vmem_limit_bytes=32 * 1024 * 1024)


def send_order(devices):
    own = sorted(range(0, devices, 2), reverse=True)
    return own + sorted(range(1, devices, 2), key=lambda away: (2 * away // devices, -away))


def run(copies):
    for copy in copies:
        copy.start()
    for copy in copies:
        copy.wait()


def pack(*refs):
    *operands, slot_ref, level_ref, gate_ref = refs[:6]
    *outs, slot_out, level_out, gate_out, sems, table_sems = refs[6:]
    width = gate_out.shape[-1]
    place = lax.axis_index("seq")

    def columns(place):
        return pl.ds(pl.multiple_of(place * width, width), width)

    tables = (
        (slot_ref, slot_out),
        (level_ref, level_out),
        (gate_ref.at[:, columns(place)], gate_out),
    )
    run(
        [
            pltpu.make_async_copy(
                ref.at[:, columns(place ^ away)], out_ref.at[kind], sems.at[away, kind]
            )
            for away, out_ref in zip(send_order(len(outs)), outs)
            for kind, ref in enumerate(operands)
        ]
        + [
            pltpu.make_async_copy(ref, out_ref, table_sems.at[kind])
            for kind, (ref, out_ref) in enumerate(tables)
        ]
    )


def stack(*refs):
    *pieces, out_ref, sems = refs
    run(
        [
            pltpu.make_async_copy(ref.at[pl.ds(1, 2)], out_ref.at[number], sems.at[number])
            for number, ref in enumerate(pieces)
        ]
    )


def unpack(held_ref, out_ref, sems):
    run(
        [
            pltpu.make_async_copy(held_ref.at[:, frame], out_ref.at[frame], sems.at[frame])
            for frame in range(out_ref.shape[0])
        ]
    )


def entry(ref, row, column):
    return ref[row : row + 1, column : column + 1]


def attend(slot_ref, level_ref, gate_ref, *refs, tokens):
    out_ref = refs[-1]
    devices, rows, width = out_ref.shape
    own_refs, pair_refs = refs[:devices], refs[devices:-1]
    groups, local_frames = slot_ref.shape
    group_keys = devices * rows
    key_count = groups * group_keys
    group = lax.axis_index("frame")
    index = lax.broadcasted_iota(jnp.int32, (1, key_count), 1)
    frame = (index // group_keys + group) % groups * local_frames + index // tokens % local_frames
    key_slots = jnp.zeros((1, key_count), jnp.int32)
    for one in range(groups * local_frames):
        key_slots = jnp.where(
            frame == one, entry(slot_ref, one // local_frames, one % local_frames), key_slots
        )
    gate_blocks = gate_ref[...]
    level_rows = lax.broadcasted_iota(jnp.int32, gate_blocks.shape, 0)
    shown, gate_rows = [], []
    for local in range(local_frames):
        slot, level = entry(slot_ref, 0, local), entry(level_ref, 0, local)
        for other in range(1, groups):
            slot = jnp.where(group == other, entry(slot_ref, other, local), slot)
            level = jnp.where(group == other, entry(level_ref, other, local), level)
        shown.append(jnp.where(key_slots <= slot, 0.0, -jnp.inf).reshape(1, 1, 1, key_count))
        gate = jnp.where(level_rows == level, gate_blocks, 0.0)
        gate_rows.append(jnp.sum(gate, axis=0, keepdims=True))
    shown = jnp.concatenate(shown, axis=1)
    ones = jnp.ones((key_count, HEAD), jnp.bfloat16)
    scale = math.log2(math.e) / math.sqrt(HEAD)
    step = max(1, min(devices, 128 // rows))
    for column in range(0, width, HEAD):
        part = slice(column, column + HEAD)
        gates = [row[:, part].reshape(1, 1, 1, HEAD) for row in gate_rows]
        gates = jnp.concatenate(gates, axis=1)
        keys, values = (
            jnp.concatenate(
                [ref[1 + kind, :, part] for ref in own_refs]
                + [ref[:, kind, :, part].reshape(ref.shape[0] * rows, HEAD) for ref in pair_refs]
            )
            for kind in range(2)
        )
        values = jnp.concatenate([values, ones], axis=1)
        for start in range(0, devices, step):
            queries = jnp.concatenate([ref[0, :, part] for ref in own_refs[start : start + step]])
            scores = lax.dot_general(
                queries, keys, (((1,), (1,)), ((), ())), preferred_element_type=jnp.float32
            )
            scores = scores.reshape(step, local_frames, tokens, key_count) * scale + shown
            scores = scores.reshape(step * rows, key_count)
            weights = jnp.exp2(scores - jnp.max(scores, axis=1, keepdims=True))
            mixed = jnp.dot(
                weights.astype(jnp.bfloat16), values, preferred_element_type=jnp.float32
            )
            mixed = mixed[:, :HEAD] / mixed[:, HEAD:]
            mixed = mixed.reshape(step, local_frames, tokens, HEAD) * gates
            mixed = mixed.reshape(step, rows, HEAD).astype(out_ref.dtype)
            for number, away in enumerate(send_order(devices)[start : start + step]):
                out_ref[lax.axis_index("seq") ^ away, :, part] = mixed[number]


def whole_heads(queries, keys, values, slot_of, level_of, gate_table):
    devices, groups = lax.axis_size("seq"), lax.axis_size("frame")
    _, local_frames, tokens, all_width = queries.shape
    rows, width = local_frames * tokens, all_width // devices
    half = max(1, devices // 2)

    def in_hbm(taken):
        return pltpu.with_memory_space_constraint(taken, pltpu.HBM)

    *pieces, slots, levels, gates = pl.pallas_call(
        pack,
        out_shape=[jax.ShapeDtypeStruct((3, rows, width), queries.dtype)] * devices
        + [
            jax.ShapeDtypeStruct(slot_of.shape, slot_of.dtype),
            jax.ShapeDtypeStruct(level_of.shape, level_of.dtype),
            jax.ShapeDtypeStruct((gate_table.shape[0], width), gate_table.dtype),
        ],
        in_specs=[HBM] * 6,
        out_specs=[VMEM] * (devices + 3),
        scratch_shapes=[pltpu.SemaphoreType.DMA((devices, 3)), pltpu.SemaphoreType.DMA((3,))],
        compiler_params=PARAMS,
    )(
        *(in_hbm(taken.reshape(rows, all_width)) for taken in (queries, keys, values)),
        *(in_hbm(taken) for taken in (slot_of, level_of, gate_table)),
    )
    pieces = [
        lax.ppermute(piece, "seq", [(one, one ^ away) for one in range(devices)])
        if away
        else piece
        for away, piece in zip(send_order(devices), pieces)
    ]

    def stacked(taken):
        return pl.pallas_call(
            stack,
            out_shape=jax.ShapeDtypeStruct((len(taken), 2, rows, width), queries.dtype),
            in_specs=[VMEM] * len(taken),
            out_specs=VMEM,
            scratch_shapes=[pltpu.SemaphoreType.DMA((len(taken),))],
            compiler_params=PARAMS,
        )(*taken)

    stacks = [stacked(taken) for taken in (pieces[:half], pieces[half:]) if taken]
    stacks = [
        lax.ppermute(taken, "frame", [(one, (one - away) % groups) for one in range(groups)])
        for away in range(1, groups)
        for taken in stacks
    ]
    answer = pl.pallas_call(
        functools.partial(attend, tokens=tokens),
        out_shape=jax.ShapeDtypeStruct((devices, rows, width), queries.dtype),
        in_specs=[VMEM] * (3 + devices + len(stacks)),
        out_specs=VMEM,
        compiler_params=PARAMS,
    )(slots, levels, gates, *pieces, *stacks)
    answer = answer.reshape(devices, local_frames, tokens, width)
    answer = lax.all_to_all(answer, "seq", split_axis=0, concat_axis=0, tiled=True)
    answer = pl.pallas_call(
        unpack,
        out_shape=jax.ShapeDtypeStruct((local_frames, devices, tokens, width), queries.dtype),
        in_specs=[VMEM],
        out_specs=HBM,
        scratch_shapes=[pltpu.SemaphoreType.DMA((local_frames,))],
        compiler_params=PARAMS,
    )(answer)
    return answer.transpose(0, 2, 1, 3).reshape(queries.shape)


def shared_heads(queries, keys, values, slot_of, level_of, gate_table):
    devices = lax.axis_size("frame") * lax.axis_size("seq")
    _, local_frames, tokens, _ = queries.shape
    rows, blocks = local_frames * tokens, devices // H
    block_rows = rows // blocks
    exchange = functools.partial(
        lax.all_to_all, axis_name=AXES, split_axis=0, concat_axis=0, tiled=True
    )

    def by_head(taken):
        return taken.reshape(rows, H, HEAD).transpose(1, 0, 2)

    def key_pieces(taken):
        pieces = jnp.broadcast_to(by_head(taken)[:, None], (H, blocks, rows, HEAD))
        return exchange(pieces.reshape(devices, rows, HEAD)).reshape(devices * rows, HEAD)

    key_rows, value_rows = key_pieces(keys), key_pieces(values)
    query_rows = exchange(by_head(queries).reshape(devices, block_rows, HEAD))
    query_rows = query_rows.reshape(devices * block_rows, HEAD)
    device_index = lax.axis_index("frame") * lax.axis_size("seq") + lax.axis_index("seq")
    head, block = device_index // blocks, device_index % blocks

    def per_row(table):
        table = jnp.repeat(table, tokens, axis=1)[:, None]
        return jnp.broadcast_to(table, (table.shape[0], lax.axis_size("seq"), rows))

    row_slots, row_levels = per_row(slot_of), per_row(level_of)
    query_slots = lax.dynamic_slice_in_dim(row_slots, block * block_rows, block_rows, 2)
    levels = lax.dynamic_slice_in_dim(row_levels, block * block_rows, block_rows, 2).reshape(-1)
    scores = lax.dot_general(
        query_rows, key_rows, (((1,), (1,)), ((), ())), preferred_element_type=jnp.float32
    )
    visible = row_slots.reshape(1, -1) <= query_slots.reshape(-1, 1)
    scores = jnp.where(visible, scores * (1.0 / math.sqrt(HEAD)), -jnp.inf)
    weights = jnp.exp(scores - jnp.max(scores, axis=1, keepdims=True)).astype(jnp.bfloat16)
    total = jnp.sum(weights.astype(jnp.float32), axis=1, keepdims=True)
    mixed = jnp.dot(weights, value_rows, preferred_element_type=jnp.float32) / total
    gates = lax.dynamic_slice_in_dim(gate_table, head * HEAD, HEAD, 1)[levels]
    answer = exchange((mixed * gates).astype(queries.dtype).reshape(devices, block_rows, HEAD))
    return answer.reshape(H, rows, HEAD).transpose(1, 0, 2).reshape(queries.shape)


def solution(mesh):
    seq = mesh.shape["seq"]
    tokens = P(("rollout", "frame"), None, "seq", None)
    return jax.shard_map(
        whole_heads if seq <= H and seq & (seq - 1) == 0 else shared_heads,
        mesh=mesh,
        in_specs=(tokens, tokens, tokens, P("rollout", None), P("rollout", None), P()),
        out_specs=tokens,
        check_vma=False,
    )
```

```python
import functools
import math

import jax
import jax.numpy as jnp
from jax import lax
from jax.experimental import pallas as pl
from jax.experimental.pallas import tpu as pltpu
from jax.sharding import PartitionSpec as P

H = 16
HEAD = 128
AXES = ("frame", "seq")
HBM = pl.BlockSpec(memory_space=pltpu.HBM)
VMEM = pl.BlockSpec(memory_space=pltpu.VMEM)
PARAMS = pltpu.CompilerParams(vmem_limit_bytes=32 * 1024 * 1024)


def send_order(devices):
    return sorted(
        range(devices),
        key=lambda away: (away != 2, -(2 * away // devices), away % 2, -away),
    )


def run(copies):
    for copy in copies:
        copy.start()
    for copy in copies:
        copy.wait()


def pack(*refs):
    *operands, slot_ref, level_ref, gate_ref = refs[:6]
    *outs, slot_out, level_out, gate_out, sems, table_sems = refs[6:]
    width = gate_out.shape[-1]
    place = lax.axis_index("seq")

    def columns(place):
        return pl.ds(pl.multiple_of(place * width, width), width)

    tables = (
        (slot_ref, slot_out),
        (level_ref, level_out),
        (gate_ref.at[:, columns(place)], gate_out),
    )
    run(
        [
            pltpu.make_async_copy(
                ref.at[:, columns(place ^ away)], out_ref.at[kind], sems.at[away, kind]
            )
            for away, out_ref in zip(send_order(len(outs)), outs)
            for kind, ref in enumerate(operands)
        ]
        + [
            pltpu.make_async_copy(ref, out_ref, table_sems.at[kind])
            for kind, (ref, out_ref) in enumerate(tables)
        ]
    )


def stack(*refs):
    *pieces, out_ref, sems = refs
    run(
        [
            pltpu.make_async_copy(ref.at[pl.ds(1, 2)], out_ref.at[number], sems.at[number])
            for number, ref in enumerate(pieces)
        ]
    )


def unpack(held_ref, out_ref, sems):
    run(
        [
            pltpu.make_async_copy(held_ref.at[:, frame], out_ref.at[frame], sems.at[frame])
            for frame in range(out_ref.shape[0])
        ]
    )


def entry(ref, row, column):
    return ref[row : row + 1, column : column + 1]


def attend(slot_ref, level_ref, gate_ref, *refs, tokens):
    out_ref = refs[-1]
    devices, rows, width = out_ref.shape
    own_refs, pair_refs = refs[:devices], refs[devices:-1]
    groups, local_frames = slot_ref.shape
    group_keys = devices * rows
    key_count = groups * group_keys
    group = lax.axis_index("frame")
    index = lax.broadcasted_iota(jnp.int32, (1, key_count), 1)
    frame = (index // group_keys + group) % groups * local_frames + index // tokens % local_frames
    key_slots = jnp.zeros((1, key_count), jnp.int32)
    for one in range(groups * local_frames):
        key_slots = jnp.where(
            frame == one, entry(slot_ref, one // local_frames, one % local_frames), key_slots
        )
    gate_blocks = gate_ref[...]
    level_rows = lax.broadcasted_iota(jnp.int32, gate_blocks.shape, 0)
    shown, gate_rows = [], []
    for local in range(local_frames):
        slot, level = entry(slot_ref, 0, local), entry(level_ref, 0, local)
        for other in range(1, groups):
            slot = jnp.where(group == other, entry(slot_ref, other, local), slot)
            level = jnp.where(group == other, entry(level_ref, other, local), level)
        shown.append(jnp.where(key_slots <= slot, 0.0, -jnp.inf).reshape(1, 1, 1, key_count))
        gate = jnp.where(level_rows == level, gate_blocks, 0.0)
        gate_rows.append(jnp.sum(gate, axis=0, keepdims=True))
    shown = jnp.concatenate(shown, axis=1)
    ones = jnp.ones((key_count, HEAD), jnp.bfloat16)
    scale = math.log2(math.e) / math.sqrt(HEAD)
    step = max(1, min(devices, 128 // rows))
    for column in range(0, width, HEAD):
        part = slice(column, column + HEAD)
        gates = [row[:, part].reshape(1, 1, 1, HEAD) for row in gate_rows]
        gates = jnp.concatenate(gates, axis=1)
        keys, values = (
            jnp.concatenate(
                [ref[1 + kind, :, part] for ref in own_refs]
                + [ref[:, kind, :, part].reshape(ref.shape[0] * rows, HEAD) for ref in pair_refs]
            )
            for kind in range(2)
        )
        values = jnp.concatenate([values, ones], axis=1)
        for start in range(0, devices, step):
            queries = jnp.concatenate([ref[0, :, part] for ref in own_refs[start : start + step]])
            scores = lax.dot_general(
                queries, keys, (((1,), (1,)), ((), ())), preferred_element_type=jnp.float32
            )
            scores = scores.reshape(step, local_frames, tokens, key_count) * scale + shown
            scores = scores.reshape(step * rows, key_count)
            weights = jnp.exp2(scores - jnp.max(scores, axis=1, keepdims=True))
            mixed = jnp.dot(
                weights.astype(jnp.bfloat16), values, preferred_element_type=jnp.float32
            )
            mixed = mixed[:, :HEAD] / mixed[:, HEAD:]
            mixed = mixed.reshape(step, local_frames, tokens, HEAD) * gates
            mixed = mixed.reshape(step, rows, HEAD).astype(out_ref.dtype)
            for number, away in enumerate(send_order(devices)[start : start + step]):
                out_ref[lax.axis_index("seq") ^ away, :, part] = mixed[number]


def whole_heads(queries, keys, values, slot_of, level_of, gate_table):
    devices, groups = lax.axis_size("seq"), lax.axis_size("frame")
    _, local_frames, tokens, all_width = queries.shape
    rows, width = local_frames * tokens, all_width // devices

    def in_hbm(taken):
        return pltpu.with_memory_space_constraint(taken, pltpu.HBM)

    *pieces, slots, levels, gates = pl.pallas_call(
        pack,
        out_shape=[jax.ShapeDtypeStruct((3, rows, width), queries.dtype)] * devices
        + [
            jax.ShapeDtypeStruct(slot_of.shape, slot_of.dtype),
            jax.ShapeDtypeStruct(level_of.shape, level_of.dtype),
            jax.ShapeDtypeStruct((gate_table.shape[0], width), gate_table.dtype),
        ],
        in_specs=[HBM] * 6,
        out_specs=[VMEM] * (devices + 3),
        scratch_shapes=[pltpu.SemaphoreType.DMA((devices, 3)), pltpu.SemaphoreType.DMA((3,))],
        compiler_params=PARAMS,
    )(
        *(in_hbm(taken.reshape(rows, all_width)) for taken in (queries, keys, values)),
        *(in_hbm(taken) for taken in (slot_of, level_of, gate_table)),
    )
    pieces = [
        lax.ppermute(piece, "seq", [(one, one ^ away) for one in range(devices)])
        if away
        else piece
        for away, piece in zip(send_order(devices), pieces)
    ]

    stacked = pl.pallas_call(
        stack,
        out_shape=jax.ShapeDtypeStruct((devices, 2, rows, width), queries.dtype),
        in_specs=[VMEM] * devices,
        out_specs=VMEM,
        scratch_shapes=[pltpu.SemaphoreType.DMA((devices,))],
        compiler_params=PARAMS,
    )(*pieces)
    stacks = [
        lax.ppermute(stacked, "frame", [(one, (one - away) % groups) for one in range(groups)])
        for away in range(1, groups)
    ]
    answer = pl.pallas_call(
        functools.partial(attend, tokens=tokens),
        out_shape=jax.ShapeDtypeStruct((devices, rows, width), queries.dtype),
        in_specs=[VMEM] * (3 + devices + len(stacks)),
        out_specs=VMEM,
        compiler_params=PARAMS,
    )(slots, levels, gates, *pieces, *stacks)
    answer = answer.reshape(devices, local_frames, tokens, width)
    answer = lax.all_to_all(answer, "seq", split_axis=0, concat_axis=0, tiled=True)
    answer = pl.pallas_call(
        unpack,
        out_shape=jax.ShapeDtypeStruct((local_frames, devices, tokens, width), queries.dtype),
        in_specs=[VMEM],
        out_specs=HBM,
        scratch_shapes=[pltpu.SemaphoreType.DMA((local_frames,))],
        compiler_params=PARAMS,
    )(answer)
    return answer.transpose(0, 2, 1, 3).reshape(queries.shape)


def shared_heads(queries, keys, values, slot_of, level_of, gate_table):
    devices = lax.axis_size("frame") * lax.axis_size("seq")
    _, local_frames, tokens, _ = queries.shape
    rows, blocks = local_frames * tokens, devices // H
    block_rows = rows // blocks
    exchange = functools.partial(
        lax.all_to_all, axis_name=AXES, split_axis=0, concat_axis=0, tiled=True
    )

    def by_head(taken):
        return taken.reshape(rows, H, HEAD).transpose(1, 0, 2)

    def key_pieces(taken):
        pieces = jnp.broadcast_to(by_head(taken)[:, None], (H, blocks, rows, HEAD))
        return exchange(pieces.reshape(devices, rows, HEAD)).reshape(devices * rows, HEAD)

    key_rows, value_rows = key_pieces(keys), key_pieces(values)
    query_rows = exchange(by_head(queries).reshape(devices, block_rows, HEAD))
    query_rows = query_rows.reshape(devices * block_rows, HEAD)
    device_index = lax.axis_index("frame") * lax.axis_size("seq") + lax.axis_index("seq")
    head, block = device_index // blocks, device_index % blocks

    def per_row(table):
        table = jnp.repeat(table, tokens, axis=1)[:, None]
        return jnp.broadcast_to(table, (table.shape[0], lax.axis_size("seq"), rows))

    row_slots, row_levels = per_row(slot_of), per_row(level_of)
    query_slots = lax.dynamic_slice_in_dim(row_slots, block * block_rows, block_rows, 2)
    levels = lax.dynamic_slice_in_dim(row_levels, block * block_rows, block_rows, 2).reshape(-1)
    scores = lax.dot_general(
        query_rows, key_rows, (((1,), (1,)), ((), ())), preferred_element_type=jnp.float32
    )
    visible = row_slots.reshape(1, -1) <= query_slots.reshape(-1, 1)
    scores = jnp.where(visible, scores * (1.0 / math.sqrt(HEAD)), -jnp.inf)
    weights = jnp.exp(scores - jnp.max(scores, axis=1, keepdims=True)).astype(jnp.bfloat16)
    total = jnp.sum(weights.astype(jnp.float32), axis=1, keepdims=True)
    mixed = jnp.dot(weights, value_rows, preferred_element_type=jnp.float32) / total
    gates = lax.dynamic_slice_in_dim(gate_table, head * HEAD, HEAD, 1)[levels]
    answer = exchange((mixed * gates).astype(queries.dtype).reshape(devices, block_rows, HEAD))
    return answer.reshape(H, rows, HEAD).transpose(1, 0, 2).reshape(queries.shape)


def solution(mesh):
    seq = mesh.shape["seq"]
    tokens = P(("rollout", "frame"), None, "seq", None)
    return jax.shard_map(
        whole_heads if seq <= H and seq & (seq - 1) == 0 else shared_heads,
        mesh=mesh,
        in_specs=(tokens, tokens, tokens, P("rollout", None), P("rollout", None), P()),
        out_specs=tokens,
        check_vma=False,
    )
```

```python
import functools
import math

import jax
import jax.numpy as jnp
from jax import lax
from jax.experimental import pallas as pl
from jax.experimental.pallas import tpu as pltpu
from jax.sharding import PartitionSpec as P

H = 16
HEAD = 128
AXES = ("frame", "seq")
HBM = pl.BlockSpec(memory_space=pltpu.HBM)
VMEM = pl.BlockSpec(memory_space=pltpu.VMEM)
PARAMS = pltpu.CompilerParams(vmem_limit_bytes=32 * 1024 * 1024)


def send_order(devices):
    half = devices // 2
    far = [*range(half + 1, devices), half][:half]
    order = far[:1]
    for pair in zip(far[1:], range(half - 1, 0, -1)):
        order += pair
    return order + [0]


def run(copies):
    for copy in copies:
        copy.start()
    for copy in copies:
        copy.wait()


def pack(*refs):
    *operands, slot_ref, level_ref, gate_ref = refs[:6]
    *outs, slot_out, level_out, gate_out, sems, table_sems = refs[6:]
    width = gate_out.shape[-1]
    place = lax.axis_index("seq")

    def columns(place):
        return pl.ds(pl.multiple_of(place * width, width), width)

    tables = (
        (slot_ref, slot_out),
        (level_ref, level_out),
        (gate_ref.at[:, columns(place)], gate_out),
    )
    run(
        [
            pltpu.make_async_copy(
                ref.at[:, columns(place ^ away)], out_ref.at[kind], sems.at[away, kind]
            )
            for away, out_ref in zip(send_order(len(outs)), outs)
            for kind, ref in enumerate(operands)
        ]
        + [
            pltpu.make_async_copy(ref, out_ref, table_sems.at[kind])
            for kind, (ref, out_ref) in enumerate(tables)
        ]
    )


def stack(*refs):
    *pieces, out_ref, sems = refs
    run(
        [
            pltpu.make_async_copy(ref.at[pl.ds(1, 2)], out_ref.at[number], sems.at[number])
            for number, ref in enumerate(pieces)
        ]
    )


def unpack(held_ref, out_ref, sems):
    run(
        [
            pltpu.make_async_copy(held_ref.at[:, frame], out_ref.at[frame], sems.at[frame])
            for frame in range(out_ref.shape[0])
        ]
    )


def entry(ref, row, column):
    return ref[row : row + 1, column : column + 1]


def attend(slot_ref, level_ref, gate_ref, *refs, tokens):
    out_ref = refs[-1]
    devices, rows, width = out_ref.shape
    own_refs, pair_refs = refs[:devices], refs[devices:-1]
    groups, local_frames = slot_ref.shape
    group_keys = devices * rows
    key_count = groups * group_keys
    group = lax.axis_index("frame")
    index = lax.broadcasted_iota(jnp.int32, (1, key_count), 1)
    frame = (index // group_keys + group) % groups * local_frames + index // tokens % local_frames
    key_slots = jnp.zeros((1, key_count), jnp.int32)
    for one in range(groups * local_frames):
        key_slots = jnp.where(
            frame == one, entry(slot_ref, one // local_frames, one % local_frames), key_slots
        )
    gate_blocks = gate_ref[...]
    level_rows = lax.broadcasted_iota(jnp.int32, gate_blocks.shape, 0)
    shown, gate_rows = [], []
    for local in range(local_frames):
        slot, level = entry(slot_ref, 0, local), entry(level_ref, 0, local)
        for other in range(1, groups):
            slot = jnp.where(group == other, entry(slot_ref, other, local), slot)
            level = jnp.where(group == other, entry(level_ref, other, local), level)
        shown.append(jnp.where(key_slots <= slot, 0.0, -jnp.inf).reshape(1, 1, 1, key_count))
        gate = jnp.where(level_rows == level, gate_blocks, 0.0)
        gate_rows.append(jnp.sum(gate, axis=0, keepdims=True))
    shown = jnp.concatenate(shown, axis=1)
    ones = jnp.ones((key_count, HEAD), jnp.bfloat16)
    scale = math.log2(math.e) / math.sqrt(HEAD)
    step = max(1, min(devices, 128 // rows))
    for column in range(0, width, HEAD):
        part = slice(column, column + HEAD)
        gates = [row[:, part].reshape(1, 1, 1, HEAD) for row in gate_rows]
        gates = jnp.concatenate(gates, axis=1)
        keys, values = (
            jnp.concatenate(
                [ref[1 + kind, :, part] for ref in own_refs]
                + [ref[:, kind, :, part].reshape(ref.shape[0] * rows, HEAD) for ref in pair_refs]
            )
            for kind in range(2)
        )
        values = jnp.concatenate([values, ones], axis=1)
        for start in range(0, devices, step):
            queries = jnp.concatenate([ref[0, :, part] for ref in own_refs[start : start + step]])
            scores = lax.dot_general(
                queries, keys, (((1,), (1,)), ((), ())), preferred_element_type=jnp.float32
            )
            scores = scores.reshape(step, local_frames, tokens, key_count) * scale + shown
            scores = scores.reshape(step * rows, key_count)
            weights = jnp.exp2(scores - jnp.max(scores, axis=1, keepdims=True))
            mixed = jnp.dot(
                weights.astype(jnp.bfloat16), values, preferred_element_type=jnp.float32
            )
            mixed = mixed[:, :HEAD] / mixed[:, HEAD:]
            mixed = mixed.reshape(step, local_frames, tokens, HEAD) * gates
            mixed = mixed.reshape(step, rows, HEAD).astype(out_ref.dtype)
            for number, away in enumerate(send_order(devices)[start : start + step]):
                out_ref[lax.axis_index("seq") ^ away, :, part] = mixed[number]


def whole_heads(queries, keys, values, slot_of, level_of, gate_table):
    devices, groups = lax.axis_size("seq"), lax.axis_size("frame")
    _, local_frames, tokens, all_width = queries.shape
    rows, width = local_frames * tokens, all_width // devices

    def in_hbm(taken):
        return pltpu.with_memory_space_constraint(taken, pltpu.HBM)

    *pieces, slots, levels, gates = pl.pallas_call(
        pack,
        out_shape=[jax.ShapeDtypeStruct((3, rows, width), queries.dtype)] * devices
        + [
            jax.ShapeDtypeStruct(slot_of.shape, slot_of.dtype),
            jax.ShapeDtypeStruct(level_of.shape, level_of.dtype),
            jax.ShapeDtypeStruct((gate_table.shape[0], width), gate_table.dtype),
        ],
        in_specs=[HBM] * 6,
        out_specs=[VMEM] * (devices + 3),
        scratch_shapes=[pltpu.SemaphoreType.DMA((devices, 3)), pltpu.SemaphoreType.DMA((3,))],
        compiler_params=PARAMS,
    )(
        *(in_hbm(taken.reshape(rows, all_width)) for taken in (queries, keys, values)),
        *(in_hbm(taken) for taken in (slot_of, level_of, gate_table)),
    )
    pieces = [
        lax.ppermute(piece, "seq", [(one, one ^ away) for one in range(devices)])
        if away
        else piece
        for away, piece in zip(send_order(devices), pieces)
    ]

    stacked = pl.pallas_call(
        stack,
        out_shape=jax.ShapeDtypeStruct((devices, 2, rows, width), queries.dtype),
        in_specs=[VMEM] * devices,
        out_specs=VMEM,
        scratch_shapes=[pltpu.SemaphoreType.DMA((devices,))],
        compiler_params=PARAMS,
    )(*pieces)
    stacks = [
        lax.ppermute(stacked, "frame", [(one, (one - away) % groups) for one in range(groups)])
        for away in range(1, groups)
    ]
    answer = pl.pallas_call(
        functools.partial(attend, tokens=tokens),
        out_shape=jax.ShapeDtypeStruct((devices, rows, width), queries.dtype),
        in_specs=[VMEM] * (3 + devices + len(stacks)),
        out_specs=VMEM,
        compiler_params=PARAMS,
    )(slots, levels, gates, *pieces, *stacks)
    answer = answer.reshape(devices, local_frames, tokens, width)
    answer = lax.all_to_all(answer, "seq", split_axis=0, concat_axis=0, tiled=True)
    answer = pl.pallas_call(
        unpack,
        out_shape=jax.ShapeDtypeStruct((local_frames, devices, tokens, width), queries.dtype),
        in_specs=[VMEM],
        out_specs=HBM,
        scratch_shapes=[pltpu.SemaphoreType.DMA((local_frames,))],
        compiler_params=PARAMS,
    )(answer)
    return answer.transpose(0, 2, 1, 3).reshape(queries.shape)


def shared_heads(queries, keys, values, slot_of, level_of, gate_table):
    devices = lax.axis_size("frame") * lax.axis_size("seq")
    _, local_frames, tokens, _ = queries.shape
    rows, blocks = local_frames * tokens, devices // H
    block_rows = rows // blocks
    exchange = functools.partial(
        lax.all_to_all, axis_name=AXES, split_axis=0, concat_axis=0, tiled=True
    )

    def by_head(taken):
        return taken.reshape(rows, H, HEAD).transpose(1, 0, 2)

    def key_pieces(taken):
        pieces = jnp.broadcast_to(by_head(taken)[:, None], (H, blocks, rows, HEAD))
        return exchange(pieces.reshape(devices, rows, HEAD)).reshape(devices * rows, HEAD)

    key_rows, value_rows = key_pieces(keys), key_pieces(values)
    query_rows = exchange(by_head(queries).reshape(devices, block_rows, HEAD))
    query_rows = query_rows.reshape(devices * block_rows, HEAD)
    device_index = lax.axis_index("frame") * lax.axis_size("seq") + lax.axis_index("seq")
    head, block = device_index // blocks, device_index % blocks

    def per_row(table):
        table = jnp.repeat(table, tokens, axis=1)[:, None]
        return jnp.broadcast_to(table, (table.shape[0], lax.axis_size("seq"), rows))

    row_slots, row_levels = per_row(slot_of), per_row(level_of)
    query_slots = lax.dynamic_slice_in_dim(row_slots, block * block_rows, block_rows, 2)
    levels = lax.dynamic_slice_in_dim(row_levels, block * block_rows, block_rows, 2).reshape(-1)
    scores = lax.dot_general(
        query_rows, key_rows, (((1,), (1,)), ((), ())), preferred_element_type=jnp.float32
    )
    visible = row_slots.reshape(1, -1) <= query_slots.reshape(-1, 1)
    scores = jnp.where(visible, scores * (1.0 / math.sqrt(HEAD)), -jnp.inf)
    weights = jnp.exp(scores - jnp.max(scores, axis=1, keepdims=True)).astype(jnp.bfloat16)
    total = jnp.sum(weights.astype(jnp.float32), axis=1, keepdims=True)
    mixed = jnp.dot(weights, value_rows, preferred_element_type=jnp.float32) / total
    gates = lax.dynamic_slice_in_dim(gate_table, head * HEAD, HEAD, 1)[levels]
    answer = exchange((mixed * gates).astype(queries.dtype).reshape(devices, block_rows, HEAD))
    return answer.reshape(H, rows, HEAD).transpose(1, 0, 2).reshape(queries.shape)


def solution(mesh):
    seq = mesh.shape["seq"]
    tokens = P(("rollout", "frame"), None, "seq", None)
    return jax.shard_map(
        whole_heads if seq <= H and seq & (seq - 1) == 0 else shared_heads,
        mesh=mesh,
        in_specs=(tokens, tokens, tokens, P("rollout", None), P("rollout", None), P()),
        out_specs=tokens,
        check_vma=False,
    )
```

```python
import functools
import math

import jax
import jax.numpy as jnp
from jax import lax
from jax.experimental import pallas as pl
from jax.experimental.pallas import tpu as pltpu
from jax.sharding import PartitionSpec as P

H = 16
HEAD = 128
AXES = ("frame", "seq")
HBM = pl.BlockSpec(memory_space=pltpu.HBM)
VMEM = pl.BlockSpec(memory_space=pltpu.VMEM)
PARAMS = pltpu.CompilerParams(vmem_limit_bytes=32 * 1024 * 1024)


def send_order(devices):
    half = devices // 2
    far = [*range(half + 1, devices), half][:half]
    far[:2] = far[1::-1]
    return far + [*range(half - 1, 0, -1)] + [0]


def run(copies):
    for copy in copies:
        copy.start()
    for copy in copies:
        copy.wait()


def pack(*refs):
    *operands, slot_ref, level_ref, gate_ref = refs[:6]
    *outs, slot_out, level_out, gate_out, sems, table_sems = refs[6:]
    width = gate_out.shape[-1]
    place = lax.axis_index("seq")

    def columns(place):
        return pl.ds(pl.multiple_of(place * width, width), width)

    tables = (
        (slot_ref, slot_out),
        (level_ref, level_out),
        (gate_ref.at[:, columns(place)], gate_out),
    )
    run(
        [
            pltpu.make_async_copy(
                ref.at[:, columns(place ^ away)], out_ref.at[kind], sems.at[away, kind]
            )
            for away, out_ref in zip(send_order(len(outs)), outs)
            for kind, ref in enumerate(operands)
        ]
        + [
            pltpu.make_async_copy(ref, out_ref, table_sems.at[kind])
            for kind, (ref, out_ref) in enumerate(tables)
        ]
    )


def stack(*refs):
    *pieces, out_ref = refs
    for number, ref in enumerate(pieces):
        out_ref[number] = ref[1:3]


def unpack(held_ref, out_ref, sems):
    run(
        [
            pltpu.make_async_copy(held_ref.at[:, frame], out_ref.at[frame], sems.at[frame])
            for frame in range(out_ref.shape[0])
        ]
    )


def entry(ref, row, column):
    return ref[row : row + 1, column : column + 1]


def attend(slot_ref, level_ref, gate_ref, *refs, tokens):
    out_ref = refs[-1]
    devices, rows, width = out_ref.shape
    own_refs, pair_refs = refs[:devices], refs[devices:-1]
    groups, local_frames = slot_ref.shape
    group_keys = devices * rows
    key_count = groups * group_keys
    group = lax.axis_index("frame")
    index = lax.broadcasted_iota(jnp.int32, (1, key_count), 1)
    frame = (index // group_keys + group) % groups * local_frames + index // tokens % local_frames
    key_slots = jnp.zeros((1, key_count), jnp.int32)
    for one in range(groups * local_frames):
        key_slots = jnp.where(
            frame == one, entry(slot_ref, one // local_frames, one % local_frames), key_slots
        )
    gate_blocks = gate_ref[...]
    level_rows = lax.broadcasted_iota(jnp.int32, gate_blocks.shape, 0)
    shown, gate_rows = [], []
    for local in range(local_frames):
        slot, level = entry(slot_ref, 0, local), entry(level_ref, 0, local)
        for other in range(1, groups):
            slot = jnp.where(group == other, entry(slot_ref, other, local), slot)
            level = jnp.where(group == other, entry(level_ref, other, local), level)
        shown.append(jnp.where(key_slots <= slot, 0.0, -jnp.inf).reshape(1, 1, 1, key_count))
        gate = jnp.where(level_rows == level, gate_blocks, 0.0)
        gate_rows.append(jnp.sum(gate, axis=0, keepdims=True))
    shown = jnp.concatenate(shown, axis=1)
    ones = jnp.ones((key_count, HEAD), jnp.bfloat16)
    scale = math.log2(math.e) / math.sqrt(HEAD)
    step = max(1, min(devices, 128 // rows))
    for column in range(0, width, HEAD):
        part = slice(column, column + HEAD)
        gates = [row[:, part].reshape(1, 1, 1, HEAD) for row in gate_rows]
        gates = jnp.concatenate(gates, axis=1)
        keys, values = (
            jnp.concatenate(
                [ref[1 + kind, :, part] for ref in own_refs]
                + [ref[:, kind, :, part].reshape(ref.shape[0] * rows, HEAD) for ref in pair_refs]
            )
            for kind in range(2)
        )
        values = jnp.concatenate([values, ones], axis=1)
        for start in range(0, devices, step):
            queries = jnp.concatenate([ref[0, :, part] for ref in own_refs[start : start + step]])
            scores = lax.dot_general(
                queries, keys, (((1,), (1,)), ((), ())), preferred_element_type=jnp.float32
            )
            scores = scores.reshape(step, local_frames, tokens, key_count) * scale + shown
            scores = scores.reshape(step * rows, key_count)
            weights = jnp.exp2(scores - jnp.max(scores, axis=1, keepdims=True))
            mixed = jnp.dot(
                weights.astype(jnp.bfloat16), values, preferred_element_type=jnp.float32
            )
            mixed = mixed[:, :HEAD] / mixed[:, HEAD:]
            mixed = mixed.reshape(step, local_frames, tokens, HEAD) * gates
            mixed = mixed.reshape(step, rows, HEAD).astype(out_ref.dtype)
            for number, away in enumerate(send_order(devices)[start : start + step]):
                out_ref[lax.axis_index("seq") ^ away, :, part] = mixed[number]


def whole_heads(queries, keys, values, slot_of, level_of, gate_table):
    devices, groups = lax.axis_size("seq"), lax.axis_size("frame")
    _, local_frames, tokens, all_width = queries.shape
    rows, width = local_frames * tokens, all_width // devices

    def in_hbm(taken):
        return pltpu.with_memory_space_constraint(taken, pltpu.HBM)

    *pieces, slots, levels, gates = pl.pallas_call(
        pack,
        out_shape=[jax.ShapeDtypeStruct((3, rows, width), queries.dtype)] * devices
        + [
            jax.ShapeDtypeStruct(slot_of.shape, slot_of.dtype),
            jax.ShapeDtypeStruct(level_of.shape, level_of.dtype),
            jax.ShapeDtypeStruct((gate_table.shape[0], width), gate_table.dtype),
        ],
        in_specs=[HBM] * 6,
        out_specs=[VMEM] * (devices + 3),
        scratch_shapes=[pltpu.SemaphoreType.DMA((devices, 3)), pltpu.SemaphoreType.DMA((3,))],
        compiler_params=PARAMS,
    )(
        *(in_hbm(taken.reshape(rows, all_width)) for taken in (queries, keys, values)),
        *(in_hbm(taken) for taken in (slot_of, level_of, gate_table)),
    )
    pieces = [
        lax.ppermute(piece, "seq", [(one, one ^ away) for one in range(devices)])
        if away
        else piece
        for away, piece in zip(send_order(devices), pieces)
    ]

    stacked = pl.pallas_call(
        stack,
        out_shape=jax.ShapeDtypeStruct((devices, 2, rows, width), queries.dtype),
        in_specs=[VMEM] * devices,
        out_specs=VMEM,
        compiler_params=PARAMS,
    )(*pieces)
    stacks = [
        lax.ppermute(stacked, "frame", [(one, (one - away) % groups) for one in range(groups)])
        for away in range(1, groups)
    ]
    answer = pl.pallas_call(
        functools.partial(attend, tokens=tokens),
        out_shape=jax.ShapeDtypeStruct((devices, rows, width), queries.dtype),
        in_specs=[VMEM] * (3 + devices + len(stacks)),
        out_specs=VMEM,
        compiler_params=PARAMS,
    )(slots, levels, gates, *pieces, *stacks)
    answer = answer.reshape(devices, local_frames, tokens, width)
    answer = lax.all_to_all(answer, "seq", split_axis=0, concat_axis=0, tiled=True)
    answer = pl.pallas_call(
        unpack,
        out_shape=jax.ShapeDtypeStruct((local_frames, devices, tokens, width), queries.dtype),
        in_specs=[VMEM],
        out_specs=HBM,
        scratch_shapes=[pltpu.SemaphoreType.DMA((local_frames,))],
        compiler_params=PARAMS,
    )(answer)
    return answer.transpose(0, 2, 1, 3).reshape(queries.shape)


def shared_heads(queries, keys, values, slot_of, level_of, gate_table):
    devices = lax.axis_size("frame") * lax.axis_size("seq")
    _, local_frames, tokens, _ = queries.shape
    rows, blocks = local_frames * tokens, devices // H
    block_rows = rows // blocks
    exchange = functools.partial(
        lax.all_to_all, axis_name=AXES, split_axis=0, concat_axis=0, tiled=True
    )

    def by_head(taken):
        return taken.reshape(rows, H, HEAD).transpose(1, 0, 2)

    def key_pieces(taken):
        pieces = jnp.broadcast_to(by_head(taken)[:, None], (H, blocks, rows, HEAD))
        return exchange(pieces.reshape(devices, rows, HEAD)).reshape(devices * rows, HEAD)

    key_rows, value_rows = key_pieces(keys), key_pieces(values)
    query_rows = exchange(by_head(queries).reshape(devices, block_rows, HEAD))
    query_rows = query_rows.reshape(devices * block_rows, HEAD)
    device_index = lax.axis_index("frame") * lax.axis_size("seq") + lax.axis_index("seq")
    head, block = device_index // blocks, device_index % blocks

    def per_row(table):
        table = jnp.repeat(table, tokens, axis=1)[:, None]
        return jnp.broadcast_to(table, (table.shape[0], lax.axis_size("seq"), rows))

    row_slots, row_levels = per_row(slot_of), per_row(level_of)
    query_slots = lax.dynamic_slice_in_dim(row_slots, block * block_rows, block_rows, 2)
    levels = lax.dynamic_slice_in_dim(row_levels, block * block_rows, block_rows, 2).reshape(-1)
    scores = lax.dot_general(
        query_rows, key_rows, (((1,), (1,)), ((), ())), preferred_element_type=jnp.float32
    )
    visible = row_slots.reshape(1, -1) <= query_slots.reshape(-1, 1)
    scores = jnp.where(visible, scores * (1.0 / math.sqrt(HEAD)), -jnp.inf)
    weights = jnp.exp(scores - jnp.max(scores, axis=1, keepdims=True)).astype(jnp.bfloat16)
    total = jnp.sum(weights.astype(jnp.float32), axis=1, keepdims=True)
    mixed = jnp.dot(weights, value_rows, preferred_element_type=jnp.float32) / total
    gates = lax.dynamic_slice_in_dim(gate_table, head * HEAD, HEAD, 1)[levels]
    answer = exchange((mixed * gates).astype(queries.dtype).reshape(devices, block_rows, HEAD))
    return answer.reshape(H, rows, HEAD).transpose(1, 0, 2).reshape(queries.shape)


def solution(mesh):
    seq = mesh.shape["seq"]
    tokens = P(("rollout", "frame"), None, "seq", None)
    return jax.shard_map(
        whole_heads if seq <= H and seq & (seq - 1) == 0 else shared_heads,
        mesh=mesh,
        in_specs=(tokens, tokens, tokens, P("rollout", None), P("rollout", None), P()),
        out_specs=tokens,
        check_vma=False,
    )
```

```python
import functools
import math

import jax
import jax.numpy as jnp
from jax import lax
from jax.experimental import pallas as pl
from jax.experimental.pallas import tpu as pltpu
from jax.sharding import PartitionSpec as P

H = 16
HEAD = 128
AXES = ("frame", "seq")
HBM = pl.BlockSpec(memory_space=pltpu.HBM)
VMEM = pl.BlockSpec(memory_space=pltpu.VMEM)
PARAMS = pltpu.CompilerParams(vmem_limit_bytes=32 * 1024 * 1024)


def send_order(devices):
    half = devices // 2
    far = [*range(half + 1, devices), half][:half]
    order = far[:1]
    for pair in zip(far[1:], range(half - 1, 0, -1)):
        order += pair
    return order + [0]


def run(copies):
    for copy in copies:
        copy.start()
    for copy in copies:
        copy.wait()


def pack(*refs):
    *operands, slot_ref, level_ref, gate_ref = refs[:6]
    *outs, slot_out, level_out, gate_out, sems, table_sems = refs[6:]
    width = gate_out.shape[-1]
    place = lax.axis_index("seq")

    def columns(place):
        return pl.ds(pl.multiple_of(place * width, width), width)

    tables = (
        (slot_ref, slot_out),
        (level_ref, level_out),
        (gate_ref.at[:, columns(place)], gate_out),
    )
    run(
        [
            pltpu.make_async_copy(
                ref.at[:, columns(place ^ away)], out_ref.at[kind], sems.at[away, kind]
            )
            for away, out_ref in zip(send_order(len(outs)), outs)
            for kind, ref in enumerate(operands)
        ]
        + [
            pltpu.make_async_copy(ref, out_ref, table_sems.at[kind])
            for kind, (ref, out_ref) in enumerate(tables)
        ]
    )


def stack(*refs):
    *pieces, out_ref = refs
    for number, ref in enumerate(pieces):
        out_ref[number] = ref[1:3]


def unpack(held_ref, out_ref, sems):
    run(
        [
            pltpu.make_async_copy(held_ref.at[:, frame], out_ref.at[frame], sems.at[frame])
            for frame in range(out_ref.shape[0])
        ]
    )


def entry(ref, row, column):
    return ref[row : row + 1, column : column + 1]


def attend(slot_ref, level_ref, gate_ref, *refs, tokens):
    out_ref = refs[-1]
    devices, rows, width = out_ref.shape
    own_refs, pair_refs = refs[:devices], refs[devices:-1]
    groups, local_frames = slot_ref.shape
    group_keys = devices * rows
    key_count = groups * group_keys
    group = lax.axis_index("frame")
    index = lax.broadcasted_iota(jnp.int32, (1, key_count), 1)
    frame = (index // group_keys + group) % groups * local_frames + index // tokens % local_frames
    key_slots = jnp.zeros((1, key_count), jnp.int32)
    for one in range(groups * local_frames):
        key_slots = jnp.where(
            frame == one, entry(slot_ref, one // local_frames, one % local_frames), key_slots
        )
    gate_blocks = gate_ref[...]
    level_rows = lax.broadcasted_iota(jnp.int32, gate_blocks.shape, 0)
    shown, gate_rows = [], []
    for local in range(local_frames):
        slot, level = entry(slot_ref, 0, local), entry(level_ref, 0, local)
        for other in range(1, groups):
            slot = jnp.where(group == other, entry(slot_ref, other, local), slot)
            level = jnp.where(group == other, entry(level_ref, other, local), level)
        shown.append(jnp.where(key_slots <= slot, 0.0, -jnp.inf).reshape(1, 1, 1, key_count))
        gate = jnp.where(level_rows == level, gate_blocks, 0.0)
        gate_rows.append(jnp.sum(gate, axis=0, keepdims=True))
    shown = jnp.concatenate(shown, axis=1)
    ones = jnp.ones((key_count, HEAD), jnp.bfloat16)
    scale = math.log2(math.e) / math.sqrt(HEAD)
    step = max(1, min(devices, 128 // rows))
    for column in range(0, width, HEAD):
        part = slice(column, column + HEAD)
        gates = [row[:, part].reshape(1, 1, 1, HEAD) for row in gate_rows]
        gates = jnp.concatenate(gates, axis=1)
        keys, values = (
            jnp.concatenate(
                [ref[1 + kind, :, part] for ref in own_refs]
                + [ref[:, kind, :, part].reshape(ref.shape[0] * rows, HEAD) for ref in pair_refs]
            )
            for kind in range(2)
        )
        values = jnp.concatenate([values, ones], axis=1)
        for start in range(0, devices, step):
            queries = jnp.concatenate([ref[0, :, part] for ref in own_refs[start : start + step]])
            scores = lax.dot_general(
                queries, keys, (((1,), (1,)), ((), ())), preferred_element_type=jnp.float32
            )
            scores = scores.reshape(step, local_frames, tokens, key_count) * scale + shown
            scores = scores.reshape(step * rows, key_count)
            weights = jnp.exp2(scores - jnp.max(scores, axis=1, keepdims=True))
            mixed = jnp.dot(
                weights.astype(jnp.bfloat16), values, preferred_element_type=jnp.float32
            )
            mixed = mixed[:, :HEAD] / mixed[:, HEAD:]
            mixed = mixed.reshape(step, local_frames, tokens, HEAD) * gates
            mixed = mixed.reshape(step, rows, HEAD).astype(out_ref.dtype)
            for number, away in enumerate(send_order(devices)[start : start + step]):
                out_ref[lax.axis_index("seq") ^ away, :, part] = mixed[number]


def whole_heads(queries, keys, values, slot_of, level_of, gate_table):
    devices, groups = lax.axis_size("seq"), lax.axis_size("frame")
    _, local_frames, tokens, all_width = queries.shape
    rows, width = local_frames * tokens, all_width // devices

    def in_hbm(taken):
        return pltpu.with_memory_space_constraint(taken, pltpu.HBM)

    *pieces, slots, levels, gates = pl.pallas_call(
        pack,
        out_shape=[jax.ShapeDtypeStruct((3, rows, width), queries.dtype)] * devices
        + [
            jax.ShapeDtypeStruct(slot_of.shape, slot_of.dtype),
            jax.ShapeDtypeStruct(level_of.shape, level_of.dtype),
            jax.ShapeDtypeStruct((gate_table.shape[0], width), gate_table.dtype),
        ],
        in_specs=[HBM] * 6,
        out_specs=[VMEM] * (devices + 3),
        scratch_shapes=[pltpu.SemaphoreType.DMA((devices, 3)), pltpu.SemaphoreType.DMA((3,))],
        compiler_params=PARAMS,
    )(
        *(in_hbm(taken.reshape(rows, all_width)) for taken in (queries, keys, values)),
        *(in_hbm(taken) for taken in (slot_of, level_of, gate_table)),
    )
    pieces = [
        lax.ppermute(piece, "seq", [(one, one ^ away) for one in range(devices)])
        if away
        else piece
        for away, piece in zip(send_order(devices), pieces)
    ]

    stacked = pl.pallas_call(
        stack,
        out_shape=jax.ShapeDtypeStruct((devices, 2, rows, width), queries.dtype),
        in_specs=[VMEM] * devices,
        out_specs=VMEM,
        compiler_params=PARAMS,
    )(*pieces)
    stacks = [
        lax.ppermute(stacked, "frame", [(one, (one - away) % groups) for one in range(groups)])
        for away in range(1, groups)
    ]
    answer = pl.pallas_call(
        functools.partial(attend, tokens=tokens),
        out_shape=jax.ShapeDtypeStruct((devices, rows, width), queries.dtype),
        in_specs=[VMEM] * (3 + devices + len(stacks)),
        out_specs=VMEM,
        compiler_params=PARAMS,
    )(slots, levels, gates, *pieces, *stacks)
    answer = answer.reshape(devices, local_frames, tokens, width)
    answer = lax.all_to_all(answer, "seq", split_axis=0, concat_axis=0, tiled=True)
    answer = pl.pallas_call(
        unpack,
        out_shape=jax.ShapeDtypeStruct((local_frames, devices, tokens, width), queries.dtype),
        in_specs=[VMEM],
        out_specs=HBM,
        scratch_shapes=[pltpu.SemaphoreType.DMA((local_frames,))],
        compiler_params=PARAMS,
    )(answer)
    return answer.transpose(0, 2, 1, 3).reshape(queries.shape)


def shared_heads(queries, keys, values, slot_of, level_of, gate_table):
    devices = lax.axis_size("frame") * lax.axis_size("seq")
    _, local_frames, tokens, _ = queries.shape
    rows, blocks = local_frames * tokens, devices // H
    block_rows = rows // blocks
    exchange = functools.partial(
        lax.all_to_all, axis_name=AXES, split_axis=0, concat_axis=0, tiled=True
    )

    def by_head(taken):
        return taken.reshape(rows, H, HEAD).transpose(1, 0, 2)

    def key_pieces(taken):
        pieces = jnp.broadcast_to(by_head(taken)[:, None], (H, blocks, rows, HEAD))
        return exchange(pieces.reshape(devices, rows, HEAD)).reshape(devices * rows, HEAD)

    key_rows, value_rows = key_pieces(keys), key_pieces(values)
    query_rows = exchange(by_head(queries).reshape(devices, block_rows, HEAD))
    query_rows = query_rows.reshape(devices * block_rows, HEAD)
    device_index = lax.axis_index("frame") * lax.axis_size("seq") + lax.axis_index("seq")
    head, block = device_index // blocks, device_index % blocks

    def per_row(table):
        table = jnp.repeat(table, tokens, axis=1)[:, None]
        return jnp.broadcast_to(table, (table.shape[0], lax.axis_size("seq"), rows))

    row_slots, row_levels = per_row(slot_of), per_row(level_of)
    query_slots = lax.dynamic_slice_in_dim(row_slots, block * block_rows, block_rows, 2)
    levels = lax.dynamic_slice_in_dim(row_levels, block * block_rows, block_rows, 2).reshape(-1)
    scores = lax.dot_general(
        query_rows, key_rows, (((1,), (1,)), ((), ())), preferred_element_type=jnp.float32
    )
    visible = row_slots.reshape(1, -1) <= query_slots.reshape(-1, 1)
    scores = jnp.where(visible, scores * (1.0 / math.sqrt(HEAD)), -jnp.inf)
    weights = jnp.exp(scores - jnp.max(scores, axis=1, keepdims=True)).astype(jnp.bfloat16)
    total = jnp.sum(weights.astype(jnp.float32), axis=1, keepdims=True)
    mixed = jnp.dot(weights, value_rows, preferred_element_type=jnp.float32) / total
    gates = lax.dynamic_slice_in_dim(gate_table, head * HEAD, HEAD, 1)[levels]
    answer = exchange((mixed * gates).astype(queries.dtype).reshape(devices, block_rows, HEAD))
    return answer.reshape(H, rows, HEAD).transpose(1, 0, 2).reshape(queries.shape)


def solution(mesh):
    seq = mesh.shape["seq"]
    tokens = P(("rollout", "frame"), None, "seq", None)
    return jax.shard_map(
        whole_heads if seq <= H and seq & (seq - 1) == 0 else shared_heads,
        mesh=mesh,
        in_specs=(tokens, tokens, tokens, P("rollout", None), P("rollout", None), P()),
        out_specs=tokens,
        check_vma=False,
    )
```

```python
import functools
import math

import jax
import jax.numpy as jnp
from jax import lax
from jax.experimental import pallas as pl
from jax.experimental.pallas import tpu as pltpu
from jax.sharding import PartitionSpec as P

H = 16
HEAD = 128
AXES = ("frame", "seq")
HBM = pl.BlockSpec(memory_space=pltpu.HBM)
VMEM = pl.BlockSpec(memory_space=pltpu.VMEM)
PARAMS = pltpu.CompilerParams(vmem_limit_bytes=32 * 1024 * 1024)


def send_order(devices):
    half = devices // 2
    far = [*range(half + 1, devices), half][:half]
    order = far[:1]
    for pair in zip(far[1:], range(half - 1, 0, -1)):
        order += pair
    return order + [0]


def run(copies):
    for copy in copies:
        copy.start()
    for copy in copies:
        copy.wait()


def pack(*refs):
    operands, outs, sems = refs[:3], refs[3:-1], refs[-1]
    place, width = lax.axis_index("seq"), outs[0].shape[-1]
    copies = []
    for away, out_ref in zip(send_order(len(outs)), outs):
        columns = pl.ds(pl.multiple_of((place ^ away) * width, width), width)
        copies += [
            pltpu.make_async_copy(ref.at[:, columns], out_ref.at[kind], sems.at[away, kind])
            for kind, ref in enumerate(operands)
        ]
    run(copies)


def stack(*refs):
    *pieces, out_ref = refs
    for number, ref in enumerate(pieces):
        out_ref[number] = ref[1:3]


def unpack(held_ref, out_ref, sems):
    run(
        [
            pltpu.make_async_copy(held_ref.at[:, frame], out_ref.at[frame], sems.at[frame])
            for frame in range(out_ref.shape[0])
        ]
    )


def entry(ref, row, column):
    return ref[row : row + 1, column : column + 1]


def attend(slot_ref, level_ref, gate_ref, *refs, tokens):
    out_ref = refs[-1]
    devices, rows, width = out_ref.shape
    own_refs, pair_refs = refs[:devices], refs[devices:-1]
    groups, local_frames = slot_ref.shape
    group_keys = devices * rows
    key_count = groups * group_keys
    group = lax.axis_index("frame")
    index = lax.broadcasted_iota(jnp.int32, (1, key_count), 1)
    frame = (index // group_keys + group) % groups * local_frames + index // tokens % local_frames
    key_slots = jnp.zeros((1, key_count), jnp.int32)
    for one in range(groups * local_frames):
        key_slots = jnp.where(
            frame == one, entry(slot_ref, one // local_frames, one % local_frames), key_slots
        )
    place = lax.axis_index("seq")
    gate_blocks = gate_ref[:, pl.ds(pl.multiple_of(place * width, width), width)]
    level_rows = lax.broadcasted_iota(jnp.int32, gate_blocks.shape, 0)
    shown, gate_rows = [], []
    for local in range(local_frames):
        slot, level = entry(slot_ref, 0, local), entry(level_ref, 0, local)
        for other in range(1, groups):
            slot = jnp.where(group == other, entry(slot_ref, other, local), slot)
            level = jnp.where(group == other, entry(level_ref, other, local), level)
        shown.append(jnp.where(key_slots <= slot, 0.0, -jnp.inf).reshape(1, 1, 1, key_count))
        gate = jnp.where(level_rows == level, gate_blocks, 0.0)
        gate_rows.append(jnp.sum(gate, axis=0, keepdims=True))
    shown = jnp.concatenate(shown, axis=1)
    ones = jnp.ones((key_count, HEAD), jnp.bfloat16)
    scale = math.log2(math.e) / math.sqrt(HEAD)
    step = max(1, min(devices, 128 // rows))
    for column in range(0, width, HEAD):
        part = slice(column, column + HEAD)
        gates = [row[:, part].reshape(1, 1, 1, HEAD) for row in gate_rows]
        gates = jnp.concatenate(gates, axis=1)
        keys, values = (
            jnp.concatenate(
                [ref[1 + kind, :, part] for ref in own_refs]
                + [ref[:, kind, :, part].reshape(ref.shape[0] * rows, HEAD) for ref in pair_refs]
            )
            for kind in range(2)
        )
        values = jnp.concatenate([values, ones], axis=1)
        for start in range(0, devices, step):
            queries = jnp.concatenate([ref[0, :, part] for ref in own_refs[start : start + step]])
            scores = lax.dot_general(
                queries, keys, (((1,), (1,)), ((), ())), preferred_element_type=jnp.float32
            )
            scores = scores.reshape(step, local_frames, tokens, key_count) * scale + shown
            scores = scores.reshape(step * rows, key_count)
            weights = jnp.exp2(scores - jnp.max(scores, axis=1, keepdims=True))
            mixed = jnp.dot(
                weights.astype(jnp.bfloat16), values, preferred_element_type=jnp.float32
            )
            mixed = mixed[:, :HEAD] / mixed[:, HEAD:]
            mixed = mixed.reshape(step, local_frames, tokens, HEAD) * gates
            mixed = mixed.reshape(step, rows, HEAD).astype(out_ref.dtype)
            for number, away in enumerate(send_order(devices)[start : start + step]):
                out_ref[place ^ away, :, part] = mixed[number]


def whole_heads(queries, keys, values, slot_of, level_of, gate_table):
    devices, groups = lax.axis_size("seq"), lax.axis_size("frame")
    _, local_frames, tokens, all_width = queries.shape
    rows, width = local_frames * tokens, all_width // devices

    pieces = pl.pallas_call(
        pack,
        out_shape=[jax.ShapeDtypeStruct((3, rows, width), queries.dtype)] * devices,
        in_specs=[HBM] * 3,
        out_specs=[VMEM] * devices,
        scratch_shapes=[pltpu.SemaphoreType.DMA((devices, 3))],
        compiler_params=PARAMS,
    )(
        *(
            pltpu.with_memory_space_constraint(taken.reshape(rows, all_width), pltpu.HBM)
            for taken in (queries, keys, values)
        )
    )
    pieces = [
        lax.ppermute(piece, "seq", [(one, one ^ away) for one in range(devices)])
        if away
        else piece
        for away, piece in zip(send_order(devices), pieces)
    ]

    stacked = pl.pallas_call(
        stack,
        out_shape=jax.ShapeDtypeStruct((devices, 2, rows, width), queries.dtype),
        in_specs=[VMEM] * devices,
        out_specs=VMEM,
        compiler_params=PARAMS,
    )(*pieces)
    stacks = [
        lax.ppermute(stacked, "frame", [(one, (one - away) % groups) for one in range(groups)])
        for away in range(1, groups)
    ]
    answer = pl.pallas_call(
        functools.partial(attend, tokens=tokens),
        out_shape=jax.ShapeDtypeStruct((devices, rows, width), queries.dtype),
        in_specs=[VMEM] * (3 + devices + len(stacks)),
        out_specs=VMEM,
        compiler_params=PARAMS,
    )(slot_of, level_of, gate_table, *pieces, *stacks)
    answer = answer.reshape(devices, local_frames, tokens, width)
    answer = lax.all_to_all(answer, "seq", split_axis=0, concat_axis=0, tiled=True)
    answer = pl.pallas_call(
        unpack,
        out_shape=jax.ShapeDtypeStruct((local_frames, devices, tokens, width), queries.dtype),
        in_specs=[VMEM],
        out_specs=HBM,
        scratch_shapes=[pltpu.SemaphoreType.DMA((local_frames,))],
        compiler_params=PARAMS,
    )(answer)
    return answer.transpose(0, 2, 1, 3).reshape(queries.shape)


def shared_heads(queries, keys, values, slot_of, level_of, gate_table):
    devices = lax.axis_size("frame") * lax.axis_size("seq")
    _, local_frames, tokens, _ = queries.shape
    rows, blocks = local_frames * tokens, devices // H
    block_rows = rows // blocks
    exchange = functools.partial(
        lax.all_to_all, axis_name=AXES, split_axis=0, concat_axis=0, tiled=True
    )

    def by_head(taken):
        return taken.reshape(rows, H, HEAD).transpose(1, 0, 2)

    def key_pieces(taken):
        pieces = jnp.broadcast_to(by_head(taken)[:, None], (H, blocks, rows, HEAD))
        return exchange(pieces.reshape(devices, rows, HEAD)).reshape(devices * rows, HEAD)

    key_rows, value_rows = key_pieces(keys), key_pieces(values)
    query_rows = exchange(by_head(queries).reshape(devices, block_rows, HEAD))
    query_rows = query_rows.reshape(devices * block_rows, HEAD)
    device_index = lax.axis_index("frame") * lax.axis_size("seq") + lax.axis_index("seq")
    head, block = device_index // blocks, device_index % blocks

    def per_row(table):
        table = jnp.repeat(table, tokens, axis=1)[:, None]
        return jnp.broadcast_to(table, (table.shape[0], lax.axis_size("seq"), rows))

    row_slots, row_levels = per_row(slot_of), per_row(level_of)
    query_slots = lax.dynamic_slice_in_dim(row_slots, block * block_rows, block_rows, 2)
    levels = lax.dynamic_slice_in_dim(row_levels, block * block_rows, block_rows, 2).reshape(-1)
    scores = lax.dot_general(
        query_rows, key_rows, (((1,), (1,)), ((), ())), preferred_element_type=jnp.float32
    )
    visible = row_slots.reshape(1, -1) <= query_slots.reshape(-1, 1)
    scores = jnp.where(visible, scores * (1.0 / math.sqrt(HEAD)), -jnp.inf)
    weights = jnp.exp(scores - jnp.max(scores, axis=1, keepdims=True)).astype(jnp.bfloat16)
    total = jnp.sum(weights.astype(jnp.float32), axis=1, keepdims=True)
    mixed = jnp.dot(weights, value_rows, preferred_element_type=jnp.float32) / total
    gates = lax.dynamic_slice_in_dim(gate_table, head * HEAD, HEAD, 1)[levels]
    answer = exchange((mixed * gates).astype(queries.dtype).reshape(devices, block_rows, HEAD))
    return answer.reshape(H, rows, HEAD).transpose(1, 0, 2).reshape(queries.shape)


def solution(mesh):
    seq = mesh.shape["seq"]
    tokens = P(("rollout", "frame"), None, "seq", None)
    return jax.shard_map(
        whole_heads if seq <= H and seq & (seq - 1) == 0 else shared_heads,
        mesh=mesh,
        in_specs=(tokens, tokens, tokens, P("rollout", None), P("rollout", None), P()),
        out_specs=tokens,
        check_vma=False,
    )
```

```python
import functools
import math

import jax
import jax.numpy as jnp
from jax import lax
from jax.experimental import pallas as pl
from jax.experimental.pallas import tpu as pltpu
from jax.sharding import PartitionSpec as P

H = 16
HEAD = 128
AXES = ("frame", "seq")
HBM = pl.BlockSpec(memory_space=pltpu.HBM)
VMEM = pl.BlockSpec(memory_space=pltpu.VMEM)
PARAMS = pltpu.CompilerParams(vmem_limit_bytes=32 * 1024 * 1024)


def send_order(devices):
    half = devices // 2
    far = [*range(half + 1, devices), half][:half]
    order = far[:1]
    for pair in zip(far[1:], range(half - 1, 0, -1)):
        order += pair
    return order + [0]


BLOCKS = 4


def blocks_of(width):
    return [pl.ds(start, width // BLOCKS) for start in range(0, width, width // BLOCKS)]


def pack(*refs):
    operands, outs, held_ref, sems = refs[:3], refs[3:-2], refs[-2], refs[-1]
    place, width = lax.axis_index("seq"), outs[0].shape[-1]
    copies = [
        [
            pltpu.make_async_copy(
                ref.at[:, block], held_ref.at[kind, :, block], sems.at[kind, number]
            )
            for number, block in enumerate(blocks_of(ref.shape[-1]))
        ]
        for kind, ref in enumerate(operands)
    ]
    for copy in sum(copies, []):
        copy.start()
    for kind, parts in enumerate(copies):
        for copy in parts:
            copy.wait()
        for away, out_ref in zip(send_order(len(outs)), outs):
            columns = pl.ds(pl.multiple_of((place ^ away) * width, width), width)
            out_ref[kind] = held_ref[kind, :, columns]


def stack(*refs):
    *pieces, out_ref = refs
    for number, ref in enumerate(pieces):
        out_ref[number] = ref[1:3]


def unpack(held_ref, out_ref, joined_ref, sems):
    width = held_ref.shape[-1]
    for device in range(held_ref.shape[0]):
        joined_ref[:, device * width : (device + 1) * width] = held_ref[device]
    copies = [
        pltpu.make_async_copy(joined_ref.at[:, block], out_ref.at[:, block], sems.at[number])
        for number, block in enumerate(blocks_of(out_ref.shape[-1]))
    ]
    for copy in copies:
        copy.start()
    for copy in copies:
        copy.wait()


def entry(ref, row, column):
    return ref[row : row + 1, column : column + 1]


def attend(slot_ref, level_ref, gate_ref, *refs, tokens):
    out_ref = refs[-1]
    devices, rows, width = out_ref.shape
    own_refs, pair_refs = refs[:devices], refs[devices:-1]
    groups, local_frames = slot_ref.shape
    group_keys = devices * rows
    key_count = groups * group_keys
    group = lax.axis_index("frame")
    index = lax.broadcasted_iota(jnp.int32, (1, key_count), 1)
    frame = (index // group_keys + group) % groups * local_frames + index // tokens % local_frames
    key_slots = jnp.zeros((1, key_count), jnp.int32)
    for one in range(groups * local_frames):
        key_slots = jnp.where(
            frame == one, entry(slot_ref, one // local_frames, one % local_frames), key_slots
        )
    place = lax.axis_index("seq")
    gate_blocks = gate_ref[:, pl.ds(pl.multiple_of(place * width, width), width)]
    level_rows = lax.broadcasted_iota(jnp.int32, gate_blocks.shape, 0)
    shown, gate_rows = [], []
    for local in range(local_frames):
        slot, level = entry(slot_ref, 0, local), entry(level_ref, 0, local)
        for other in range(1, groups):
            slot = jnp.where(group == other, entry(slot_ref, other, local), slot)
            level = jnp.where(group == other, entry(level_ref, other, local), level)
        shown.append(jnp.where(key_slots <= slot, 0.0, -jnp.inf).reshape(1, 1, 1, key_count))
        gate = jnp.where(level_rows == level, gate_blocks, 0.0)
        gate_rows.append(jnp.sum(gate, axis=0, keepdims=True))
    shown = jnp.concatenate(shown, axis=1)
    ones = jnp.ones((key_count, HEAD), jnp.bfloat16)
    scale = math.log2(math.e) / math.sqrt(HEAD)
    step = max(1, min(devices, 128 // rows))
    for column in range(0, width, HEAD):
        part = slice(column, column + HEAD)
        gates = [row[:, part].reshape(1, 1, 1, HEAD) for row in gate_rows]
        gates = jnp.concatenate(gates, axis=1)
        keys, values = (
            jnp.concatenate(
                [ref[1 + kind, :, part] for ref in own_refs]
                + [ref[:, kind, :, part].reshape(ref.shape[0] * rows, HEAD) for ref in pair_refs]
            )
            for kind in range(2)
        )
        values = jnp.concatenate([values, ones], axis=1)
        for start in range(0, devices, step):
            queries = jnp.concatenate([ref[0, :, part] for ref in own_refs[start : start + step]])
            scores = lax.dot_general(
                queries, keys, (((1,), (1,)), ((), ())), preferred_element_type=jnp.float32
            )
            scores = scores.reshape(step, local_frames, tokens, key_count) * scale + shown
            scores = scores.reshape(step * rows, key_count)
            weights = jnp.exp2(scores - jnp.max(scores, axis=1, keepdims=True))
            mixed = jnp.dot(
                weights.astype(jnp.bfloat16), values, preferred_element_type=jnp.float32
            )
            mixed = mixed[:, :HEAD] / mixed[:, HEAD:]
            mixed = mixed.reshape(step, local_frames, tokens, HEAD) * gates
            mixed = mixed.reshape(step, rows, HEAD).astype(out_ref.dtype)
            for number, away in enumerate(send_order(devices)[start : start + step]):
                out_ref[place ^ away, :, part] = mixed[number]


def whole_heads(queries, keys, values, slot_of, level_of, gate_table):
    devices, groups = lax.axis_size("seq"), lax.axis_size("frame")
    _, local_frames, tokens, all_width = queries.shape
    rows, width = local_frames * tokens, all_width // devices

    pieces = pl.pallas_call(
        pack,
        out_shape=[jax.ShapeDtypeStruct((3, rows, width), queries.dtype)] * devices,
        in_specs=[HBM] * 3,
        out_specs=[VMEM] * devices,
        scratch_shapes=[
            pltpu.VMEM((3, rows, all_width), queries.dtype),
            pltpu.SemaphoreType.DMA((3, BLOCKS)),
        ],
        compiler_params=PARAMS,
    )(
        *(
            pltpu.with_memory_space_constraint(taken.reshape(rows, all_width), pltpu.HBM)
            for taken in (queries, keys, values)
        )
    )
    pieces = [
        lax.ppermute(piece, "seq", [(one, one ^ away) for one in range(devices)])
        if away
        else piece
        for away, piece in zip(send_order(devices), pieces)
    ]

    stacked = pl.pallas_call(
        stack,
        out_shape=jax.ShapeDtypeStruct((devices, 2, rows, width), queries.dtype),
        in_specs=[VMEM] * devices,
        out_specs=VMEM,
        compiler_params=PARAMS,
    )(*pieces)
    stacks = [
        lax.ppermute(stacked, "frame", [(one, (one - away) % groups) for one in range(groups)])
        for away in range(1, groups)
    ]
    answer = pl.pallas_call(
        functools.partial(attend, tokens=tokens),
        out_shape=jax.ShapeDtypeStruct((devices, rows, width), queries.dtype),
        in_specs=[VMEM] * (3 + devices + len(stacks)),
        out_specs=VMEM,
        compiler_params=PARAMS,
    )(slot_of, level_of, gate_table, *pieces, *stacks)
    answer = lax.all_to_all(answer, "seq", split_axis=0, concat_axis=0, tiled=True)
    answer = pl.pallas_call(
        unpack,
        out_shape=jax.ShapeDtypeStruct((rows, all_width), queries.dtype),
        in_specs=[VMEM],
        out_specs=HBM,
        scratch_shapes=[
            pltpu.VMEM((rows, all_width), queries.dtype),
            pltpu.SemaphoreType.DMA((BLOCKS,)),
        ],
        compiler_params=PARAMS,
    )(answer)
    return answer.reshape(queries.shape)


def shared_heads(queries, keys, values, slot_of, level_of, gate_table):
    devices = lax.axis_size("frame") * lax.axis_size("seq")
    _, local_frames, tokens, _ = queries.shape
    rows, blocks = local_frames * tokens, devices // H
    block_rows = rows // blocks
    exchange = functools.partial(
        lax.all_to_all, axis_name=AXES, split_axis=0, concat_axis=0, tiled=True
    )

    def by_head(taken):
        return taken.reshape(rows, H, HEAD).transpose(1, 0, 2)

    def key_pieces(taken):
        pieces = jnp.broadcast_to(by_head(taken)[:, None], (H, blocks, rows, HEAD))
        return exchange(pieces.reshape(devices, rows, HEAD)).reshape(devices * rows, HEAD)

    key_rows, value_rows = key_pieces(keys), key_pieces(values)
    query_rows = exchange(by_head(queries).reshape(devices, block_rows, HEAD))
    query_rows = query_rows.reshape(devices * block_rows, HEAD)
    device_index = lax.axis_index("frame") * lax.axis_size("seq") + lax.axis_index("seq")
    head, block = device_index // blocks, device_index % blocks

    def per_row(table):
        table = jnp.repeat(table, tokens, axis=1)[:, None]
        return jnp.broadcast_to(table, (table.shape[0], lax.axis_size("seq"), rows))

    row_slots, row_levels = per_row(slot_of), per_row(level_of)
    query_slots = lax.dynamic_slice_in_dim(row_slots, block * block_rows, block_rows, 2)
    levels = lax.dynamic_slice_in_dim(row_levels, block * block_rows, block_rows, 2).reshape(-1)
    scores = lax.dot_general(
        query_rows, key_rows, (((1,), (1,)), ((), ())), preferred_element_type=jnp.float32
    )
    visible = row_slots.reshape(1, -1) <= query_slots.reshape(-1, 1)
    scores = jnp.where(visible, scores * (1.0 / math.sqrt(HEAD)), -jnp.inf)
    weights = jnp.exp(scores - jnp.max(scores, axis=1, keepdims=True)).astype(jnp.bfloat16)
    total = jnp.sum(weights.astype(jnp.float32), axis=1, keepdims=True)
    mixed = jnp.dot(weights, value_rows, preferred_element_type=jnp.float32) / total
    gates = lax.dynamic_slice_in_dim(gate_table, head * HEAD, HEAD, 1)[levels]
    answer = exchange((mixed * gates).astype(queries.dtype).reshape(devices, block_rows, HEAD))
    return answer.reshape(H, rows, HEAD).transpose(1, 0, 2).reshape(queries.shape)


def solution(mesh):
    seq = mesh.shape["seq"]
    tokens = P(("rollout", "frame"), None, "seq", None)
    return jax.shard_map(
        whole_heads if seq <= H and seq & (seq - 1) == 0 else shared_heads,
        mesh=mesh,
        in_specs=(tokens, tokens, tokens, P("rollout", None), P("rollout", None), P()),
        out_specs=tokens,
        check_vma=False,
    )
```

```python
import functools
import math

import jax
import jax.numpy as jnp
from jax import lax
from jax.experimental import pallas as pl
from jax.experimental.pallas import tpu as pltpu
from jax.sharding import PartitionSpec as P

H = 16
HEAD = 128
AXES = ("frame", "seq")
HBM = pl.BlockSpec(memory_space=pltpu.HBM)
VMEM = pl.BlockSpec(memory_space=pltpu.VMEM)
PARAMS = pltpu.CompilerParams(vmem_limit_bytes=32 * 1024 * 1024)


def send_order(devices):
    half = devices // 2
    far = [*range(half + 1, devices), half][:half]
    order = far[:1]
    for pair in zip(far[1:], range(half - 1, 0, -1)):
        order += pair
    return order + [0]


BLOCKS = 4


def blocks_of(width):
    return [pl.ds(start, width // BLOCKS) for start in range(0, width, width // BLOCKS)]


def pack(*refs):
    operands, outs, held_ref, sems = refs[:3], refs[3:-2], refs[-2], refs[-1]
    place, width = lax.axis_index("seq"), outs[0].shape[-1]
    copies = [
        [
            pltpu.make_async_copy(
                ref.at[:, block], held_ref.at[kind, :, block], sems.at[kind, number]
            )
            for number, block in enumerate(blocks_of(ref.shape[-1]))
        ]
        for kind, ref in enumerate(operands)
    ]
    for copy in sum(copies, []):
        copy.start()
    for kind, parts in enumerate(copies):
        for copy in parts:
            copy.wait()
        for away, out_ref in zip(send_order(len(outs)), outs):
            columns = pl.ds(pl.multiple_of((place ^ away) * width, width), width)
            out_ref[kind] = held_ref[kind, :, columns]


def stack(*refs):
    *pieces, out_ref = refs
    for number, ref in enumerate(pieces):
        out_ref[number] = ref[1:3]


def unpack(held_ref, out_ref, joined_ref, sems):
    width = held_ref.shape[-1]
    for device in range(held_ref.shape[0]):
        joined_ref[:, device * width : (device + 1) * width] = held_ref[device]
    copies = [
        pltpu.make_async_copy(joined_ref.at[:, block], out_ref.at[:, block], sems.at[number])
        for number, block in enumerate(blocks_of(out_ref.shape[-1]))
    ]
    for copy in copies:
        copy.start()
    for copy in copies:
        copy.wait()


def entry(ref, row, column):
    return ref[row : row + 1, column : column + 1]


def attend(slot_ref, level_ref, gate_ref, *refs, tokens):
    out_ref = refs[-1]
    devices, rows, width = out_ref.shape
    own_refs, pair_refs = refs[:devices], refs[devices:-1]
    groups, local_frames = slot_ref.shape
    group_keys = devices * rows
    key_count = groups * group_keys
    group = lax.axis_index("frame")
    index = lax.broadcasted_iota(jnp.int32, (1, key_count), 1)
    frame = (index // group_keys + group) % groups * local_frames + index // tokens % local_frames
    key_slots = jnp.zeros((1, key_count), jnp.int32)
    for one in range(groups * local_frames):
        key_slots = jnp.where(
            frame == one, entry(slot_ref, one // local_frames, one % local_frames), key_slots
        )
    place = lax.axis_index("seq")
    gate_blocks = gate_ref[:, pl.ds(pl.multiple_of(place * width, width), width)]
    level_rows = lax.broadcasted_iota(jnp.int32, gate_blocks.shape, 0)
    shown, gate_rows = [], []
    for local in range(local_frames):
        slot, level = entry(slot_ref, 0, local), entry(level_ref, 0, local)
        for other in range(1, groups):
            slot = jnp.where(group == other, entry(slot_ref, other, local), slot)
            level = jnp.where(group == other, entry(level_ref, other, local), level)
        shown.append(jnp.where(key_slots <= slot, 0.0, -jnp.inf).reshape(1, 1, 1, key_count))
        gate = jnp.where(level_rows == level, gate_blocks, 0.0)
        gate_rows.append(jnp.sum(gate, axis=0, keepdims=True))
    shown = jnp.concatenate(shown, axis=1)
    ones = jnp.ones((key_count, HEAD), jnp.bfloat16)
    scale = math.log2(math.e) / math.sqrt(HEAD)
    step = max(1, min(devices, 256 // rows))
    for column in range(0, width, HEAD):
        part = slice(column, column + HEAD)
        gates = [row[:, part].reshape(1, 1, 1, HEAD) for row in gate_rows]
        gates = jnp.concatenate(gates, axis=1)
        keys, values = (
            jnp.concatenate(
                [ref[1 + kind, :, part] for ref in own_refs]
                + [ref[:, kind, :, part].reshape(ref.shape[0] * rows, HEAD) for ref in pair_refs]
            )
            for kind in range(2)
        )
        values = jnp.concatenate([values, ones], axis=1)
        for start in range(0, devices, step):
            queries = jnp.concatenate([ref[0, :, part] for ref in own_refs[start : start + step]])
            scores = lax.dot_general(
                queries, keys, (((1,), (1,)), ((), ())), preferred_element_type=jnp.float32
            )
            scores = scores.reshape(step, local_frames, tokens, key_count) * scale + shown
            scores = scores.reshape(step * rows, key_count)
            weights = jnp.exp2(scores - jnp.max(scores, axis=1, keepdims=True))
            mixed = jnp.dot(
                weights.astype(jnp.bfloat16), values, preferred_element_type=jnp.float32
            )
            mixed = mixed[:, :HEAD] / mixed[:, HEAD:]
            mixed = mixed.reshape(step, local_frames, tokens, HEAD) * gates
            mixed = mixed.reshape(step, rows, HEAD).astype(out_ref.dtype)
            for number, away in enumerate(send_order(devices)[start : start + step]):
                out_ref[place ^ away, :, part] = mixed[number]


def whole_heads(queries, keys, values, slot_of, level_of, gate_table):
    devices, groups = lax.axis_size("seq"), lax.axis_size("frame")
    _, local_frames, tokens, all_width = queries.shape
    rows, width = local_frames * tokens, all_width // devices

    pieces = pl.pallas_call(
        pack,
        out_shape=[jax.ShapeDtypeStruct((3, rows, width), queries.dtype)] * devices,
        in_specs=[HBM] * 3,
        out_specs=[VMEM] * devices,
        scratch_shapes=[
            pltpu.VMEM((3, rows, all_width), queries.dtype),
            pltpu.SemaphoreType.DMA((3, BLOCKS)),
        ],
        compiler_params=PARAMS,
    )(
        *(
            pltpu.with_memory_space_constraint(taken.reshape(rows, all_width), pltpu.HBM)
            for taken in (queries, keys, values)
        )
    )
    pieces = [
        lax.ppermute(piece, "seq", [(one, one ^ away) for one in range(devices)])
        if away
        else piece
        for away, piece in zip(send_order(devices), pieces)
    ]

    stacked = pl.pallas_call(
        stack,
        out_shape=jax.ShapeDtypeStruct((devices, 2, rows, width), queries.dtype),
        in_specs=[VMEM] * devices,
        out_specs=VMEM,
        compiler_params=PARAMS,
    )(*pieces)
    stacks = [
        lax.ppermute(stacked, "frame", [(one, (one - away) % groups) for one in range(groups)])
        for away in range(1, groups)
    ]
    answer = pl.pallas_call(
        functools.partial(attend, tokens=tokens),
        out_shape=jax.ShapeDtypeStruct((devices, rows, width), queries.dtype),
        in_specs=[VMEM] * (3 + devices + len(stacks)),
        out_specs=VMEM,
        compiler_params=PARAMS,
    )(slot_of, level_of, gate_table, *pieces, *stacks)
    answer = lax.all_to_all(answer, "seq", split_axis=0, concat_axis=0, tiled=True)
    answer = pl.pallas_call(
        unpack,
        out_shape=jax.ShapeDtypeStruct((rows, all_width), queries.dtype),
        in_specs=[VMEM],
        out_specs=HBM,
        scratch_shapes=[
            pltpu.VMEM((rows, all_width), queries.dtype),
            pltpu.SemaphoreType.DMA((BLOCKS,)),
        ],
        compiler_params=PARAMS,
    )(answer)
    return answer.reshape(queries.shape)


def shared_heads(queries, keys, values, slot_of, level_of, gate_table):
    devices = lax.axis_size("frame") * lax.axis_size("seq")
    _, local_frames, tokens, _ = queries.shape
    rows, blocks = local_frames * tokens, devices // H
    block_rows = rows // blocks
    exchange = functools.partial(
        lax.all_to_all, axis_name=AXES, split_axis=0, concat_axis=0, tiled=True
    )

    def by_head(taken):
        return taken.reshape(rows, H, HEAD).transpose(1, 0, 2)

    def key_pieces(taken):
        pieces = jnp.broadcast_to(by_head(taken)[:, None], (H, blocks, rows, HEAD))
        return exchange(pieces.reshape(devices, rows, HEAD)).reshape(devices * rows, HEAD)

    key_rows, value_rows = key_pieces(keys), key_pieces(values)
    query_rows = exchange(by_head(queries).reshape(devices, block_rows, HEAD))
    query_rows = query_rows.reshape(devices * block_rows, HEAD)
    device_index = lax.axis_index("frame") * lax.axis_size("seq") + lax.axis_index("seq")
    head, block = device_index // blocks, device_index % blocks

    def per_row(table):
        table = jnp.repeat(table, tokens, axis=1)[:, None]
        return jnp.broadcast_to(table, (table.shape[0], lax.axis_size("seq"), rows))

    row_slots, row_levels = per_row(slot_of), per_row(level_of)
    query_slots = lax.dynamic_slice_in_dim(row_slots, block * block_rows, block_rows, 2)
    levels = lax.dynamic_slice_in_dim(row_levels, block * block_rows, block_rows, 2).reshape(-1)
    scores = lax.dot_general(
        query_rows, key_rows, (((1,), (1,)), ((), ())), preferred_element_type=jnp.float32
    )
    visible = row_slots.reshape(1, -1) <= query_slots.reshape(-1, 1)
    scores = jnp.where(visible, scores * (1.0 / math.sqrt(HEAD)), -jnp.inf)
    weights = jnp.exp(scores - jnp.max(scores, axis=1, keepdims=True)).astype(jnp.bfloat16)
    total = jnp.sum(weights.astype(jnp.float32), axis=1, keepdims=True)
    mixed = jnp.dot(weights, value_rows, preferred_element_type=jnp.float32) / total
    gates = lax.dynamic_slice_in_dim(gate_table, head * HEAD, HEAD, 1)[levels]
    answer = exchange((mixed * gates).astype(queries.dtype).reshape(devices, block_rows, HEAD))
    return answer.reshape(H, rows, HEAD).transpose(1, 0, 2).reshape(queries.shape)


def solution(mesh):
    seq = mesh.shape["seq"]
    tokens = P(("rollout", "frame"), None, "seq", None)
    return jax.shard_map(
        whole_heads if seq <= H and seq & (seq - 1) == 0 else shared_heads,
        mesh=mesh,
        in_specs=(tokens, tokens, tokens, P("rollout", None), P("rollout", None), P()),
        out_specs=tokens,
        check_vma=False,
    )
```

```python
import functools
import math

import jax
import jax.numpy as jnp
from jax import lax
from jax.experimental import pallas as pl
from jax.experimental.pallas import tpu as pltpu
from jax.sharding import PartitionSpec as P

H = 16
HEAD = 128
AXES = ("frame", "seq")
HBM = pl.BlockSpec(memory_space=pltpu.HBM)
VMEM = pl.BlockSpec(memory_space=pltpu.VMEM)
PARAMS = pltpu.CompilerParams(vmem_limit_bytes=32 * 1024 * 1024)


def send_order(devices):
    half = devices // 2
    far = [*range(half + 1, devices), half][:half]
    order = far[:1]
    for pair in zip(far[1:], range(half - 1, 0, -1)):
        order += pair
    return order + [0]


BLOCKS = 4


def blocks_of(width):
    return [pl.ds(start, width // BLOCKS) for start in range(0, width, width // BLOCKS)]


def pack(*refs):
    operands, outs, held_ref, sems = refs[:3], refs[3:-2], refs[-2], refs[-1]
    place, width = lax.axis_index("seq"), outs[0].shape[-1]
    copies = [
        [
            pltpu.make_async_copy(
                ref.at[:, block], held_ref.at[kind, :, block], sems.at[kind, number]
            )
            for number, block in enumerate(blocks_of(ref.shape[-1]))
        ]
        for kind, ref in enumerate(operands)
    ]
    for copy in sum(copies, []):
        copy.start()
    for kind, parts in enumerate(copies):
        for copy in parts:
            copy.wait()
        for away, out_ref in zip(send_order(len(outs)), outs):
            columns = pl.ds(pl.multiple_of((place ^ away) * width, width), width)
            out_ref[kind] = held_ref[kind, :, columns]


def stack(*refs):
    *pieces, out_ref = refs
    for number, ref in enumerate(pieces):
        out_ref[number] = ref[1:3]


def unpack(held_ref, out_ref, joined_ref, sems):
    width = held_ref.shape[-1]
    for device in range(held_ref.shape[0]):
        joined_ref[:, device * width : (device + 1) * width] = held_ref[device]
    copies = [
        pltpu.make_async_copy(joined_ref.at[:, block], out_ref.at[:, block], sems.at[number])
        for number, block in enumerate(blocks_of(out_ref.shape[-1]))
    ]
    for copy in copies:
        copy.start()
    for copy in copies:
        copy.wait()


def entry(ref, row, column):
    return ref[row : row + 1, column : column + 1]


def shown_keys(slot_ref, first, last, group_keys, tokens):
    groups, local_frames = slot_ref.shape
    group = lax.axis_index("frame")
    key_count = (last - first) * group_keys
    index = lax.broadcasted_iota(jnp.int32, (1, key_count), 1)
    frame = (index // group_keys + first + group) % groups * local_frames
    frame = frame + index // tokens % local_frames
    key_slots = jnp.zeros((1, key_count), jnp.int32)
    for one in range(groups * local_frames):
        key_slots = jnp.where(
            frame == one, entry(slot_ref, one // local_frames, one % local_frames), key_slots
        )
    shown = []
    for local in range(local_frames):
        slot = entry(slot_ref, 0, local)
        for other in range(1, groups):
            slot = jnp.where(group == other, entry(slot_ref, other, local), slot)
        shown.append(jnp.where(key_slots <= slot, 0.0, -jnp.inf).reshape(1, 1, 1, key_count))
    return jnp.concatenate(shown, axis=1)


def scores_of(queries, keys, shown, tokens):
    count, local_frames = keys.shape[0], shown.shape[1]
    scores = lax.dot_general(
        queries, keys, (((1,), (1,)), ((), ())), preferred_element_type=jnp.float32
    )
    scores = scores.reshape(-1, local_frames, tokens, count)
    scores = scores * (math.log2(math.e) / math.sqrt(HEAD)) + shown
    return scores.reshape(-1, count)


def weigh(scores, values):
    values = jnp.concatenate([values, jnp.ones(values.shape, values.dtype)], axis=1)
    return jnp.dot(scores.astype(jnp.bfloat16), values, preferred_element_type=jnp.float32)


def attend_own(slot_ref, *refs, tokens):
    *own_refs, sum_ref, top_ref = refs
    devices, (_, rows, width) = len(own_refs), own_refs[0].shape
    shown = shown_keys(slot_ref, 0, 1, devices * rows, tokens)
    for number, column in enumerate(range(0, width, HEAD)):
        part = slice(column, column + HEAD)
        queries, keys, values = (
            jnp.concatenate([ref[kind, :, part] for ref in own_refs]) for kind in range(3)
        )
        scores = scores_of(queries, keys, shown, tokens)
        top = jnp.max(scores, axis=1, keepdims=True)
        sum_ref[number] = weigh(jnp.exp2(scores - top), values)
        top_ref[number] = jnp.broadcast_to(top, top_ref.shape[1:])


def attend(slot_ref, level_ref, gate_ref, sum_ref, top_ref, *refs, tokens):
    out_ref = refs[-1]
    devices, rows, width = out_ref.shape
    own_refs, pair_refs = refs[:devices], refs[devices:-1]
    groups, local_frames = slot_ref.shape
    group, place = lax.axis_index("frame"), lax.axis_index("seq")
    gate_blocks = gate_ref[:, pl.ds(pl.multiple_of(place * width, width), width)]
    level_rows = lax.broadcasted_iota(jnp.int32, gate_blocks.shape, 0)
    gate_rows = []
    for local in range(local_frames):
        level = entry(level_ref, 0, local)
        for other in range(1, groups):
            level = jnp.where(group == other, entry(level_ref, other, local), level)
        gate = jnp.where(level_rows == level, gate_blocks, 0.0)
        gate_rows.append(jnp.sum(gate, axis=0, keepdims=True))
    if pair_refs:
        shown = shown_keys(slot_ref, 1, groups, devices * rows, tokens)
    for number, column in enumerate(range(0, width, HEAD)):
        part = slice(column, column + HEAD)
        gates = [row[:, part].reshape(1, 1, 1, HEAD) for row in gate_rows]
        gates = jnp.concatenate(gates, axis=1)
        mixed = sum_ref[number]
        if pair_refs:
            keys, values = (
                jnp.concatenate([ref[:, kind, :, part].reshape(-1, HEAD) for ref in pair_refs])
                for kind in range(2)
            )
            queries = jnp.concatenate([ref[0, :, part] for ref in own_refs])
            scores = scores_of(queries, keys, shown, tokens)
            own_top = top_ref[number][:, :1]
            top = jnp.maximum(own_top, jnp.max(scores, axis=1, keepdims=True))
            mixed = mixed * jnp.exp2(own_top - top) + weigh(jnp.exp2(scores - top), values)
        mixed = mixed[:, :HEAD] / mixed[:, HEAD:]
        mixed = mixed.reshape(devices, local_frames, tokens, HEAD) * gates
        mixed = mixed.reshape(devices, rows, HEAD).astype(out_ref.dtype)
        for at, away in enumerate(send_order(devices)):
            out_ref[place ^ away, :, part] = mixed[at]


def whole_heads(queries, keys, values, slot_of, level_of, gate_table):
    devices, groups = lax.axis_size("seq"), lax.axis_size("frame")
    _, local_frames, tokens, all_width = queries.shape
    rows, width = local_frames * tokens, all_width // devices

    pieces = pl.pallas_call(
        pack,
        out_shape=[jax.ShapeDtypeStruct((3, rows, width), queries.dtype)] * devices,
        in_specs=[HBM] * 3,
        out_specs=[VMEM] * devices,
        scratch_shapes=[
            pltpu.VMEM((3, rows, all_width), queries.dtype),
            pltpu.SemaphoreType.DMA((3, BLOCKS)),
        ],
        compiler_params=PARAMS,
    )(
        *(
            pltpu.with_memory_space_constraint(taken.reshape(rows, all_width), pltpu.HBM)
            for taken in (queries, keys, values)
        )
    )
    pieces = [
        lax.ppermute(piece, "seq", [(one, one ^ away) for one in range(devices)])
        if away
        else piece
        for away, piece in zip(send_order(devices), pieces)
    ]

    stacked = pl.pallas_call(
        stack,
        out_shape=jax.ShapeDtypeStruct((devices, 2, rows, width), queries.dtype),
        in_specs=[VMEM] * devices,
        out_specs=VMEM,
        compiler_params=PARAMS,
    )(*pieces)
    stacks = [
        lax.ppermute(stacked, "frame", [(one, (one - away) % groups) for one in range(groups)])
        for away in range(1, groups)
    ]
    heads, own_rows = width // HEAD, devices * rows
    sums, tops = pl.pallas_call(
        functools.partial(attend_own, tokens=tokens),
        out_shape=[
            jax.ShapeDtypeStruct((heads, own_rows, 2 * HEAD), jnp.float32),
            jax.ShapeDtypeStruct((heads, own_rows, HEAD), jnp.float32),
        ],
        in_specs=[VMEM] * (1 + devices),
        out_specs=[VMEM] * 2,
        compiler_params=PARAMS,
        cost_estimate=pl.CostEstimate(
            flops=6 * heads * own_rows * own_rows * HEAD,
            bytes_accessed=2 * 4 * heads * own_rows * HEAD,
            transcendentals=heads * own_rows * own_rows,
        ),
    )(slot_of, *pieces)
    answer = pl.pallas_call(
        functools.partial(attend, tokens=tokens),
        out_shape=jax.ShapeDtypeStruct((devices, rows, width), queries.dtype),
        in_specs=[VMEM] * (5 + devices + len(stacks)),
        out_specs=VMEM,
        compiler_params=PARAMS,
    )(slot_of, level_of, gate_table, sums, tops, *pieces, *stacks)
    answer = lax.all_to_all(answer, "seq", split_axis=0, concat_axis=0, tiled=True)
    answer = pl.pallas_call(
        unpack,
        out_shape=jax.ShapeDtypeStruct((rows, all_width), queries.dtype),
        in_specs=[VMEM],
        out_specs=HBM,
        scratch_shapes=[
            pltpu.VMEM((rows, all_width), queries.dtype),
            pltpu.SemaphoreType.DMA((BLOCKS,)),
        ],
        compiler_params=PARAMS,
    )(answer)
    return answer.reshape(queries.shape)


def shared_heads(queries, keys, values, slot_of, level_of, gate_table):
    devices = lax.axis_size("frame") * lax.axis_size("seq")
    _, local_frames, tokens, _ = queries.shape
    rows, blocks = local_frames * tokens, devices // H
    block_rows = rows // blocks
    exchange = functools.partial(
        lax.all_to_all, axis_name=AXES, split_axis=0, concat_axis=0, tiled=True
    )

    def by_head(taken):
        return taken.reshape(rows, H, HEAD).transpose(1, 0, 2)

    def key_pieces(taken):
        pieces = jnp.broadcast_to(by_head(taken)[:, None], (H, blocks, rows, HEAD))
        return exchange(pieces.reshape(devices, rows, HEAD)).reshape(devices * rows, HEAD)

    key_rows, value_rows = key_pieces(keys), key_pieces(values)
    query_rows = exchange(by_head(queries).reshape(devices, block_rows, HEAD))
    query_rows = query_rows.reshape(devices * block_rows, HEAD)
    device_index = lax.axis_index("frame") * lax.axis_size("seq") + lax.axis_index("seq")
    head, block = device_index // blocks, device_index % blocks

    def per_row(table):
        table = jnp.repeat(table, tokens, axis=1)[:, None]
        return jnp.broadcast_to(table, (table.shape[0], lax.axis_size("seq"), rows))

    row_slots, row_levels = per_row(slot_of), per_row(level_of)
    query_slots = lax.dynamic_slice_in_dim(row_slots, block * block_rows, block_rows, 2)
    levels = lax.dynamic_slice_in_dim(row_levels, block * block_rows, block_rows, 2).reshape(-1)
    scores = lax.dot_general(
        query_rows, key_rows, (((1,), (1,)), ((), ())), preferred_element_type=jnp.float32
    )
    visible = row_slots.reshape(1, -1) <= query_slots.reshape(-1, 1)
    scores = jnp.where(visible, scores * (1.0 / math.sqrt(HEAD)), -jnp.inf)
    weights = jnp.exp(scores - jnp.max(scores, axis=1, keepdims=True)).astype(jnp.bfloat16)
    total = jnp.sum(weights.astype(jnp.float32), axis=1, keepdims=True)
    mixed = jnp.dot(weights, value_rows, preferred_element_type=jnp.float32) / total
    gates = lax.dynamic_slice_in_dim(gate_table, head * HEAD, HEAD, 1)[levels]
    answer = exchange((mixed * gates).astype(queries.dtype).reshape(devices, block_rows, HEAD))
    return answer.reshape(H, rows, HEAD).transpose(1, 0, 2).reshape(queries.shape)


def solution(mesh):
    seq = mesh.shape["seq"]
    tokens = P(("rollout", "frame"), None, "seq", None)
    return jax.shard_map(
        whole_heads if seq <= H and seq & (seq - 1) == 0 else shared_heads,
        mesh=mesh,
        in_specs=(tokens, tokens, tokens, P("rollout", None), P("rollout", None), P()),
        out_specs=tokens,
        check_vma=False,
    )
```

```python
import functools
import math

import jax
import jax.numpy as jnp
from jax import lax
from jax.experimental import pallas as pl
from jax.experimental.pallas import tpu as pltpu
from jax.sharding import PartitionSpec as P

H = 16
HEAD = 128
AXES = ("frame", "seq")
HBM = pl.BlockSpec(memory_space=pltpu.HBM)
VMEM = pl.BlockSpec(memory_space=pltpu.VMEM)
PARAMS = pltpu.CompilerParams(vmem_limit_bytes=32 * 1024 * 1024)


def send_order(devices):
    half = devices // 2
    far = [*range(half + 1, devices), half][:half]
    order = far[:1]
    for pair in zip(far[1:], range(half - 1, 0, -1)):
        order += pair
    return order + [0]


BLOCKS = 8


def blocks_of(width):
    return [pl.ds(start, width // BLOCKS) for start in range(0, width, width // BLOCKS)]


def pack(*refs):
    operands, outs, held_ref, sems = refs[:3], refs[3:-2], refs[-2], refs[-1]
    place, width = lax.axis_index("seq"), outs[0].shape[-1]
    copies = [
        [
            pltpu.make_async_copy(
                ref.at[:, block], held_ref.at[kind, :, block], sems.at[kind, number]
            )
            for number, block in enumerate(blocks_of(ref.shape[-1]))
        ]
        for kind, ref in enumerate(operands)
    ]
    for copy in sum(copies, []):
        copy.start()
    for kind, parts in enumerate(copies):
        for copy in parts:
            copy.wait()
        for away, out_ref in zip(send_order(len(outs)), outs):
            columns = pl.ds(pl.multiple_of((place ^ away) * width, width), width)
            out_ref[kind] = held_ref[kind, :, columns]


def stack(*refs):
    *pieces, out_ref = refs
    for number, ref in enumerate(pieces):
        out_ref[number] = ref[1:3]


def unpack(held_ref, out_ref, joined_ref, sems):
    devices, _, width = held_ref.shape
    blocks = blocks_of(out_ref.shape[-1])
    copies = []
    for number, block in enumerate(blocks):
        for device in range(devices):
            start = max(device * width, block.start)
            stop = min((device + 1) * width, block.start + block.size)
            if start < stop:
                own = slice(start - device * width, stop - device * width)
                joined_ref[:, start:stop] = held_ref[device, :, own]
        copies.append(
            pltpu.make_async_copy(joined_ref.at[:, block], out_ref.at[:, block], sems.at[number])
        )
        copies[-1].start()
    for copy in copies:
        copy.wait()


def entry(ref, row, column):
    return ref[row : row + 1, column : column + 1]


def attend(slot_ref, level_ref, gate_ref, *refs, tokens):
    out_ref = refs[-1]
    devices, rows, width = out_ref.shape
    own_refs, pair_refs = refs[:devices], refs[devices:-1]
    groups, local_frames = slot_ref.shape
    group_keys = devices * rows
    key_count = groups * group_keys
    group = lax.axis_index("frame")
    index = lax.broadcasted_iota(jnp.int32, (1, key_count), 1)
    frame = (index // group_keys + group) % groups * local_frames + index // tokens % local_frames
    key_slots = jnp.zeros((1, key_count), jnp.int32)
    for one in range(groups * local_frames):
        key_slots = jnp.where(
            frame == one, entry(slot_ref, one // local_frames, one % local_frames), key_slots
        )
    place = lax.axis_index("seq")
    gate_blocks = gate_ref[:, pl.ds(pl.multiple_of(place * width, width), width)]
    level_rows = lax.broadcasted_iota(jnp.int32, gate_blocks.shape, 0)
    shown, gate_rows = [], []
    for local in range(local_frames):
        slot, level = entry(slot_ref, 0, local), entry(level_ref, 0, local)
        for other in range(1, groups):
            slot = jnp.where(group == other, entry(slot_ref, other, local), slot)
            level = jnp.where(group == other, entry(level_ref, other, local), level)
        shown.append(jnp.where(key_slots <= slot, 0.0, -jnp.inf).reshape(1, 1, 1, key_count))
        gate = jnp.where(level_rows == level, gate_blocks, 0.0)
        gate_rows.append(jnp.sum(gate, axis=0, keepdims=True))
    shown = jnp.concatenate(shown, axis=1)
    ones = jnp.ones((key_count, HEAD), jnp.bfloat16)
    scale = math.log2(math.e) / math.sqrt(HEAD)
    step = max(1, min(devices, 128 // rows))
    for column in range(0, width, HEAD):
        part = slice(column, column + HEAD)
        gates = [row[:, part].reshape(1, 1, 1, HEAD) for row in gate_rows]
        gates = jnp.concatenate(gates, axis=1)
        keys, values = (
            jnp.concatenate(
                [ref[1 + kind, :, part] for ref in own_refs]
                + [ref[:, kind, :, part].reshape(ref.shape[0] * rows, HEAD) for ref in pair_refs]
            )
            for kind in range(2)
        )
        values = jnp.concatenate([values, ones], axis=1)
        for start in range(0, devices, step):
            queries = jnp.concatenate([ref[0, :, part] for ref in own_refs[start : start + step]])
            scores = lax.dot_general(
                queries, keys, (((1,), (1,)), ((), ())), preferred_element_type=jnp.float32
            )
            scores = scores.reshape(step, local_frames, tokens, key_count) * scale + shown
            scores = scores.reshape(step * rows, key_count)
            weights = jnp.exp2(scores - jnp.max(scores, axis=1, keepdims=True))
            mixed = jnp.dot(
                weights.astype(jnp.bfloat16), values, preferred_element_type=jnp.float32
            )
            mixed = mixed[:, :HEAD] / mixed[:, HEAD:]
            mixed = mixed.reshape(step, local_frames, tokens, HEAD) * gates
            mixed = mixed.reshape(step, rows, HEAD).astype(out_ref.dtype)
            for number, away in enumerate(send_order(devices)[start : start + step]):
                out_ref[place ^ away, :, part] = mixed[number]


def whole_heads(queries, keys, values, slot_of, level_of, gate_table):
    devices, groups = lax.axis_size("seq"), lax.axis_size("frame")
    _, local_frames, tokens, all_width = queries.shape
    rows, width = local_frames * tokens, all_width // devices

    pieces = pl.pallas_call(
        pack,
        out_shape=[jax.ShapeDtypeStruct((3, rows, width), queries.dtype)] * devices,
        in_specs=[HBM] * 3,
        out_specs=[VMEM] * devices,
        scratch_shapes=[
            pltpu.VMEM((3, rows, all_width), queries.dtype),
            pltpu.SemaphoreType.DMA((3, BLOCKS)),
        ],
        compiler_params=PARAMS,
    )(
        *(
            pltpu.with_memory_space_constraint(taken.reshape(rows, all_width), pltpu.HBM)
            for taken in (queries, keys, values)
        )
    )
    pieces = [
        lax.ppermute(piece, "seq", [(one, one ^ away) for one in range(devices)])
        if away
        else piece
        for away, piece in zip(send_order(devices), pieces)
    ]

    stacked = pl.pallas_call(
        stack,
        out_shape=jax.ShapeDtypeStruct((devices, 2, rows, width), queries.dtype),
        in_specs=[VMEM] * devices,
        out_specs=VMEM,
        compiler_params=PARAMS,
    )(*pieces)
    stacks = [
        lax.ppermute(stacked, "frame", [(one, (one - away) % groups) for one in range(groups)])
        for away in range(1, groups)
    ]
    answer = pl.pallas_call(
        functools.partial(attend, tokens=tokens),
        out_shape=jax.ShapeDtypeStruct((devices, rows, width), queries.dtype),
        in_specs=[VMEM] * (3 + devices + len(stacks)),
        out_specs=VMEM,
        compiler_params=PARAMS,
    )(slot_of, level_of, gate_table, *pieces, *stacks)
    answer = lax.all_to_all(answer, "seq", split_axis=0, concat_axis=0, tiled=True)
    answer = pl.pallas_call(
        unpack,
        out_shape=jax.ShapeDtypeStruct((rows, all_width), queries.dtype),
        in_specs=[VMEM],
        out_specs=HBM,
        scratch_shapes=[
            pltpu.VMEM((rows, all_width), queries.dtype),
            pltpu.SemaphoreType.DMA((BLOCKS,)),
        ],
        compiler_params=PARAMS,
    )(answer)
    return answer.reshape(queries.shape)


def shared_heads(queries, keys, values, slot_of, level_of, gate_table):
    devices = lax.axis_size("frame") * lax.axis_size("seq")
    _, local_frames, tokens, _ = queries.shape
    rows, blocks = local_frames * tokens, devices // H
    block_rows = rows // blocks
    exchange = functools.partial(
        lax.all_to_all, axis_name=AXES, split_axis=0, concat_axis=0, tiled=True
    )

    def by_head(taken):
        return taken.reshape(rows, H, HEAD).transpose(1, 0, 2)

    def key_pieces(taken):
        pieces = jnp.broadcast_to(by_head(taken)[:, None], (H, blocks, rows, HEAD))
        return exchange(pieces.reshape(devices, rows, HEAD)).reshape(devices * rows, HEAD)

    key_rows, value_rows = key_pieces(keys), key_pieces(values)
    query_rows = exchange(by_head(queries).reshape(devices, block_rows, HEAD))
    query_rows = query_rows.reshape(devices * block_rows, HEAD)
    device_index = lax.axis_index("frame") * lax.axis_size("seq") + lax.axis_index("seq")
    head, block = device_index // blocks, device_index % blocks

    def per_row(table):
        table = jnp.repeat(table, tokens, axis=1)[:, None]
        return jnp.broadcast_to(table, (table.shape[0], lax.axis_size("seq"), rows))

    row_slots, row_levels = per_row(slot_of), per_row(level_of)
    query_slots = lax.dynamic_slice_in_dim(row_slots, block * block_rows, block_rows, 2)
    levels = lax.dynamic_slice_in_dim(row_levels, block * block_rows, block_rows, 2).reshape(-1)
    scores = lax.dot_general(
        query_rows, key_rows, (((1,), (1,)), ((), ())), preferred_element_type=jnp.float32
    )
    visible = row_slots.reshape(1, -1) <= query_slots.reshape(-1, 1)
    scores = jnp.where(visible, scores * (1.0 / math.sqrt(HEAD)), -jnp.inf)
    weights = jnp.exp(scores - jnp.max(scores, axis=1, keepdims=True)).astype(jnp.bfloat16)
    total = jnp.sum(weights.astype(jnp.float32), axis=1, keepdims=True)
    mixed = jnp.dot(weights, value_rows, preferred_element_type=jnp.float32) / total
    gates = lax.dynamic_slice_in_dim(gate_table, head * HEAD, HEAD, 1)[levels]
    answer = exchange((mixed * gates).astype(queries.dtype).reshape(devices, block_rows, HEAD))
    return answer.reshape(H, rows, HEAD).transpose(1, 0, 2).reshape(queries.shape)


def solution(mesh):
    seq = mesh.shape["seq"]
    tokens = P(("rollout", "frame"), None, "seq", None)
    return jax.shard_map(
        whole_heads if seq <= H and seq & (seq - 1) == 0 else shared_heads,
        mesh=mesh,
        in_specs=(tokens, tokens, tokens, P("rollout", None), P("rollout", None), P()),
        out_specs=tokens,
        check_vma=False,
    )
```
